512 devices in a mesh: wide: 128 (over z, x, core), narrow: 4 (over y).
Axes of the slice: x: 4, y: 4, z: 16, core: 2. Of those that a mesh axis runs over, the one named last changes fastest.
Arguments:
- piece_ids: int32 [131072], P('wide'), may hold values from 0 to 131071, as said below
- point_counts: int32 [131072, 128], P('wide'), may hold values from 0 to 15, as said below
- wavenumber: float32 [4], P('narrow'), may hold values from 0.05 to 0.6
- strength: float32 [4], P('narrow'), may hold values from 0.5 to 2
- displacement: float32 [2, 4], P(None, 'narrow'), may hold values from -0.5 to 0.5
- node_position: float32 [2, 15], replicated, may hold values from -0.5 to 0.5
- node_weights: float32 [15], replicated, may hold values from 0.25 to 1
Outputs:
- spectrum_real: float32 [4, 4096, 4096], P(None, ('wide', 'narrow'))
- spectrum_imag: float32 [4, 4096, 4096], P(None, ('wide', 'narrow'))
The draws below stay inside these ranges and needn't reach their ends.
Inputs may be any that keep to these rules, and one draw needn't show every extreme that they name: `piece_ids`: each of the 131072 piece numbers appears exactly once. The 1024 entries of one index of wide hold, from each block of 1024 consecutive piece numbers, between 4 and 12 numbers, and exactly 12 from some block. `point_counts`: zero exactly at offsets whose row or column offset exceeds 1536 - 1 in size; 15 at offset (0, 0); 7 to 15 where both offsets are within 8 of zero; 1 to 3 elsewhere.
All inputs are finite; a program needn't handle non-finite values.
Results may differ from the reference program's by a relative error of at most 0.0003.
Values sent between devices are 32-bit elements; how exact they have to be, the bound alone decides.
No kernel may reach another device: no remote copies, remote signals or barrier semaphores. Data moves between devices by JAX's collectives and lax.ppermute only.
A program may use at most 64 MiB of HBM per device.

```python
import math
import jax
import jax.numpy as jnp
from jax import lax

LATTICE = 1536
LENGTH = 4096
PLANES = 4
NODES = 15
SEG = 128
NEAR = 8
OWNERS = 128
BLOCKS = 32
PIECES = 131072
PER_OWNER = 1024
SHARE = 8


def deal_pieces(key):
    first_key, second_key, third_key = jax.random.split(key, 3)
    owner_order = jax.random.permutation(first_key, OWNERS)
    owner_range = jnp.arange(OWNERS, dtype=jnp.int32)
    plus_block = owner_order
    minus_block = owner_order[(owner_range + 1) % OWNERS]
    block_range = jnp.arange(OWNERS, dtype=jnp.int32)
    extra = SHARE // 2
    counts = SHARE + extra * (block_range[None, :] == plus_block[:, None]).astype(jnp.int32) - extra * (block_range[None, :] == minus_block[:, None]).astype(jnp.int32)
    bounds = jnp.cumsum(counts, axis=0)
    position = jnp.arange(PER_OWNER, dtype=jnp.int32)
    owner_of = jnp.sum((bounds.T[:, None, :] <= position[None, :, None]).astype(jnp.int32), axis=2)
    block_keys = jax.random.split(second_key, OWNERS)
    shuffled = jax.vmap(lambda one_key: jax.random.permutation(one_key, PER_OWNER))(block_keys)
    piece_numbers = block_range[:, None] * PER_OWNER + shuffled.astype(jnp.int32)
    tie_break = jax.random.permutation(third_key, PIECES).astype(jnp.int32)
    scores = owner_of.reshape(PIECES) * PIECES + tie_break
    ordering = jnp.argsort(scores, stable=True)
    return piece_numbers.reshape(PIECES)[ordering].astype(jnp.int32)


def draw_piece_ids(key, part):
    dealt = deal_pieces(key)
    return dealt


def draw_point_counts(key, part):
    dealt = deal_pieces(key)
    key = jax.random.fold_in(key, 5)
    near_key, far_key = jax.random.split(key)
    rows = dealt // BLOCKS
    columns = (dealt % BLOCKS)[:, None] * SEG + jnp.arange(SEG, dtype=jnp.int32)[None, :]
    row_offset = jnp.where(rows < LENGTH // 2, rows, rows - LENGTH)[:, None]
    col_offset = jnp.where(columns < LENGTH // 2, columns, columns - LENGTH)
    largest = jnp.maximum(jnp.abs(row_offset), jnp.abs(col_offset))
    inside = largest <= LATTICE - 1
    near_count = jax.random.randint(near_key, (PIECES, SEG), NODES // 2, NODES + 1)
    far_count = jax.random.randint(far_key, (PIECES, SEG), 1, 4)
    counts = jnp.where(inside, jnp.where(largest <= NEAR, near_count, far_count), 0)
    counts = jnp.where(largest == 0, NODES, counts)
    return counts.astype(jnp.int32)


def shard_levels(own_key, dims, pieces, smallest, top_value):
    gain = 1.0
    for axis_at, shards_of in pieces:
        heights = jax.random.uniform(jax.random.fold_in(jax.random.fold_in(own_key, 6), axis_at), (shards_of,), jnp.float32, smallest / len(pieces), top_value / len(pieces))
        gain = gain * jnp.repeat(jnp.exp(heights), dims[axis_at] // shards_of).reshape((-1,) + (1,) * (len(dims) - 1 - axis_at))
    return gain


def setup_inputs(seed: int = 0) -> dict:
    key_of = jax.random.split(jax.random.key(seed), 8)
    return {
        "piece_ids": draw_piece_ids(jax.random.fold_in(key_of[7], 71), 0),
        "point_counts": draw_point_counts(jax.random.fold_in(key_of[7], 71), 0),
        "wavenumber": jnp.clip(jnp.exp(math.log(0.6) - 2.4849067 * jax.random.uniform(key_of[2], (PLANES,), jnp.float32) ** shard_levels(key_of[2], (PLANES,), ((0, 4),), -0.2, 0.2)), 0.05, 0.6),
        "strength": jnp.clip(jnp.exp(math.log(2.0) - 1.3862944 * jax.random.uniform(key_of[3], (PLANES,), jnp.float32) ** shard_levels(key_of[3], (PLANES,), ((0, 4),), -0.2, 0.2)), 0.5, 2.0),
        "displacement": jnp.clip(jax.random.uniform(key_of[4], (2, PLANES), jnp.float32, -0.5, 0.5) * shard_levels(key_of[4], (2, PLANES), ((1, 4),), -0.4, 0.0), -0.5, 0.5),
        "node_position": jnp.clip(jax.random.uniform(key_of[5], (2, NODES), jnp.float32, -0.5, 0.5), -0.5, 0.5),
        "node_weights": jnp.clip(jnp.exp(jax.random.uniform(key_of[6], (NODES,), jnp.float32, math.log(0.25), math.log(1.0))), 0.25, 1.0),
    }


def fill_plane(counts_grid, signed_index, wave_one, strength_one, shift_row, shift_col, node_position, node_weights):
    row_base = signed_index[:, None] + shift_row
    col_base = signed_index[None, :] + shift_col

    def accumulate(q, running):
        real_part, imag_part = running
        row_pos = row_base + node_position[0, q]
        col_pos = col_base + node_position[1, q]
        radius = jnp.sqrt(row_pos * row_pos + col_pos * col_pos + 0.0625)
        active = (counts_grid > q).astype(jnp.float32)
        amplitude = node_weights[q] * (1.0 + strength_one / radius) * active
        phase_angle = wave_one * radius
        return (real_part + amplitude * jnp.cos(phase_angle), imag_part - amplitude * jnp.sin(phase_angle))
    initial = jnp.zeros((LENGTH, LENGTH), jnp.float32)
    return lax.fori_loop(0, NODES, accumulate, (initial, initial))

def reference(piece_ids, point_counts, wavenumber, strength, displacement, node_position, node_weights):
    counts_grid = jnp.zeros((PIECES, SEG), jnp.int32).at[piece_ids].set(point_counts).reshape(LENGTH, LENGTH)
    grid_index = jnp.arange(LENGTH, dtype=jnp.int32)
    signed_index = jnp.where(grid_index < LENGTH // 2, grid_index, grid_index - LENGTH).astype(jnp.float32)

    def one_plane(plane):
        real_part, imag_part = fill_plane(counts_grid, signed_index, wavenumber[plane], strength[plane], displacement[0, plane], displacement[1, plane], node_position, node_weights)
        spectrum = jnp.fft.fft2(lax.complex(real_part, imag_part)) / LENGTH
        return (jnp.real(spectrum).T, jnp.imag(spectrum).T)
    spectrum_real, spectrum_imag = lax.map(one_plane, jnp.arange(PLANES, dtype=jnp.int32))
    return (spectrum_real, spectrum_imag)
```

```python
import functools
import math

import jax
import jax.numpy as jnp
import numpy as np
from jax import lax
from jax.experimental import pallas as pl
from jax.experimental.pallas import tpu as pltpu
from jax.sharding import Mesh, PartitionSpec as P

LENGTH = 4096
NODES = 15
FAR = 3
HEIGHT_SQ = 0.0625
RANKS = 12
SHARED = 3
LIVE_BLOCKS = 24
HALF = 1536
ROWS = 6
PLANES = 4

PI_HI = 6.28125
PI_LO = 2.0 * math.pi - 6.28125
ROUNDER = 12582912.0


def fit_even(function, degree):
    top = math.pi**2
    grid = (np.cos(np.pi * (np.arange(400) + 0.5) / 400) + 1.0) * 0.5 * top
    series = np.polynomial.chebyshev.Chebyshev.fit(grid, function(np.sqrt(grid)), degree, [0, top])
    return [float(x) for x in series.convert(kind=np.polynomial.Polynomial).coef]


COS_COEF = fit_even(np.cos, 6)
SIN_COEF = fit_even(lambda x: np.sin(x) / x, 6)


def split_np(values):
    high = values.astype(np.float32).astype(jnp.bfloat16)
    low = (values - high.astype(np.float64)).astype(jnp.bfloat16)
    return high, low


def tables():
    v1 = np.arange(32)
    cb = np.arange(LIVE_BLOCKS)
    angle = 2.0 * np.pi * (((cb[None, :] - 12) * v1[:, None]) % 32) / 32
    cos, sin = np.cos(angle), np.sin(angle)
    first = np.concatenate(
        [np.concatenate([cos, sin], 1), np.concatenate([-sin, cos], 1)], 0
    )
    high, low = split_np(first)
    first = np.concatenate([high, high, low], 1)
    t = np.arange(128)
    angle = 2.0 * np.pi * (v1[:, None] * t[None, :]) / LENGTH
    turn_one = np.concatenate([np.cos(angle), -np.sin(angle)], 0).astype(np.float32)
    angle = 2.0 * np.pi * ((t[:, None] * t[None, :]) % 128) / 128
    second = split_np(np.concatenate([np.cos(angle), np.sin(angle)], 1) / 64.0)
    z = np.arange(16)
    third = np.zeros((2, 2, 128, 2, 2, 128))
    for b_low in range(2):
        for q2 in range(2):
            for k in range(3):
                c = z + 16 * (2 * k + b_low)
                angle = 2.0 * np.pi * (((c[:, None] - 48) * t[None, :]) % 128) / 128
                lanes = slice((q2 * 3 + k) * 16, (q2 * 3 + k) * 16 + 16)
                third[b_low, 0, lanes, q2, 0] = np.cos(angle)
                third[b_low, 0, lanes, q2, 1] = -np.sin(angle)
                third[b_low, 1, lanes, q2, 0] = np.sin(angle)
                third[b_low, 1, lanes, q2, 1] = np.cos(angle)
    third = split_np(third.reshape(512, 512) / 64.0)
    angle = 2.0 * np.pi * (v1[:, None] * t[None, :]) / LENGTH
    turn_two = np.concatenate([np.cos(angle), -np.sin(angle)], 0).astype(np.float32)
    return first, turn_one, second, third, turn_two


def iota(shape, axis):
    return lax.broadcasted_iota(jnp.int32, shape, axis)


def dot(left, right):
    return jnp.dot(left, right, preferred_element_type=jnp.float32)


def as_mask(chosen):
    return jnp.where(chosen, 1.0, 0.0).astype(jnp.bfloat16)


def split(values):
    high = values.astype(jnp.bfloat16)
    low = (values - high.astype(jnp.float32)).astype(jnp.bfloat16)
    return high, low


def sort_kernel(copy_ref, ids_ref, counts_ref, out_ref):
    base = copy_ref[0] * SHARED
    ids = ids_ref[...]
    block = ((ids >> 10) + 48) & 127
    target = ((block & 15) << 3) | (block >> 4)
    local = (ids & 1023) + 1
    owner = iota((128, 128), 0)
    lane = iota((128, 128), 1)
    prefix = jnp.concatenate([as_mask(owner < lane), jnp.ones((128, 128), jnp.bfloat16)], 1)
    running = jnp.zeros((128, 128), jnp.float32)
    picked = [jnp.zeros((128, 128), jnp.float32) for _ in range(SHARED)]
    names = [jnp.zeros((128, 128), jnp.int32) for _ in range(SHARED)]
    for k in range(8):
        here = owner == target[k : k + 1, :]
        sums = dot(as_mask(here), prefix)
        rank = running + sums[:, :128]
        running = running + sums[:, 128:]
        counts = counts_ref[k * 128 : (k + 1) * 128, :].astype(jnp.float32).astype(jnp.bfloat16)
        for s in range(SHARED):
            chosen = here & (rank == (base + s).astype(jnp.float32))
            picked[s] = picked[s] + dot(as_mask(chosen), counts)
            names[s] = names[s] + jnp.where(chosen, local[k : k + 1, :], 0)
    named = jnp.zeros((128, 128), jnp.int32)
    for s in range(SHARED):
        out_ref[pl.ds(s, 128, stride=4), :] = picked[s].astype(jnp.int32)
        total = jnp.sum(names[s].astype(jnp.float32), axis=1, keepdims=True).astype(jnp.int32)
        named = jnp.where(lane == s, total, named)
    out_ref[pl.ds(3, 128, stride=4), :] = named


def place_kernel(slot_ref, plane_ref, got_ref, out_ref):
    names = got_ref[pl.ds(3, 128, stride=4), :].astype(jnp.float32).T
    row = iota((768, 128), 0)
    grid = jnp.zeros((768, 128), jnp.float32)
    for s in range(SHARED):
        name = names[s : s + 1, :].astype(jnp.int32)
        local = name - 1
        column = ((local & 31) + 12) & 31
        valid = (name > 0) & (column < LIVE_BLOCKS)
        key = jnp.where(valid, (local >> 5) * LIVE_BLOCKS + column, -1)
        counts = got_ref[pl.ds(s, 128, stride=4), :].astype(jnp.float32).astype(jnp.bfloat16)
        grid = grid + dot(as_mask(row == key), counts)
    lane = iota((768, 128), 1)
    traits = jnp.zeros((768, 128), jnp.float32)
    for i in range(4):
        traits = jnp.where(lane == i, plane_ref[i], traits)
    out_ref[...] = jnp.where(slot_ref[0] >= ROWS, traits, grid)


def evaluate(square, wave, strength, weight):
    inverse = lax.rsqrt(square)
    radius = square * inverse
    phase = wave * radius
    turns = (phase * (0.5 / math.pi) + ROUNDER) - ROUNDER
    angle = (phase - turns * PI_HI) - turns * PI_LO
    arg = angle * angle
    cosine = jnp.full_like(arg, COS_COEF[-1])
    for value in COS_COEF[-2::-1]:
        cosine = cosine * arg + value
    sine = jnp.full_like(arg, SIN_COEF[-1])
    for value in SIN_COEF[-2::-1]:
        sine = sine * arg + value
    amplitude = weight * (1.0 + strength * inverse)
    return amplitude * cosine, amplitude * (angle * sine)


def fill_kernel(
    place_ref,
    position_ref,
    weight_ref,
    got_ref,
    first_ref,
    turn_ref,
    high_ref,
    low_ref,
    out_ref,
    fill_ref,
    turned_ref,
):
    device = place_ref[0]
    column = (
        iota((LIVE_BLOCKS, 128), 0) * 128 + iota((LIVE_BLOCKS, 128), 1) - HALF
    ).astype(jnp.float32)
    counts = []
    for b in range(ROWS):
        parts = [got_ref[(b * 4 + j) * 24 : (b * 4 + j) * 24 + 24, :] for j in range(4)]
        counts.append((parts[0] + parts[1]) + (parts[2] + parts[3]))
    lower = device < 256
    near_counts = jnp.where(lower, counts[3][8:16], counts[2][8:16])
    near_row = jnp.where(lower, device, device - 512).astype(jnp.float32)
    weights = [
        [jnp.where(counts[b] > float(q), weight_ref[q], 0.0) for q in range(FAR)]
        for b in range(ROWS)
    ]
    for p in range(PLANES):
        traits = got_ref[(24 + p) * 24 : (24 + p) * 24 + 1, :]
        wave, strength = traits[:, 0:1], traits[:, 1:2]
        shift_row, shift_col = traits[:, 2:3], traits[:, 3:4]
        col_base = column + shift_col
        col_sq = []
        for q in range(FAR):
            col_pos = col_base + position_ref[1, q]
            col_sq.append(col_pos * col_pos)
        extra_real = jnp.zeros((8, 128), jnp.float32)
        extra_imag = jnp.zeros((8, 128), jnp.float32)
        for q in range(FAR, NODES):
            row_pos = (near_row + shift_row) + position_ref[0, q]
            col_pos = col_base[8:16] + position_ref[1, q]
            square = row_pos * row_pos + col_pos * col_pos + HEIGHT_SQ
            weight = jnp.where(near_counts > float(q), weight_ref[q], 0.0)
            real, imag = evaluate(square, wave, strength, weight)
            extra_real = extra_real + real
            extra_imag = extra_imag + imag
        for b in range(ROWS):
            row_offset = (device + (512 * b - HALF)).astype(jnp.float32)
            total_real = jnp.zeros((LIVE_BLOCKS, 128), jnp.float32)
            total_imag = jnp.zeros((LIVE_BLOCKS, 128), jnp.float32)
            for q in range(FAR):
                row_pos = (row_offset + shift_row) + position_ref[0, q]
                square = row_pos * row_pos + col_sq[q] + HEIGHT_SQ
                real, imag = evaluate(square, wave, strength, weights[b][q])
                total_real = total_real + real
                total_imag = total_imag + imag
            lanes = slice((p * ROWS + b) * 128, (p * ROWS + b) * 128 + 128)
            fill_ref[0:24, lanes] = total_real
            fill_ref[24:48, lanes] = -total_imag
            if b in (2, 3):
                use = lower if b == 3 else jnp.logical_not(lower)
                fill_ref[8:16, lanes] = total_real[8:16] + jnp.where(use, extra_real, 0.0)
                fill_ref[32:40, lanes] = -(total_imag[8:16] + jnp.where(use, extra_imag, 0.0))
    turn_real = turn_ref[0:32, :]
    turn_imag = turn_ref[32:64, :]
    for p in range(PLANES):
        lanes = slice(p * ROWS * 128, (p + 1) * ROWS * 128)
        high, low = split(fill_ref[:, lanes])
        stage = dot(first_ref[...], jnp.concatenate([high, low, high], 0))
        for b in range(ROWS):
            real = stage[0:32, b * 128 : (b + 1) * 128]
            imag = stage[32:64, b * 128 : (b + 1) * 128]
            next_real = real * turn_real - imag * turn_imag
            next_imag = real * turn_imag + imag * turn_real
            for j in range(4):
                rows = slice(j * 8, j * 8 + 8)
                at = (j * 12 + b * 2) * 32 + p * 8
                turned_ref[at : at + 8, 0:128] = next_real[rows]
                turned_ref[at : at + 8, 128:256] = next_imag[rows]
                turned_ref[at + 32 : at + 40, 0:128] = next_imag[rows]
                turned_ref[at + 32 : at + 40, 128:256] = -next_real[rows]
    contract = (((1,), (1,)), ((), ()))
    for j in range(4):
        high, low = split(turned_ref[j * 384 : (j + 1) * 384, :])
        product = lax.dot_general(
            high_ref[...], high, contract, preferred_element_type=jnp.float32
        )
        product = product + lax.dot_general(
            high_ref[...], low, contract, preferred_element_type=jnp.float32
        )
        product = product + lax.dot_general(
            low_ref[...], high, contract, preferred_element_type=jnp.float32
        )
        for k in range(3):
            out_ref[pl.ds(j * 3 + k, 128, stride=12), :] = product[:, k * 128 : (k + 1) * 128]


def fft_list(values):
    size = len(values)
    if size == 1:
        return values
    even = fft_list(values[0::2])
    odd = fft_list(values[1::2])
    top, bottom = [], []
    for k in range(size // 2):
        real, imag = odd[k]
        if k == 0:
            pass
        elif 4 * k == size:
            real, imag = imag, -real
        elif 8 * k == size:
            half = math.sqrt(0.5)
            real, imag = (real + imag) * half, (imag - real) * half
        elif 8 * k == 3 * size:
            half = math.sqrt(0.5)
            real, imag = (imag - real) * half, -(real + imag) * half
        else:
            cos = math.cos(2.0 * math.pi * k / size)
            sin = math.sin(2.0 * math.pi * k / size)
            real, imag = real * cos + imag * sin, imag * cos - real * sin
        top.append((even[k][0] + real, even[k][1] + imag))
        bottom.append((even[k][0] - real, even[k][1] - imag))
    return top + bottom


def column_kernel(got_ref, high_ref, low_ref, turn_ref, real_ref, imag_ref, gathered_ref, stage_ref):
    blank = jnp.zeros((32, 128), jnp.float32)
    for pair in range(16):
        parts = []
        for q2 in range(2):
            for k in range(3):
                parts.append(got_ref[pl.ds((pair * 2 + q2) * 3 + k, 16, stride=96), :])
        flipped = jnp.concatenate(parts + [blank], 0).T
        for block in range(4):
            gathered_ref[pair * 32 : pair * 32 + 32, block * 128 : (block + 1) * 128] = flipped[
                block * 32 : block * 32 + 32
            ]
    for part in range(4):
        rows = slice(part * 128, (part + 1) * 128)
        high, low = split(gathered_ref[rows, :])
        stage_ref[rows, :] = (
            dot(high, high_ref[...]) + dot(low, high_ref[...]) + dot(high, low_ref[...])
        )
    for p in range(PLANES):
        values = []
        for q in range(32):
            at = (q // 2) * 32 + p * 8
            lane = (q % 2) * 256
            real = stage_ref[at : at + 8, lane : lane + 128]
            imag = stage_ref[at : at + 8, lane + 128 : lane + 256]
            if q:
                turn_real = turn_ref[q : q + 1, :]
                turn_imag = turn_ref[32 + q : 33 + q, :]
                real, imag = (
                    real * turn_real - imag * turn_imag,
                    real * turn_imag + imag * turn_real,
                )
            values.append((real, imag))
        for u, (real, imag) in enumerate(fft_list(values)):
            real_ref[p, :, u * 128 : (u + 1) * 128] = real
            imag_ref[p, :, u * 128 : (u + 1) * 128] = imag


VMEM = pl.BlockSpec(memory_space=pltpu.VMEM)
SMEM = pl.BlockSpec(memory_space=pltpu.SMEM)
PARAMS = pltpu.CompilerParams(vmem_limit_bytes=40 * 1024 * 1024)


def exchange(values, axes):
    return lax.all_to_all(values, axes, split_axis=0, concat_axis=0, tiled=True)


def shards(
    piece_ids, point_counts, wavenumber, strength, displacement, node_position, node_weights
):
    first, turn_one, second, third, turn_two = tables()
    copy = lax.axis_index("y").astype(jnp.int32).reshape(1)
    slot = (lax.axis_index("x") * 2 + lax.axis_index("core")).astype(jnp.int32).reshape(1)
    device = lax.axis_index(("z", "x", "core", "y")).astype(jnp.int32).reshape(1)
    traits = jnp.concatenate([wavenumber, strength, displacement[0], displacement[1]])
    sent = pl.pallas_call(
        sort_kernel,
        out_shape=jax.ShapeDtypeStruct((512, 128), jnp.int32),
        in_specs=[SMEM, VMEM, VMEM],
        out_specs=VMEM,
        compiler_params=PARAMS,
    )(copy, piece_ids.reshape(8, 128), point_counts)
    got = exchange(sent.reshape(128, 4, 128), ("z", "x", "core")).reshape(512, 128)
    grid = pl.pallas_call(
        place_kernel,
        out_shape=jax.ShapeDtypeStruct((768, 128), jnp.float32),
        in_specs=[SMEM, SMEM, VMEM],
        out_specs=VMEM,
        compiler_params=PARAMS,
    )(slot, traits, got)
    grid = exchange(grid, ("x", "core", "y"))
    sent = pl.pallas_call(
        fill_kernel,
        out_shape=jax.ShapeDtypeStruct((1536, 128), jnp.float32),
        in_specs=[SMEM, SMEM, SMEM] + [VMEM] * 5,
        out_specs=VMEM,
        scratch_shapes=[
            pltpu.VMEM((48, PLANES * ROWS * 128), jnp.float32),
            pltpu.VMEM((1536, 256), jnp.float32),
        ],
        compiler_params=PARAMS,
    )(device, node_position, node_weights, grid, first, turn_one, second[0], second[1])
    got = exchange(sent.reshape(1536, 1, 128), ("z", "x", "core", "y")).reshape(1536, 128)
    shape = jax.ShapeDtypeStruct((PLANES, 8, LENGTH), jnp.float32)
    return pl.pallas_call(
        column_kernel,
        out_shape=(shape, shape),
        in_specs=[VMEM] * 4,
        out_specs=(VMEM, VMEM),
        scratch_shapes=[
            pltpu.VMEM((512, 512), jnp.float32),
            pltpu.VMEM((512, 512), jnp.float32),
        ],
        compiler_params=PARAMS,
    )(got, third[0], third[1], turn_two)


def solution(mesh):
    fine = Mesh(mesh.devices.reshape(16, 4, 2, 4), ("z", "x", "core", "y"))
    wide = ("z", "x", "core")
    every = ("z", "x", "core", "y")
    placed = (P(wide), P(wide, None), P("y"), P("y"), P(None, "y"), P(), P())
    return jax.shard_map(
        shards,
        mesh=fine,
        in_specs=placed,
        out_specs=(P(None, every, None), P(None, every, None)),
        check_vma=False,
    )
```

```python
import functools
import math

import jax
import jax.numpy as jnp
import numpy as np
from jax import lax
from jax.experimental import pallas as pl
from jax.experimental.pallas import tpu as pltpu
from jax.sharding import Mesh, PartitionSpec as P

LENGTH = 4096
NODES = 15
FAR = 3
HEIGHT_SQ = 0.0625
SHARED = 3
LIVE_BLOCKS = 24
HALF = 1536
ROWS = 6
PLANES = 4

ROUNDER = 12582912.0


def fit_even(function, degree):
    top = math.pi**2
    grid = (np.cos(np.pi * (np.arange(400) + 0.5) / 400) + 1.0) * 0.5 * top
    series = np.polynomial.chebyshev.Chebyshev.fit(grid, function(np.sqrt(grid)), degree, [0, top])
    return [float(x) for x in series.convert(kind=np.polynomial.Polynomial).coef]


COS_COEF = fit_even(np.cos, 6)
SIN_COEF = fit_even(lambda x: np.sin(x) / x, 5)
COS_TURN = [c * (2.0 * math.pi) ** (2 * k) for k, c in enumerate(COS_COEF)]
SIN_TURN = [c * (2.0 * math.pi) ** (2 * k + 1) for k, c in enumerate(SIN_COEF)]


def split_np(values):
    high = values.astype(np.float32).astype(jnp.bfloat16)
    low = (values - high.astype(np.float64)).astype(jnp.bfloat16)
    return high, low


def tables():
    v1 = np.arange(32)
    cb = np.arange(LIVE_BLOCKS)
    angle = 2.0 * np.pi * (((cb[None, :] - 12) * v1[:, None]) % 32) / 32
    cos, sin = np.cos(angle), np.sin(angle)
    first = np.concatenate(
        [np.concatenate([cos, sin], 1), np.concatenate([-sin, cos], 1)], 0
    )
    high, low = split_np(first)
    first = np.concatenate([high, high, low], 1)
    t = np.arange(128)
    angle = 2.0 * np.pi * (v1[:, None] * t[None, :]) / LENGTH
    turn_one = np.concatenate([np.cos(angle), -np.sin(angle)], 0).astype(np.float32)
    angle = 2.0 * np.pi * ((t[:, None] * t[None, :]) % 128) / 128
    second = split_np(np.concatenate([np.cos(angle), np.sin(angle)], 1) / 64.0)
    c = np.arange(96)
    angle = 2.0 * np.pi * (((c[:, None] - 48) * t[None, :]) % 128) / 128
    third = np.zeros((2, 128, 2, 128))
    third[0, :96, 0] = np.cos(angle)
    third[0, :96, 1] = -np.sin(angle)
    third[1, :96, 0] = np.sin(angle)
    third[1, :96, 1] = np.cos(angle)
    third = split_np(third.reshape(256, 256) / 64.0)
    angle = 2.0 * np.pi * (v1[:, None] * t[None, :]) / LENGTH
    turn_two = np.concatenate([np.cos(angle), -np.sin(angle)], 0).astype(np.float32)
    return first, turn_one, second, third, turn_two


def iota(shape, axis):
    return lax.broadcasted_iota(jnp.int32, shape, axis)


def dot(left, right):
    return jnp.dot(left, right, preferred_element_type=jnp.float32)


def as_mask(chosen):
    return jnp.where(chosen, 1.0, 0.0).astype(jnp.bfloat16)


def split(values):
    high = values.astype(jnp.bfloat16)
    low = (values - high.astype(jnp.float32)).astype(jnp.bfloat16)
    return high, low


def sort_kernel(copy_ref, ids_hbm, counts_hbm, out_ref, ids_ref, counts_ref, sem):
    ids_copy = pltpu.make_async_copy(ids_hbm, ids_ref, sem.at[0])
    ids_copy.start()
    counts_copy = pltpu.make_async_copy(counts_hbm, counts_ref, sem.at[1])
    counts_copy.start()
    base = copy_ref[0] * SHARED
    owner = iota((128, 128), 0)
    lane = iota((128, 128), 1)
    prefix = jnp.concatenate([as_mask(owner < lane), jnp.ones((128, 128), jnp.bfloat16)], 1)
    ids_copy.wait()
    ids = ids_ref[...]
    block = ((ids >> 10) + 48) & 127
    part = block >> 4
    seat = jnp.where(part < 3, part, jnp.where(part < ROWS, part + 1, part * 4 - 21))
    target = ((block & 15) << 3) | seat
    local = ids & 1023
    high = ((local >> 5) + 1).astype(jnp.float32)
    low = (local & 31).astype(jnp.float32)
    pad = jnp.zeros((120, 128), jnp.float32)
    high = jnp.concatenate([high, pad], 0).T
    low = jnp.concatenate([low, pad], 0).T
    here = [owner == target[k : k + 1, :] for k in range(8)]
    sums = [dot(as_mask(here[k]), prefix) for k in range(8)]
    running = jnp.zeros((128, 128), jnp.float32)
    chosen = []
    for k in range(8):
        rank = running + sums[k][:, :128]
        running = running + sums[k][:, 128:]
        chosen.append(
            jnp.concatenate(
                [as_mask(here[k] & (rank == (base + s).astype(jnp.float32))) for s in range(SHARED)],
                0,
            )
        )
    counts_copy.wait()
    picked = jnp.zeros((SHARED * 128, 256), jnp.float32)
    for k in range(0, 8, 2):
        rows = []
        for m in (k, k + 1):
            counts = counts_ref[m * 128 : (m + 1) * 128, :].astype(jnp.float32)
            name = jnp.where(
                lane == 0, high[:, m : m + 1], jnp.where(lane == 1, low[:, m : m + 1], 0.0)
            )
            rows.append(jnp.concatenate([counts, name], 1).astype(jnp.bfloat16))
        picked = picked + dot(
            jnp.concatenate([chosen[k], chosen[k + 1]], 1), jnp.concatenate(rows, 0)
        )
    named = jnp.zeros((128, 128), jnp.float32)
    for s in range(SHARED):
        rows = slice(s * 128, (s + 1) * 128)
        out_ref[pl.ds(s, 128, stride=4), :] = picked[rows, :128].astype(jnp.int32)
        name = picked[rows, 128:129] * 32.0 + picked[rows, 129:130]
        named = jnp.where(lane == s, name, named)
    out_ref[pl.ds(3, 128, stride=4), :] = named.astype(jnp.int32)


def place_kernel(seat_ref, traits_ref, got_ref, out_ref):
    names = got_ref[pl.ds(3, 128, stride=4), :].astype(jnp.float32).T
    row = iota((768, 128), 0)
    masks, counts = [], []
    for s in range(SHARED):
        name = names[s : s + 1, :].astype(jnp.int32)
        column = ((name & 31) + 12) & 31
        valid = (name > 0) & (column < LIVE_BLOCKS)
        key = jnp.where(valid, ((name >> 5) - 1) * LIVE_BLOCKS + column, -1)
        masks.append(as_mask(row == key))
        counts.append(got_ref[pl.ds(s, 128, stride=4), :].astype(jnp.float32).astype(jnp.bfloat16))
    vacant = seat_ref[0] == 3

    @pl.when(vacant)
    def _():
        out_ref[...] = jnp.broadcast_to(traits_ref[0:1, :], (768, 128))

    @pl.when(jnp.logical_not(vacant))
    def _():
        out_ref[...] = dot(jnp.concatenate(masks, 1), jnp.concatenate(counts, 0))


def evaluate(square, wave, strength, weight):
    inverse = lax.rsqrt(square)
    turns = wave * (square * inverse)
    turns = turns - ((turns + ROUNDER) - ROUNDER)
    arg = turns * turns
    cosine = COS_TURN[-1] * arg + COS_TURN[-2]
    for value in COS_TURN[-3::-1]:
        cosine = cosine * arg + value
    sine = SIN_TURN[-1] * arg + SIN_TURN[-2]
    for value in SIN_TURN[-3::-1]:
        sine = sine * arg + value
    amplitude = weight * (1.0 + strength * inverse)
    return amplitude * cosine, amplitude * (turns * sine)


def fill_kernel(
    place_ref,
    got_ref,
    first_ref,
    turn_ref,
    high_ref,
    low_ref,
    out_ref,
    near_ref,
    fill_ref,
    turned_ref,
):
    device = place_ref[0]
    z = device >> 5
    side = (device >> 4) & 1
    base = z * 32 + side * HALF + (device & 15) * 2 - HALF
    column = (
        iota((LIVE_BLOCKS, 128), 0) * 128 + iota((LIVE_BLOCKS, 128), 1) - HALF
    ).astype(jnp.float32)
    traits = [got_ref[(12 + p) * 48 : (12 + p) * 48 + 1, :] for p in range(PLANES)]
    counts = []
    for b in range(ROWS):
        parts = []
        for j in range(4):
            at = ((b // 2) * 4 + j) * 48 + (b % 2) * 24
            parts.append(got_ref[at : at + 24, :])
        counts.append((parts[0] + parts[1]) + (parts[2] + parts[3]))
    right = side == 1
    near_ref[...] = jnp.zeros((8, 128), jnp.float32)
    for m in range(2):
        near_ref[m * 2 : m * 2 + 2, :] = jnp.where(right, counts[m][11:13], counts[4 + m][11:13])
    near_counts = near_ref[...]
    sub = iota((8, 128), 0)
    near_row = (base + jnp.where(right, 0, 1024) + (sub >> 1)).astype(jnp.float32)
    near_col = ((sub & 1) * 128 + iota((8, 128), 1) - 128).astype(jnp.float32)
    node_row = [traits[0][:, 16 + q : 17 + q] for q in range(NODES)]
    node_col = [traits[0][:, 32 + q : 33 + q] for q in range(NODES)]
    node_weight = [traits[0][:, 48 + q : 49 + q] for q in range(NODES)]
    weights = [
        [jnp.where(counts[b] > float(q), node_weight[q], 0.0) for q in range(FAR)]
        for b in range(ROWS)
    ]
    near_weights = [jnp.where(near_counts > float(q), node_weight[q], 0.0) for q in range(NODES)]
    turn_real = turn_ref[0:32, :]
    turn_imag = turn_ref[32:64, :]
    for p in range(PLANES):
        wave, strength = traits[p][:, 0:1] * (0.5 / math.pi), traits[p][:, 1:2]
        shift_row, shift_col = traits[p][:, 2:3], traits[p][:, 3:4]
        col_base = column + shift_col
        col_sq = []
        for q in range(FAR):
            col_pos = col_base + node_col[q]
            col_sq.append(col_pos * col_pos)
        extra_real = jnp.zeros((8, 128), jnp.float32)
        extra_imag = jnp.zeros((8, 128), jnp.float32)
        for q in range(FAR, NODES):
            row_pos = (near_row + shift_row) + node_row[q]
            col_pos = (near_col + shift_col) + node_col[q]
            square = row_pos * row_pos + col_pos * col_pos + HEIGHT_SQ
            real, imag = evaluate(square, wave, strength, near_weights[q])
            extra_real = extra_real + real
            extra_imag = extra_imag + imag
        for b in range(ROWS):
            row_offset = (base + (512 * (b // 2) + b % 2)).astype(jnp.float32)
            total_real = jnp.zeros((LIVE_BLOCKS, 128), jnp.float32)
            total_imag = jnp.zeros((LIVE_BLOCKS, 128), jnp.float32)
            for q in range(FAR):
                row_pos = (row_offset + shift_row) + node_row[q]
                square = col_sq[q] + (row_pos * row_pos + HEIGHT_SQ)
                real, imag = evaluate(square, wave, strength, weights[b][q])
                total_real = total_real + real
                total_imag = total_imag + imag
            lanes = slice((p * ROWS + b) * 128, (p * ROWS + b) * 128 + 128)
            fill_ref[0:24, lanes] = total_real
            fill_ref[24:48, lanes] = -total_imag
            if b // 2 != 1:
                use = right if b // 2 == 0 else jnp.logical_not(right)
                m = (b % 2) * 2
                fill_ref[11:13, lanes] = fill_ref[11:13, lanes] + jnp.where(
                    use, extra_real[m : m + 2], 0.0
                )
                fill_ref[35:37, lanes] = fill_ref[35:37, lanes] - jnp.where(
                    use, extra_imag[m : m + 2], 0.0
                )
        lanes = slice(p * ROWS * 128, (p + 1) * ROWS * 128)
        high, low = split(fill_ref[:, lanes])
        stage = dot(first_ref[...], jnp.concatenate([high, low, high], 0))
        for b in range(ROWS):
            real = stage[0:32, b * 128 : (b + 1) * 128]
            imag = stage[32:64, b * 128 : (b + 1) * 128]
            next_real = real * turn_real - imag * turn_imag
            next_imag = real * turn_imag + imag * turn_real
            for j in range(4):
                rows = slice(j * 8, j * 8 + 8)
                at = ((j * 3 + b // 2) * 4 + (b % 2) * 2) * 32 + p * 8
                turned_ref[at : at + 8, 0:128] = next_real[rows]
                turned_ref[at : at + 8, 128:256] = next_imag[rows]
                turned_ref[at + 32 : at + 40, 0:128] = next_imag[rows]
                turned_ref[at + 32 : at + 40, 128:256] = -next_real[rows]
    contract = (((1,), (1,)), ((), ()))
    for j in range(4):
        high, low = split(turned_ref[j * 384 : (j + 1) * 384, :])
        product = lax.dot_general(
            high_ref[...], high, contract, preferred_element_type=jnp.float32
        )
        product = product + lax.dot_general(
            high_ref[...], low, contract, preferred_element_type=jnp.float32
        )
        product = product + lax.dot_general(
            low_ref[...], high, contract, preferred_element_type=jnp.float32
        )
        for k in range(3):
            out_ref[pl.ds(j * 3 + k, 128, stride=12), :] = product[:, k * 128 : (k + 1) * 128]


def fft_list(values):
    size = len(values)
    if size == 1:
        return values
    even = fft_list(values[0::2])
    odd = fft_list(values[1::2])
    top, bottom = [], []
    for k in range(size // 2):
        real, imag = odd[k]
        if k == 0:
            pass
        elif 4 * k == size:
            real, imag = imag, -real
        elif 8 * k == size:
            half = math.sqrt(0.5)
            real, imag = (real + imag) * half, (imag - real) * half
        elif 8 * k == 3 * size:
            half = math.sqrt(0.5)
            real, imag = (imag - real) * half, -(real + imag) * half
        else:
            cos = math.cos(2.0 * math.pi * k / size)
            sin = math.sin(2.0 * math.pi * k / size)
            real, imag = real * cos + imag * sin, imag * cos - real * sin
        top.append((even[k][0] + real, even[k][1] + imag))
        bottom.append((even[k][0] - real, even[k][1] - imag))
    return top + bottom


def column_kernel(
    got_ref,
    high_ref,
    low_ref,
    turn_ref,
    real_hbm,
    imag_hbm,
    gathered_ref,
    stage_ref,
    real_ref,
    imag_ref,
    sem,
):
    blank = jnp.zeros((32, 128), jnp.float32)
    for pair in range(16):
        parts = []
        for side in range(2):
            for k in range(3):
                parts.append(got_ref[pl.ds((side * 16 + pair) * 3 + k, 16, stride=96), :])
        flipped = jnp.concatenate(parts + [blank], 0).T
        for m in range(2):
            for ri in range(2):
                at = (pair * 2 + m) * 32
                gathered_ref[at : at + 32, ri * 128 : (ri + 1) * 128] = flipped[
                    (m * 2 + ri) * 32 : (m * 2 + ri) * 32 + 32
                ]
    for part in range(4):
        rows = slice(part * 256, (part + 1) * 256)
        high, low = split(gathered_ref[rows, :])
        stage_ref[rows, :] = (
            dot(high, high_ref[...]) + dot(low, high_ref[...]) + dot(high, low_ref[...])
        )
    copies = []
    for p in range(PLANES):
        values = []
        for r in range(32):
            at = r * 32 + p * 8
            real = stage_ref[at : at + 8, 0:128]
            imag = stage_ref[at : at + 8, 128:256]
            if r:
                turn_real = turn_ref[r : r + 1, :]
                turn_imag = turn_ref[32 + r : 33 + r, :]
                real, imag = (
                    real * turn_real - imag * turn_imag,
                    real * turn_imag + imag * turn_real,
                )
            values.append((real, imag))
        for u, (real, imag) in enumerate(fft_list(values)):
            real_ref[p, :, u * 128 : (u + 1) * 128] = real
            imag_ref[p, :, u * 128 : (u + 1) * 128] = imag
        for m, (source, target) in enumerate(((real_ref, real_hbm), (imag_ref, imag_hbm))):
            copy = pltpu.make_async_copy(source.at[p], target.at[p], sem.at[p * 2 + m])
            copy.start()
            copies.append(copy)
    for copy in copies:
        copy.wait()


VMEM = pl.BlockSpec(memory_space=pltpu.VMEM)
SMEM = pl.BlockSpec(memory_space=pltpu.SMEM)
HBM = pl.BlockSpec(memory_space=pltpu.HBM)
PARAMS = pltpu.CompilerParams(vmem_limit_bytes=40 * 1024 * 1024)


def exchange(values, axes):
    return lax.all_to_all(values, axes, split_axis=0, concat_axis=0, tiled=True)


def shards(
    piece_ids, point_counts, wavenumber, strength, displacement, node_position, node_weights
):
    first, turn_one, second, third, turn_two = tables()
    copy = lax.axis_index("y").astype(jnp.int32).reshape(1)
    seat = lax.axis_index(("x_low", "core")).astype(jnp.int32).reshape(1)
    device = lax.axis_index(("z", "x_high", "x_low", "core", "y")).astype(jnp.int32).reshape(1)
    traits = jnp.concatenate([wavenumber, strength, displacement[0], displacement[1]])
    traits = jnp.concatenate(
        [
            jnp.pad(traits, (0, 12)),
            jnp.pad(node_position, ((0, 0), (0, 1))).reshape(32),
            jnp.pad(node_weights, (0, 65)),
        ]
    ).reshape(1, 128)
    sent = pl.pallas_call(
        sort_kernel,
        out_shape=jax.ShapeDtypeStruct((512, 128), jnp.int32),
        in_specs=[SMEM, HBM, HBM],
        out_specs=VMEM,
        scratch_shapes=[
            pltpu.VMEM((8, 128), jnp.int32),
            pltpu.VMEM((1024, 128), jnp.int32),
            pltpu.SemaphoreType.DMA((2,)),
        ],
        compiler_params=PARAMS,
    )(copy, piece_ids.reshape(8, 128), point_counts)
    got = exchange(sent.reshape(128, 4, 128), ("z", "x_high", "x_low", "core")).reshape(512, 128)
    grid = pl.pallas_call(
        place_kernel,
        out_shape=jax.ShapeDtypeStruct((768, 128), jnp.float32),
        in_specs=[SMEM, VMEM, VMEM],
        out_specs=VMEM,
        compiler_params=PARAMS,
    )(seat, traits, got)
    grid = exchange(grid, ("x_low", "core", "y"))
    sent = pl.pallas_call(
        fill_kernel,
        out_shape=jax.ShapeDtypeStruct((1536, 128), jnp.float32),
        in_specs=[SMEM] + [VMEM] * 5,
        out_specs=VMEM,
        scratch_shapes=[
            pltpu.VMEM((8, 128), jnp.float32),
            pltpu.VMEM((48, PLANES * ROWS * 128), jnp.float32),
            pltpu.VMEM((1536, 256), jnp.float32),
        ],
        compiler_params=PARAMS,
    )(device, grid, first, turn_one, second[0], second[1])
    got = exchange(
        sent.reshape(1536, 1, 128), ("z", "x_high", "x_low", "core", "y")
    ).reshape(1536, 128)
    shape = jax.ShapeDtypeStruct((PLANES, 8, LENGTH), jnp.float32)
    return pl.pallas_call(
        column_kernel,
        out_shape=(shape, shape),
        in_specs=[VMEM] * 4,
        out_specs=(HBM, HBM),
        scratch_shapes=[
            pltpu.VMEM((1024, 256), jnp.float32),
            pltpu.VMEM((1024, 256), jnp.float32),
            pltpu.VMEM((PLANES, 8, LENGTH), jnp.float32),
            pltpu.VMEM((PLANES, 8, LENGTH), jnp.float32),
            pltpu.SemaphoreType.DMA((2 * PLANES,)),
        ],
        compiler_params=PARAMS,
    )(got, third[0], third[1], turn_two)


def solution(mesh):
    every = ("z", "x_high", "x_low", "core", "y")
    fine = Mesh(mesh.devices.reshape(16, 2, 2, 2, 4), every)
    wide = every[:4]
    placed = (P(wide), P(wide, None), P("y"), P("y"), P(None, "y"), P(), P())
    return jax.shard_map(
        shards,
        mesh=fine,
        in_specs=placed,
        out_specs=(P(None, every, None), P(None, every, None)),
        check_vma=False,
    )
```

```python
import functools
import math

import jax
import jax.numpy as jnp
import numpy as np
from jax import lax
from jax.experimental import pallas as pl
from jax.experimental.pallas import tpu as pltpu
from jax.sharding import Mesh, PartitionSpec as P

LENGTH = 4096
NODES = 15
FAR = 3
HEIGHT_SQ = 0.0625
SHARED = 3
LIVE_BLOCKS = 24
HALF = 1536
ROWS = 6
PLANES = 4

ROUNDER = 12582912.0


def fit_even(function, degree):
    top = math.pi**2
    grid = (np.cos(np.pi * (np.arange(400) + 0.5) / 400) + 1.0) * 0.5 * top
    series = np.polynomial.chebyshev.Chebyshev.fit(grid, function(np.sqrt(grid)), degree, [0, top])
    return [float(x) for x in series.convert(kind=np.polynomial.Polynomial).coef]


COS_COEF = fit_even(np.cos, 6)
SIN_COEF = fit_even(lambda x: np.sin(x) / x, 5)
COS_TURN = [c * (2.0 * math.pi) ** (2 * k) for k, c in enumerate(COS_COEF)]
SIN_TURN = [c * (2.0 * math.pi) ** (2 * k + 1) for k, c in enumerate(SIN_COEF)]


def split_np(values):
    high = values.astype(np.float32).astype(jnp.bfloat16)
    low = (values - high.astype(np.float64)).astype(jnp.bfloat16)
    return high, low


def tables():
    v1 = np.arange(32)
    cb = np.arange(LIVE_BLOCKS)
    angle = 2.0 * np.pi * (((cb[None, :] - 12) * v1[:, None]) % 32) / 32
    cos, sin = np.cos(angle), np.sin(angle)
    first = np.concatenate(
        [np.concatenate([cos, sin], 1), np.concatenate([-sin, cos], 1)], 0
    )
    high, low = split_np(first)
    first = np.concatenate([high, high, low], 1)
    t = np.arange(128)
    angle = 2.0 * np.pi * (v1[:, None] * t[None, :]) / LENGTH
    turn_one = np.concatenate([np.cos(angle), -np.sin(angle)], 0).astype(np.float32)
    angle = 2.0 * np.pi * ((t[:, None] * t[None, :]) % 128) / 128
    second = split_np(np.concatenate([np.cos(angle), np.sin(angle)], 1) / 64.0)
    c = np.arange(96)
    angle = 2.0 * np.pi * (((c[:, None] - 48) * t[None, :]) % 128) / 128
    third = np.zeros((2, 128, 2, 128))
    third[0, :96, 0] = np.cos(angle)
    third[0, :96, 1] = -np.sin(angle)
    third[1, :96, 0] = np.sin(angle)
    third[1, :96, 1] = np.cos(angle)
    third = split_np(third.reshape(256, 256) / 64.0)
    angle = 2.0 * np.pi * (v1[:, None] * t[None, :]) / LENGTH
    turn_two = np.concatenate([np.cos(angle), -np.sin(angle)], 0).astype(np.float32)
    return first, turn_one, second, third, turn_two


def iota(shape, axis):
    return lax.broadcasted_iota(jnp.int32, shape, axis)


def dot(left, right):
    return jnp.dot(left, right, preferred_element_type=jnp.float32)


def as_mask(chosen):
    return jnp.where(chosen, 1.0, 0.0).astype(jnp.bfloat16)


def split(values):
    high = values.astype(jnp.bfloat16)
    low = (values - high.astype(jnp.float32)).astype(jnp.bfloat16)
    return high, low


def sort_kernel(copy_ref, ids_hbm, counts_hbm, out_ref, ids_ref, counts_ref, sem):
    ids_copy = pltpu.make_async_copy(ids_hbm, ids_ref, sem.at[0])
    ids_copy.start()
    counts_copy = pltpu.make_async_copy(counts_hbm, counts_ref, sem.at[1])
    counts_copy.start()
    base = copy_ref[0] * SHARED
    owner = iota((128, 128), 0)
    lane = iota((128, 128), 1)
    prefix = jnp.concatenate([as_mask(owner < lane), jnp.ones((128, 128), jnp.bfloat16)], 1)
    ids_copy.wait()
    ids = ids_ref[...]
    block = ((ids >> 10) + 48) & 127
    part = block >> 4
    side = jnp.where(part < 3, 0, 1)
    target = (part - 3 * side) * 32 + ((block & 15) << 1) + side
    target = jnp.where(part < ROWS, target, block)
    local = ids & 1023
    high = ((local >> 5) + 1).astype(jnp.float32)
    low = (local & 31).astype(jnp.float32)
    pad = jnp.zeros((120, 128), jnp.float32)
    high = jnp.concatenate([high, pad], 0).T
    low = jnp.concatenate([low, pad], 0).T
    here = [owner == target[k : k + 1, :] for k in range(8)]
    sums = [dot(as_mask(here[k]), prefix) for k in range(8)]
    running = jnp.zeros((128, 128), jnp.float32)
    chosen = []
    for k in range(8):
        rank = running + sums[k][:, :128]
        running = running + sums[k][:, 128:]
        chosen.append(
            jnp.concatenate(
                [as_mask(here[k] & (rank == (base + s).astype(jnp.float32))) for s in range(SHARED)],
                0,
            )
        )
    counts_copy.wait()
    picked = jnp.zeros((SHARED * 128, 256), jnp.float32)
    for k in range(0, 8, 2):
        rows = []
        for m in (k, k + 1):
            counts = counts_ref[m * 128 : (m + 1) * 128, :].astype(jnp.float32)
            name = jnp.where(
                lane == 0, high[:, m : m + 1], jnp.where(lane == 1, low[:, m : m + 1], 0.0)
            )
            rows.append(jnp.concatenate([counts, name], 1).astype(jnp.bfloat16))
        picked = picked + dot(
            jnp.concatenate([chosen[k], chosen[k + 1]], 1), jnp.concatenate(rows, 0)
        )
    named = jnp.zeros((32, 128), jnp.float32)
    for i in range(3):
        for s in range(SHARED):
            rows = slice(s * 128 + i * 32, s * 128 + i * 32 + 32)
            out_ref[pl.ds(i * SHARED + s, 32, stride=10), :] = picked[rows, :128]
            name = picked[rows, 128:129] * 32.0 + picked[rows, 129:130]
            named = jnp.where(lane[:32] == i * SHARED + s, name, named)
    out_ref[pl.ds(9, 32, stride=10), :] = named


def place_kernel(core_ref, traits_ref, got_ref, out_ref):
    names = got_ref[pl.ds(9, 64, stride=10), :]
    names = jnp.concatenate([names, pltpu.roll(names, 127, 1)], 0).T
    cell = iota((384, 128), 0)
    row = iota((48, 128), 0)
    first_lane = iota((48, 128), 1) == 0
    for i in range(3):
        masks, counts = [], []
        for s, width in ((0, 128), (2, 64)):
            name = names[i * SHARED + s : i * SHARED + s + 1, :width].astype(jnp.int32)
            line = (name >> 5) - 1
            column = ((name & 31) + 12) & 31
            valid = (name > 0) & (column < LIVE_BLOCKS) & (((line >> 3) & 1) == core_ref[0])
            seat = (line >> 4) * 4 + ((line >> 1) & 3)
            key = jnp.where(valid, seat * 48 + (line & 1) * 24 + column, -1)
            masks.append(as_mask(cell[:, :width] == key))
        for s in range(SHARED):
            counts.append(got_ref[pl.ds(i * SHARED + s, 64, stride=10), :].astype(jnp.bfloat16))
        grid = dot(jnp.concatenate(masks, 1), jnp.concatenate(counts, 0))
        extra = jnp.zeros((48, 128), jnp.float32)
        if i < 2:
            for m in range(2):
                extra = jnp.where(first_lane & (row == m * 24), traits_ref[i * 2 + m], extra)
        for d in range(8):
            out_ref[d * 144 + i * 48 : d * 144 + i * 48 + 48, :] = (
                grid[d * 48 : d * 48 + 48] + extra
            )


def evaluate(square, wave, strength, weight):
    inverse = lax.rsqrt(square)
    turns = wave * (square * inverse)
    turns = turns - ((turns + ROUNDER) - ROUNDER)
    arg = turns * turns
    cosine = COS_TURN[-1] * arg + COS_TURN[-2]
    for value in COS_TURN[-3::-1]:
        cosine = cosine * arg + value
    sine = SIN_TURN[-1] * arg + SIN_TURN[-2]
    for value in SIN_TURN[-3::-1]:
        sine = sine * arg + value
    amplitude = weight * (1.0 + strength * inverse)
    return amplitude * cosine, amplitude * (turns * sine)


def fill_kernel(
    place_ref,
    nodes_ref,
    got_ref,
    first_ref,
    turn_ref,
    high_ref,
    low_ref,
    out_ref,
    near_ref,
    fill_ref,
    turned_ref,
):
    base = place_ref[0]
    right = place_ref[1] == 1
    column = (
        iota((LIVE_BLOCKS, 128), 0) * 128 + iota((LIVE_BLOCKS, 128), 1) - HALF
    ).astype(jnp.float32)
    traits = [
        [got_ref[p * 144 + e * 24 : p * 144 + e * 24 + 1, 0:1] for e in range(4)]
        for p in range(PLANES)
    ]
    counts = []
    for b in range(ROWS):
        parts = [got_ref[m * 144 + b * 24 : m * 144 + b * 24 + 24, :] for m in range(8)]
        while len(parts) > 1:
            parts = [parts[m] + parts[m + 1] for m in range(0, len(parts), 2)]
        counts.append(jnp.where(column > -float(HALF), parts[0], 0.0))
    lane = iota((8, 128), 1)
    inner = lane < 64
    for m in range(2):
        pair = jnp.where(right, counts[m][11:13], counts[4 + m][11:13])
        merged = jnp.where(inner[0:1], pair[1:2], pair[0:1])
        for p in range(PLANES):
            near_ref[p * 2 + m : p * 2 + m + 1, :] = merged
    for p in range(PLANES):
        for e in range(4):
            at = 8 + e * 8 + p * 2
            near_ref[at : at + 2, :] = jnp.broadcast_to(traits[p][e], (2, 128))
    near_counts = near_ref[0:8, :]
    near_row = (base + jnp.where(right, 0, 1024) + (iota((8, 128), 0) & 1)).astype(jnp.float32)
    near_row = near_row + near_ref[24:32, :]
    near_col = jnp.where(inner, lane, lane - 128).astype(jnp.float32) + near_ref[32:40, :]
    near_wave = near_ref[8:16, :] * (0.5 / math.pi)
    near_strength = near_ref[16:24, :]
    node_row = [nodes_ref[:, q : q + 1] for q in range(NODES)]
    node_col = [nodes_ref[:, 16 + q : 17 + q] for q in range(NODES)]
    node_weight = [nodes_ref[:, 32 + q : 33 + q] for q in range(NODES)]
    weights = [
        [jnp.where(counts[b] > float(q), node_weight[q], 0.0) for q in range(FAR)]
        for b in range(ROWS)
    ]
    extra_real = jnp.zeros((8, 128), jnp.float32)
    extra_imag = jnp.zeros((8, 128), jnp.float32)
    for q in range(FAR, NODES):
        row_pos = near_row + node_row[q]
        col_pos = near_col + node_col[q]
        square = row_pos * row_pos + col_pos * col_pos + HEIGHT_SQ
        weight = jnp.where(near_counts > float(q), node_weight[q], 0.0)
        real, imag = evaluate(square, near_wave, near_strength, weight)
        extra_real = extra_real + real
        extra_imag = extra_imag + imag
    inner_pair = (iota((2, 128), 0) == 1) == inner[0:2]
    turn_real = turn_ref[0:32, :]
    turn_imag = turn_ref[32:64, :]
    for p in range(PLANES):
        wave, strength = traits[p][0] * (0.5 / math.pi), traits[p][1]
        shift_row, shift_col = traits[p][2], traits[p][3]
        col_base = column + shift_col
        col_sq = []
        for q in range(FAR):
            col_pos = col_base + node_col[q]
            col_sq.append(col_pos * col_pos)
        for b in range(ROWS):
            row_offset = (base + (512 * (b // 2) + b % 2)).astype(jnp.float32)
            total_real = jnp.zeros((LIVE_BLOCKS, 128), jnp.float32)
            total_imag = jnp.zeros((LIVE_BLOCKS, 128), jnp.float32)
            for q in range(FAR):
                row_pos = (row_offset + shift_row) + node_row[q]
                square = col_sq[q] + (row_pos * row_pos + HEIGHT_SQ)
                real, imag = evaluate(square, wave, strength, weights[b][q])
                total_real = total_real + real
                total_imag = total_imag + imag
            lanes = slice((p * ROWS + b) * 128, (p * ROWS + b) * 128 + 128)
            fill_ref[0:24, lanes] = total_real
            fill_ref[24:48, lanes] = -total_imag
            if b // 2 != 1:
                use = right if b // 2 == 0 else jnp.logical_not(right)
                use = use & inner_pair
                m = p * 2 + b % 2
                fill_ref[11:13, lanes] = fill_ref[11:13, lanes] + jnp.where(
                    use, extra_real[m : m + 1], 0.0
                )
                fill_ref[35:37, lanes] = fill_ref[35:37, lanes] - jnp.where(
                    use, extra_imag[m : m + 1], 0.0
                )
        lanes = slice(p * ROWS * 128, (p + 1) * ROWS * 128)
        high, low = split(fill_ref[:, lanes])
        stage = dot(first_ref[...], jnp.concatenate([high, low, high], 0))
        for b in range(ROWS):
            real = stage[0:32, b * 128 : (b + 1) * 128]
            imag = stage[32:64, b * 128 : (b + 1) * 128]
            next_real = real * turn_real - imag * turn_imag
            next_imag = real * turn_imag + imag * turn_real
            for j in range(4):
                rows = slice(j * 8, j * 8 + 8)
                at = ((j * 3 + b // 2) * 4 + (b % 2) * 2) * 32 + p * 8
                turned_ref[at : at + 8, 0:128] = next_real[rows]
                turned_ref[at : at + 8, 128:256] = next_imag[rows]
                turned_ref[at + 32 : at + 40, 0:128] = next_imag[rows]
                turned_ref[at + 32 : at + 40, 128:256] = -next_real[rows]
    contract = (((1,), (1,)), ((), ()))
    for j in range(4):
        high, low = split(turned_ref[j * 384 : (j + 1) * 384, :])
        product = lax.dot_general(
            high_ref[...], high, contract, preferred_element_type=jnp.float32
        )
        product = product + lax.dot_general(
            high_ref[...], low, contract, preferred_element_type=jnp.float32
        )
        product = product + lax.dot_general(
            low_ref[...], high, contract, preferred_element_type=jnp.float32
        )
        for k in range(3):
            out_ref[pl.ds(j * 3 + k, 128, stride=12), :] = product[:, k * 128 : (k + 1) * 128]


def fft_list(values):
    size = len(values)
    if size == 1:
        return values
    even = fft_list(values[0::2])
    odd = fft_list(values[1::2])
    top, bottom = [], []
    for k in range(size // 2):
        real, imag = odd[k]
        if k == 0:
            pass
        elif 4 * k == size:
            real, imag = imag, -real
        elif 8 * k == size:
            half = math.sqrt(0.5)
            real, imag = (real + imag) * half, (imag - real) * half
        elif 8 * k == 3 * size:
            half = math.sqrt(0.5)
            real, imag = (imag - real) * half, -(real + imag) * half
        else:
            cos = math.cos(2.0 * math.pi * k / size)
            sin = math.sin(2.0 * math.pi * k / size)
            real, imag = real * cos + imag * sin, imag * cos - real * sin
        top.append((even[k][0] + real, even[k][1] + imag))
        bottom.append((even[k][0] - real, even[k][1] - imag))
    return top + bottom


def column_kernel(
    got_ref,
    high_ref,
    low_ref,
    turn_ref,
    real_hbm,
    imag_hbm,
    gathered_ref,
    stage_ref,
    real_ref,
    imag_ref,
    sem,
):
    blank = jnp.zeros((32, 128), jnp.float32)
    for pair in range(16):
        parts = []
        for side in range(2):
            for k in range(3):
                parts.append(got_ref[pl.ds((side * 16 + pair) * 3 + k, 16, stride=96), :])
        flipped = jnp.concatenate(parts + [blank], 0).T
        for m in range(2):
            for ri in range(2):
                at = (pair * 2 + m) * 32
                gathered_ref[at : at + 32, ri * 128 : (ri + 1) * 128] = flipped[
                    (m * 2 + ri) * 32 : (m * 2 + ri) * 32 + 32
                ]
    for part in range(4):
        rows = slice(part * 256, (part + 1) * 256)
        high, low = split(gathered_ref[rows, :])
        stage_ref[rows, :] = (
            dot(high, high_ref[...]) + dot(low, high_ref[...]) + dot(high, low_ref[...])
        )
    copies = []
    for p in range(PLANES):
        values = []
        for r in range(32):
            at = r * 32 + p * 8
            real = stage_ref[at : at + 8, 0:128]
            imag = stage_ref[at : at + 8, 128:256]
            if r:
                turn_real = turn_ref[r : r + 1, :]
                turn_imag = turn_ref[32 + r : 33 + r, :]
                real, imag = (
                    real * turn_real - imag * turn_imag,
                    real * turn_imag + imag * turn_real,
                )
            values.append((real, imag))
        for u, (real, imag) in enumerate(fft_list(values)):
            real_ref[p, :, u * 128 : (u + 1) * 128] = real
            imag_ref[p, :, u * 128 : (u + 1) * 128] = imag
        for m, (source, target) in enumerate(((real_ref, real_hbm), (imag_ref, imag_hbm))):
            copy = pltpu.make_async_copy(source.at[p], target.at[p], sem.at[p * 2 + m])
            copy.start()
            copies.append(copy)
    for copy in copies:
        copy.wait()


VMEM = pl.BlockSpec(memory_space=pltpu.VMEM)
SMEM = pl.BlockSpec(memory_space=pltpu.SMEM)
HBM = pl.BlockSpec(memory_space=pltpu.HBM)
PARAMS = pltpu.CompilerParams(vmem_limit_bytes=40 * 1024 * 1024)


def exchange(values, axes):
    return lax.all_to_all(values, axes, split_axis=0, concat_axis=0, tiled=True)


def shards(
    piece_ids, point_counts, wavenumber, strength, displacement, node_position, node_weights
):
    first, turn_one, second, third, turn_two = tables()
    copy = lax.axis_index("y").astype(jnp.int32)
    core = lax.axis_index("core").astype(jnp.int32)
    side = lax.axis_index("x_high").astype(jnp.int32)
    seat = lax.axis_index(("x_low", "core", "y")).astype(jnp.int32)
    base = lax.axis_index("z").astype(jnp.int32) * 32 + (side - 1) * HALF + seat * 2
    traits = jnp.concatenate([wavenumber, strength, displacement[0], displacement[1]])
    nodes = jnp.concatenate(
        [
            jnp.pad(node_position, ((0, 0), (0, 1))).reshape(32),
            jnp.pad(node_weights, (0, 81)),
        ]
    ).reshape(1, 128)
    sent = pl.pallas_call(
        sort_kernel,
        out_shape=jax.ShapeDtypeStruct((320, 128), jnp.float32),
        in_specs=[SMEM, HBM, HBM],
        out_specs=VMEM,
        scratch_shapes=[
            pltpu.VMEM((8, 128), jnp.int32),
            pltpu.VMEM((1024, 128), jnp.int32),
            pltpu.SemaphoreType.DMA((2,)),
        ],
        compiler_params=pltpu.CompilerParams(vmem_limit_bytes=62 * 1024 * 1024),
    )(copy.reshape(1), piece_ids.reshape(8, 128), point_counts)
    got = exchange(sent.reshape(320, 1, 128), ("z", "x_high")).reshape(320, 128)
    got = lax.all_gather(got, "core", axis=0, tiled=True)
    grid = pl.pallas_call(
        place_kernel,
        out_shape=jax.ShapeDtypeStruct((1152, 128), jnp.float32),
        in_specs=[SMEM, SMEM, VMEM],
        out_specs=VMEM,
        compiler_params=PARAMS,
    )(core.reshape(1), traits, got)
    grid = exchange(grid.reshape(1152, 1, 128), ("x_low", "y")).reshape(1152, 128)
    sent = pl.pallas_call(
        fill_kernel,
        out_shape=jax.ShapeDtypeStruct((1536, 128), jnp.float32),
        in_specs=[SMEM] + [VMEM] * 6,
        out_specs=VMEM,
        scratch_shapes=[
            pltpu.VMEM((40, 128), jnp.float32),
            pltpu.VMEM((48, PLANES * ROWS * 128), jnp.float32),
            pltpu.VMEM((1536, 256), jnp.float32),
        ],
        compiler_params=PARAMS,
    )(jnp.stack([base, side]), nodes, grid, first, turn_one, second[0], second[1])
    got = exchange(
        sent.reshape(1536, 1, 128), ("z", "x_high", "x_low", "core", "y")
    ).reshape(1536, 128)
    shape = jax.ShapeDtypeStruct((PLANES, 8, LENGTH), jnp.float32)
    return pl.pallas_call(
        column_kernel,
        out_shape=(shape, shape),
        in_specs=[VMEM] * 4,
        out_specs=(HBM, HBM),
        scratch_shapes=[
            pltpu.VMEM((1024, 256), jnp.float32),
            pltpu.VMEM((1024, 256), jnp.float32),
            pltpu.VMEM((PLANES, 8, LENGTH), jnp.float32),
            pltpu.VMEM((PLANES, 8, LENGTH), jnp.float32),
            pltpu.SemaphoreType.DMA((2 * PLANES,)),
        ],
        compiler_params=PARAMS,
    )(got, third[0], third[1], turn_two)


def solution(mesh):
    every = ("z", "x_high", "x_low", "core", "y")
    fine = Mesh(mesh.devices.reshape(16, 2, 2, 2, 4), every)
    wide = every[:4]
    placed = (P(wide), P(wide, None), P("y"), P("y"), P(None, "y"), P(), P())
    return jax.shard_map(
        shards,
        mesh=fine,
        in_specs=placed,
        out_specs=(P(None, every, None), P(None, every, None)),
        check_vma=False,
    )
```

```python
import functools
import math

import jax
import jax.numpy as jnp
import numpy as np
from jax import lax
from jax.experimental import pallas as pl
from jax.experimental.pallas import tpu as pltpu
from jax.sharding import Mesh, PartitionSpec as P

LENGTH = 4096
NODES = 15
FAR = 3
HEIGHT_SQ = 0.0625
SHARED = 3
LIVE_BLOCKS = 24
HALF = 1536
ROWS = 6
PLANES = 4

ROUNDER = 12582912.0


def fit_even(function, degree):
    top = math.pi**2
    grid = (np.cos(np.pi * (np.arange(400) + 0.5) / 400) + 1.0) * 0.5 * top
    series = np.polynomial.chebyshev.Chebyshev.fit(grid, function(np.sqrt(grid)), degree, [0, top])
    return [float(x) for x in series.convert(kind=np.polynomial.Polynomial).coef]


COS_COEF = fit_even(np.cos, 6)
SIN_COEF = fit_even(lambda x: np.sin(x) / x, 5)
COS_TURN = [c * (2.0 * math.pi) ** (2 * k) for k, c in enumerate(COS_COEF)]
SIN_TURN = [c * (2.0 * math.pi) ** (2 * k + 1) for k, c in enumerate(SIN_COEF)]


def split_np(values):
    high = values.astype(np.float32).astype(jnp.bfloat16)
    low = (values - high.astype(np.float64)).astype(jnp.bfloat16)
    return high, low


def tables():
    v1 = np.arange(32)
    cb = np.arange(LIVE_BLOCKS)
    angle = 2.0 * np.pi * (((cb[None, :] - 12) * v1[:, None]) % 32) / 32
    cos, sin = np.cos(angle), np.sin(angle)
    first = np.concatenate(
        [np.concatenate([cos, sin], 1), np.concatenate([-sin, cos], 1)], 0
    )
    high, low = split_np(first)
    first = np.concatenate([high, high, low], 1)
    t = np.arange(128)
    angle = 2.0 * np.pi * (v1[:, None] * t[None, :]) / LENGTH
    turn_one = np.concatenate([np.cos(angle), -np.sin(angle)], 0).astype(np.float32)
    angle = 2.0 * np.pi * ((t[:, None] * t[None, :]) % 128) / 128
    cos, sin = np.cos(angle), np.sin(angle)
    second = np.concatenate([np.concatenate([cos, sin], 1), np.concatenate([-sin, cos], 1)], 0)
    second = np.concatenate(split_np(second / 64.0), 0)
    c = np.arange(96)
    angle = 2.0 * np.pi * (((c[:, None] - 48) * t[None, :]) % 128) / 128
    third = np.zeros((2, 128, 2, 128))
    third[0, :96, 0] = np.cos(angle)
    third[0, :96, 1] = -np.sin(angle)
    third[1, :96, 0] = np.sin(angle)
    third[1, :96, 1] = np.cos(angle)
    third = split_np(third.reshape(256, 256) / 64.0)
    angle = 2.0 * np.pi * (v1[:, None] * t[None, :]) / LENGTH
    turn_two = np.concatenate([np.cos(angle), -np.sin(angle)], 0).astype(np.float32)
    return first, turn_one, second, third, turn_two


def iota(shape, axis):
    return lax.broadcasted_iota(jnp.int32, shape, axis)


def dot(left, right):
    return jnp.dot(left, right, preferred_element_type=jnp.float32)


def as_mask(chosen):
    return jnp.where(chosen, 1.0, 0.0).astype(jnp.bfloat16)


def split(values):
    high = values.astype(jnp.bfloat16)
    low = (values - high.astype(jnp.float32)).astype(jnp.bfloat16)
    return high, low


def sort_kernel(ids_hbm, counts_hbm, out_ref, ids_ref, counts_ref, sem):
    ids_copy = pltpu.make_async_copy(ids_hbm, ids_ref, sem.at[0])
    ids_copy.start()
    counts_copy = pltpu.make_async_copy(counts_hbm, counts_ref, sem.at[1])
    counts_copy.start()
    base = (lax.axis_index("y") * SHARED).astype(jnp.float32)
    live = iota((96, 128), 0)
    lane = iota((128, 128), 1)
    prefix = jnp.concatenate(
        [as_mask(iota((128, 128), 0) < lane), jnp.ones((128, 128), jnp.bfloat16)], 1
    )
    ids_copy.wait()
    ids = ids_ref[...]
    block = ((ids >> 10) + 48) & 127
    part = block >> 4
    side = jnp.where(part < 3, 0, 1)
    target = (part - 3 * side) * 32 + ((block & 15) << 1) + side
    target = jnp.where(part < ROWS, target, block)
    here = [live == target[k : k + 1, :] for k in range(8)]
    sums = dot(jnp.concatenate([as_mask(mask) for mask in here], 0), prefix)
    local = ids & 1023
    high = ((local >> 5) + 1).astype(jnp.float32)
    low = (local & 31).astype(jnp.float32)
    pad = jnp.zeros((112, 128), jnp.float32)
    named = jnp.concatenate([high, low, pad], 0).T
    running = jnp.zeros((96, 128), jnp.float32) - base
    chosen = []
    for k in range(8):
        rows = slice(k * 96, (k + 1) * 96)
        rank = running + sums[rows, :128]
        running = running + sums[rows, 128:]
        chosen.append(
            jnp.concatenate([as_mask(here[k] & (rank == float(s))) for s in range(SHARED)], 0)
        )
    counts_copy.wait()
    picked = jnp.zeros((SHARED * 96, 256), jnp.float32)
    for k in range(0, 8, 2):
        rows = []
        for m in (k, k + 1):
            counts = counts_ref[m * 128 : (m + 1) * 128, :].astype(jnp.float32)
            name = jnp.where(
                lane == 0, named[:, m : m + 1], jnp.where(lane == 1, named[:, 8 + m : 9 + m], 0.0)
            )
            rows.append(jnp.concatenate([counts, name], 1).astype(jnp.bfloat16))
        picked = picked + dot(
            jnp.concatenate([chosen[k], chosen[k + 1]], 1), jnp.concatenate(rows, 0)
        )
    names = jnp.zeros((32, 128), jnp.float32)
    for i in range(3):
        for s in range(SHARED):
            rows = slice(s * 96 + i * 32, s * 96 + i * 32 + 32)
            out_ref[pl.ds(i * SHARED + s, 32, stride=10), :] = picked[rows, :128]
            name = picked[rows, 128:129] * 32.0 + picked[rows, 129:130]
            names = jnp.where(lane[:32] == i * SHARED + s, name, names)
    out_ref[pl.ds(9, 32, stride=10), :] = names


def place_kernel(traits_ref, got_ref, out_ref):
    core = lax.axis_index("core")
    traits = [traits_ref[0:1, m : m + 1] for m in range(4)]
    names = got_ref[pl.ds(9, 64, stride=10), :]
    names = jnp.concatenate([names, pltpu.roll(names, 127, 1)], 0).T
    cell = iota((384, 128), 0)
    row = iota((48, 128), 0)
    first_lane = iota((48, 128), 1) == 0
    for i in range(3):
        masks, counts = [], []
        for s, width in ((0, 128), (2, 64)):
            name = names[i * SHARED + s : i * SHARED + s + 1, :width].astype(jnp.int32)
            line = (name >> 5) - 1
            column = ((name & 31) + 12) & 31
            valid = (name > 0) & (column < LIVE_BLOCKS) & (((line >> 3) & 1) == core)
            seat = (line >> 4) * 4 + ((line >> 1) & 3)
            key = jnp.where(valid, seat * 48 + (line & 1) * 24 + column, -1)
            masks.append(as_mask(cell[:, :width] == key))
        for s in range(SHARED):
            counts.append(got_ref[pl.ds(i * SHARED + s, 64, stride=10), :].astype(jnp.bfloat16))
        grid = dot(jnp.concatenate(masks, 1), jnp.concatenate(counts, 0))
        extra = jnp.zeros((48, 128), jnp.float32)
        if i < 2:
            for m in range(2):
                extra = jnp.where(first_lane & (row == m * 24), traits[i * 2 + m], extra)
        for d in range(8):
            out_ref[d * 144 + i * 48 : d * 144 + i * 48 + 48, :] = (
                grid[d * 48 : d * 48 + 48] + extra
            )


def evaluate(square, wave, strength, weight):
    inverse = lax.rsqrt(square)
    turns = wave * (square * inverse)
    turns = turns - ((turns + ROUNDER) - ROUNDER)
    arg = turns * turns
    cosine = COS_TURN[-1] * arg + COS_TURN[-2]
    for value in COS_TURN[-3::-1]:
        cosine = cosine * arg + value
    sine = SIN_TURN[-1] * arg + SIN_TURN[-2]
    for value in SIN_TURN[-3::-1]:
        sine = sine * arg + value
    amplitude = weight * (1.0 + strength * inverse)
    return amplitude * cosine, amplitude * (turns * sine)


def fill_kernel(
    nodes_ref,
    got_ref,
    first_ref,
    turn_ref,
    second_ref,
    out_ref,
    near_ref,
    fill_ref,
    turned_ref,
):
    side = lax.axis_index("x_high")
    seat = (lax.axis_index("x_low") * 2 + lax.axis_index("core")) * 4 + lax.axis_index("y")
    base = lax.axis_index("z") * 32 + (side - 1) * HALF + seat * 2
    right = side == 1
    column = (
        iota((LIVE_BLOCKS, 128), 0) * 128 + iota((LIVE_BLOCKS, 128), 1) - HALF
    ).astype(jnp.float32)
    traits = [
        [got_ref[p * 144 + e * 24 : p * 144 + e * 24 + 1, 0:1] for e in range(4)]
        for p in range(PLANES)
    ]
    counts = []
    for b in range(ROWS):
        parts = [got_ref[m * 144 + b * 24 : m * 144 + b * 24 + 24, :] for m in range(8)]
        while len(parts) > 1:
            parts = [parts[m] + parts[m + 1] for m in range(0, len(parts), 2)]
        counts.append(jnp.where(column > -float(HALF), parts[0], 0.0))
    lane = iota((8, 128), 1)
    inner = lane < 64
    for m in range(2):
        pair = jnp.where(right, counts[m][11:13], counts[4 + m][11:13])
        merged = jnp.where(inner[0:1], pair[1:2], pair[0:1])
        for p in range(PLANES):
            near_ref[p * 2 + m : p * 2 + m + 1, :] = merged
    for p in range(PLANES):
        for e in range(4):
            at = 8 + e * 8 + p * 2
            near_ref[at : at + 2, :] = jnp.broadcast_to(traits[p][e], (2, 128))
    near_counts = near_ref[0:8, :]
    near_row = (base + jnp.where(right, 0, 1024) + (iota((8, 128), 0) & 1)).astype(jnp.float32)
    near_row = near_row + near_ref[24:32, :]
    near_col = jnp.where(inner, lane, lane - 128).astype(jnp.float32) + near_ref[32:40, :]
    near_wave = near_ref[8:16, :] * (0.5 / math.pi)
    near_strength = near_ref[16:24, :]
    node_row = [nodes_ref[0:1, 16 + q : 17 + q] for q in range(NODES)]
    node_col = [nodes_ref[0:1, 32 + q : 33 + q] for q in range(NODES)]
    node_weight = [nodes_ref[0:1, 48 + q : 49 + q] for q in range(NODES)]
    weights = [
        [jnp.where(counts[b] > float(q), node_weight[q], 0.0) for q in range(FAR)]
        for b in range(ROWS)
    ]
    extra_real = jnp.zeros((8, 128), jnp.float32)
    extra_imag = jnp.zeros((8, 128), jnp.float32)
    for q in range(FAR, NODES):
        row_pos = near_row + node_row[q]
        col_pos = near_col + node_col[q]
        square = row_pos * row_pos + col_pos * col_pos + HEIGHT_SQ
        weight = jnp.where(near_counts > float(q), node_weight[q], 0.0)
        real, imag = evaluate(square, near_wave, near_strength, weight)
        extra_real = extra_real + real
        extra_imag = extra_imag + imag
    inner_pair = (iota((2, 128), 0) == 1) == inner[0:2]
    turn_real = turn_ref[0:32, :]
    turn_imag = turn_ref[32:64, :]
    for p in range(PLANES):
        wave, strength = traits[p][0] * (0.5 / math.pi), traits[p][1]
        shift_row, shift_col = traits[p][2], traits[p][3]
        col_base = column + shift_col
        col_sq = []
        for q in range(FAR):
            col_pos = col_base + node_col[q]
            col_sq.append(col_pos * col_pos)
        for b in range(ROWS):
            row_offset = (base + (512 * (b // 2) + b % 2)).astype(jnp.float32)
            total_real = jnp.zeros((LIVE_BLOCKS, 128), jnp.float32)
            total_imag = jnp.zeros((LIVE_BLOCKS, 128), jnp.float32)
            for q in range(FAR):
                row_pos = (row_offset + shift_row) + node_row[q]
                square = col_sq[q] + (row_pos * row_pos + HEIGHT_SQ)
                real, imag = evaluate(square, wave, strength, weights[b][q])
                total_real = total_real + real
                total_imag = total_imag + imag
            lanes = slice((p * ROWS + b) * 128, (p * ROWS + b) * 128 + 128)
            fill_ref[0:24, lanes] = total_real
            fill_ref[24:48, lanes] = -total_imag
            if b // 2 != 1:
                use = right if b // 2 == 0 else jnp.logical_not(right)
                use = use & inner_pair
                m = p * 2 + b % 2
                fill_ref[11:13, lanes] = fill_ref[11:13, lanes] + jnp.where(
                    use, extra_real[m : m + 1], 0.0
                )
                fill_ref[35:37, lanes] = fill_ref[35:37, lanes] - jnp.where(
                    use, extra_imag[m : m + 1], 0.0
                )
        lanes = slice(p * ROWS * 128, (p + 1) * ROWS * 128)
        high, low = split(fill_ref[:, lanes])
        stage = dot(first_ref[...], jnp.concatenate([high, low, high], 0))
        for b in range(ROWS):
            real = stage[0:32, b * 128 : (b + 1) * 128]
            imag = stage[32:64, b * 128 : (b + 1) * 128]
            next_real = real * turn_real - imag * turn_imag
            next_imag = real * turn_imag + imag * turn_real
            for j in range(4):
                rows = slice(j * 8, j * 8 + 8)
                at = (((b // 2) * 4 + j) * 2 + b % 2) * 32 + p * 8
                turned_ref[at : at + 8, 0:128] = next_real[rows]
                turned_ref[at : at + 8, 128:256] = next_imag[rows]
    contract = (((1,), (1,)), ((), ()))
    left = iota((128, 128), 1) < 64
    for i in range(3):
        high, low = split(turned_ref[i * 256 : (i + 1) * 256, :])
        both = lax.dot_general(second_ref[...], high, contract, preferred_element_type=jnp.float32)
        rest = lax.dot_general(
            second_ref[0:256, :], low, contract, preferred_element_type=jnp.float32
        )
        product = (both[0:256] + both[256:512]) + rest
        for m in range(2):
            real = product[0:128, m * 128 : (m + 1) * 128]
            imag = product[128:256, m * 128 : (m + 1) * 128]
            even = jnp.where(left, real, pltpu.roll(imag, 64, 1))
            odd = jnp.where(left, pltpu.roll(real, 64, 1), imag)
            out_ref[pl.ds(m * 6 + i, 128, stride=12), :] = even
            out_ref[pl.ds(m * 6 + 3 + i, 128, stride=12), :] = odd


def fft_list(values):
    size = len(values)
    if size == 1:
        return values
    even = fft_list(values[0::2])
    odd = fft_list(values[1::2])
    top, bottom = [], []
    for k in range(size // 2):
        real, imag = odd[k]
        if k == 0:
            pass
        elif 4 * k == size:
            real, imag = imag, -real
        elif 8 * k == size:
            half = math.sqrt(0.5)
            real, imag = (real + imag) * half, (imag - real) * half
        elif 8 * k == 3 * size:
            half = math.sqrt(0.5)
            real, imag = (imag - real) * half, -(real + imag) * half
        else:
            cos = math.cos(2.0 * math.pi * k / size)
            sin = math.sin(2.0 * math.pi * k / size)
            real, imag = real * cos + imag * sin, imag * cos - real * sin
        top.append((even[k][0] + real, even[k][1] + imag))
        bottom.append((even[k][0] - real, even[k][1] - imag))
    return top + bottom


def column_kernel(
    got_ref,
    high_ref,
    low_ref,
    turn_ref,
    real_hbm,
    imag_hbm,
    gathered_ref,
    real_ref,
    imag_ref,
    sem,
):
    blank = jnp.zeros((32, 128), jnp.float32)
    for pair in range(16):
        parts = []
        for side in range(2):
            for k in range(3):
                parts.append(got_ref[pl.ds((side * 16 + pair) * 3 + k, 16, stride=96), :])
        flipped = jnp.concatenate(parts + [blank], 0).T
        for m in range(2):
            for ri in range(2):
                for p in range(PLANES):
                    at = (p * 32 + pair * 2 + m) * 8
                    gathered_ref[at : at + 8, ri * 128 : (ri + 1) * 128] = flipped[
                        ((ri * 2 + m) * 4 + p) * 8 : ((ri * 2 + m) * 4 + p) * 8 + 8
                    ]
    high, low = split(gathered_ref[...])
    stage = dot(high, high_ref[...]) + dot(low, high_ref[...]) + dot(high, low_ref[...])
    copies = []
    for p in range(PLANES):
        values = []
        for r in range(32):
            at = (p * 32 + r) * 8
            real = stage[at : at + 8, 0:128]
            imag = stage[at : at + 8, 128:256]
            if r:
                turn_real = turn_ref[r : r + 1, :]
                turn_imag = turn_ref[32 + r : 33 + r, :]
                real, imag = (
                    real * turn_real - imag * turn_imag,
                    real * turn_imag + imag * turn_real,
                )
            values.append((real, imag))
        for u, (real, imag) in enumerate(fft_list(values)):
            real_ref[p, :, u * 128 : (u + 1) * 128] = real
            imag_ref[p, :, u * 128 : (u + 1) * 128] = imag
        for m, (source, target) in enumerate(((real_ref, real_hbm), (imag_ref, imag_hbm))):
            copy = pltpu.make_async_copy(source.at[p], target.at[p], sem.at[p * 2 + m])
            copy.start()
            copies.append(copy)
    for copy in copies:
        copy.wait()


VMEM = pl.BlockSpec(memory_space=pltpu.VMEM)
SMEM = pl.BlockSpec(memory_space=pltpu.SMEM)
HBM = pl.BlockSpec(memory_space=pltpu.HBM)
PARAMS = pltpu.CompilerParams(vmem_limit_bytes=40 * 1024 * 1024)


def exchange(values, axes):
    return lax.all_to_all(values, axes, split_axis=0, concat_axis=0, tiled=True)


def shards(
    piece_ids, point_counts, wavenumber, strength, displacement, node_position, node_weights
):
    first, turn_one, second, third, turn_two = tables()
    nodes = jnp.concatenate(
        [
            wavenumber,
            strength,
            displacement[0],
            displacement[1],
            jnp.zeros((12,), jnp.float32),
            node_position[0],
            jnp.zeros((1,), jnp.float32),
            node_position[1],
            jnp.zeros((1,), jnp.float32),
            node_weights,
            jnp.zeros((65,), jnp.float32),
        ]
    ).reshape(1, 128)
    sent = pl.pallas_call(
        sort_kernel,
        out_shape=jax.ShapeDtypeStruct((320, 128), jnp.float32),
        in_specs=[HBM, HBM],
        out_specs=VMEM,
        scratch_shapes=[
            pltpu.VMEM((8, 128), jnp.int32),
            pltpu.VMEM((1024, 128), jnp.int32),
            pltpu.SemaphoreType.DMA((2,)),
        ],
        compiler_params=pltpu.CompilerParams(vmem_limit_bytes=62 * 1024 * 1024),
    )(piece_ids.reshape(8, 128), point_counts)
    got = exchange(sent.reshape(320, 1, 128), ("z", "x_high")).reshape(320, 128)
    got = lax.all_gather(got, "core", axis=0, tiled=True)
    grid = pl.pallas_call(
        place_kernel,
        out_shape=jax.ShapeDtypeStruct((1152, 128), jnp.float32),
        in_specs=[VMEM, VMEM],
        out_specs=VMEM,
        compiler_params=PARAMS,
    )(nodes, got)
    grid = exchange(grid.reshape(1152, 1, 128), ("x_low", "y")).reshape(1152, 128)
    sent = pl.pallas_call(
        fill_kernel,
        out_shape=jax.ShapeDtypeStruct((1536, 128), jnp.float32),
        in_specs=[VMEM] * 5,
        out_specs=VMEM,
        scratch_shapes=[
            pltpu.VMEM((40, 128), jnp.float32),
            pltpu.VMEM((48, PLANES * ROWS * 128), jnp.float32),
            pltpu.VMEM((768, 256), jnp.float32),
        ],
        compiler_params=PARAMS,
    )(nodes, grid, first, turn_one, second)
    got = exchange(
        sent.reshape(1536, 1, 128), ("z", "x_high", "x_low", "core", "y")
    ).reshape(1536, 128)
    shape = jax.ShapeDtypeStruct((PLANES, 8, LENGTH), jnp.float32)
    return pl.pallas_call(
        column_kernel,
        out_shape=(shape, shape),
        in_specs=[VMEM] * 4,
        out_specs=(HBM, HBM),
        scratch_shapes=[
            pltpu.VMEM((1024, 256), jnp.float32),
            pltpu.VMEM((PLANES, 8, LENGTH), jnp.float32),
            pltpu.VMEM((PLANES, 8, LENGTH), jnp.float32),
            pltpu.SemaphoreType.DMA((2 * PLANES,)),
        ],
        compiler_params=PARAMS,
    )(got, third[0], third[1], turn_two)


def solution(mesh):
    every = ("z", "x_high", "x_low", "core", "y")
    fine = Mesh(mesh.devices.reshape(16, 2, 2, 2, 4), every)
    wide = every[:4]
    placed = (P(wide), P(wide, None), P("y"), P("y"), P(None, "y"), P(), P())
    return jax.shard_map(
        shards,
        mesh=fine,
        in_specs=placed,
        out_specs=(P(None, every, None), P(None, every, None)),
        check_vma=False,
    )
```

```python
import functools
import math

import jax
import jax.numpy as jnp
import numpy as np
from jax import lax
from jax.experimental import pallas as pl
from jax.experimental.pallas import tpu as pltpu
from jax.sharding import Mesh, PartitionSpec as P

LENGTH = 4096
NODES = 15
FAR = 3
HEIGHT_SQ = 0.0625
RANKS = 12
LIVE_BLOCKS = 24
HALF = 1536
ROWS = 6
PLANES = 4

ROUNDER = 12582912.0


def fit_even(function, degree):
    top = math.pi**2
    grid = (np.cos(np.pi * (np.arange(400) + 0.5) / 400) + 1.0) * 0.5 * top
    series = np.polynomial.chebyshev.Chebyshev.fit(grid, function(np.sqrt(grid)), degree, [0, top])
    return [float(x) for x in series.convert(kind=np.polynomial.Polynomial).coef]


COS_COEF = fit_even(np.cos, 6)
SIN_COEF = fit_even(lambda x: np.sin(x) / x, 5)
COS_TURN = [c * (2.0 * math.pi) ** (2 * k) for k, c in enumerate(COS_COEF)]
SIN_TURN = [c * (2.0 * math.pi) ** (2 * k + 1) for k, c in enumerate(SIN_COEF)]


def split_np(values):
    high = values.astype(np.float32).astype(jnp.bfloat16)
    low = (values - high.astype(np.float64)).astype(jnp.bfloat16)
    return high, low


def tables():
    v1 = np.arange(32)
    cb = np.arange(LIVE_BLOCKS)
    angle = 2.0 * np.pi * (((cb[None, :] - 12) * v1[:, None]) % 32) / 32
    cos, sin = np.cos(angle), np.sin(angle)
    first = np.concatenate(
        [np.concatenate([cos, sin], 1), np.concatenate([-sin, cos], 1)], 0
    )
    high, low = split_np(first)
    first = np.concatenate([high, high, low], 1)
    t = np.arange(128)
    angle = 2.0 * np.pi * (v1[:, None] * t[None, :]) / LENGTH
    turn_one = np.concatenate([np.cos(angle), -np.sin(angle)], 0).astype(np.float32)
    angle = 2.0 * np.pi * ((t[:, None] * t[None, :]) % 128) / 128
    cos, sin = np.cos(angle), np.sin(angle)
    second = np.concatenate([np.concatenate([cos, sin], 1), np.concatenate([-sin, cos], 1)], 0)
    second = np.concatenate(split_np(second / 64.0), 0)
    j, z = np.arange(4)[:, None], np.arange(16)[None, :]
    whole = ((z & 1) * 32 + (z >> 1) * 4 + j).reshape(64)
    c = np.concatenate([whole, (64 + z[:, :8] * 4 + j).reshape(32)])
    angle = 2.0 * np.pi * (((c[:, None] - 48) * t[None, :]) % 128) / 128
    third = np.zeros((2, 128, 2, 128))
    third[0, :96, 0] = np.cos(angle)
    third[0, :96, 1] = -np.sin(angle)
    third[1, :96, 0] = np.sin(angle)
    third[1, :96, 1] = np.cos(angle)
    third = split_np(third.reshape(256, 256) / 64.0)
    angle = 2.0 * np.pi * (v1[:, None] * t[None, :]) / LENGTH
    turn_two = np.concatenate([np.cos(angle), -np.sin(angle)], 0).astype(np.float32)
    return first, turn_one, second, third, turn_two


def iota(shape, axis):
    return lax.broadcasted_iota(jnp.int32, shape, axis)


def dot(left, right):
    return jnp.dot(left, right, preferred_element_type=jnp.float32)


def as_mask(chosen):
    return jnp.where(chosen, 1.0, 0.0).astype(jnp.bfloat16)


def split(values):
    high = values.astype(jnp.bfloat16)
    low = (values - high.astype(jnp.float32)).astype(jnp.bfloat16)
    return high, low


def sort_kernel(ids_hbm, counts_hbm, out_ref, mark_ref, ids_ref, counts_ref, sem):
    ids_copy = pltpu.make_async_copy(ids_hbm, ids_ref, sem.at[0])
    ids_copy.start()
    counts_copy = pltpu.make_async_copy(counts_hbm, counts_ref, sem.at[1])
    counts_copy.start()
    mark_ref[...] = jnp.zeros((8, 128), jnp.float32)
    group = lax.axis_index("y")
    seat = iota((32, 128), 0)
    lane = iota((128, 128), 1)
    prefix = jnp.concatenate(
        [as_mask(iota((128, 128), 0) < lane), jnp.ones((128, 128), jnp.bfloat16)], 1
    )
    ids_copy.wait()
    ids = ids_ref[...]
    local = ids & 1023
    block = ((ids >> 10) + 48) & 127
    role = block >> 5
    low_bit = jnp.where(role == 2, local >> 9, role)
    target = ((block >> 2) & 7) * 2 + low_bit + jnp.where(role == 2, 16, 0)
    target = jnp.where(((block & 3) == group) & (role < 3), target, -1)
    here = [seat == target[k : k + 1, :] for k in range(8)]
    sums = dot(jnp.concatenate([as_mask(mask) for mask in here], 0), prefix)
    high = ((local >> 5) + 1).astype(jnp.float32)
    low = (local & 31).astype(jnp.float32)
    pad = jnp.zeros((112, 128), jnp.float32)
    named = jnp.concatenate([high, low, pad], 0).T
    running = jnp.zeros((32, 128), jnp.float32)
    chosen = []
    for k in range(8):
        rows = slice(k * 32, (k + 1) * 32)
        rank = running + sums[rows, :128]
        running = running + sums[rows, 128:]
        chosen.append(
            jnp.concatenate([as_mask(here[k] & (rank == float(s))) for s in range(RANKS)], 0)
        )
    counts_copy.wait()
    picked = jnp.zeros((RANKS * 32, 256), jnp.float32)
    for k in range(0, 8, 2):
        rows = []
        for m in (k, k + 1):
            counts = counts_ref[m * 128 : (m + 1) * 128, :].astype(jnp.float32)
            name = jnp.where(
                lane == 0, named[:, m : m + 1], jnp.where(lane == 1, named[:, 8 + m : 9 + m], 0.0)
            )
            rows.append(jnp.concatenate([counts, name], 1).astype(jnp.bfloat16))
        picked = picked + dot(
            jnp.concatenate([chosen[k], chosen[k + 1]], 1), jnp.concatenate(rows, 0)
        )
    names = jnp.zeros((16, 128), jnp.float32)
    for kind in range(2):
        for s in range(RANKS):
            rows = slice(s * 32 + kind * 16, s * 32 + kind * 16 + 16)
            out_ref[pl.ds(kind * RANKS + s, 16, stride=25), :] = picked[rows, :128]
            name = picked[rows, 128:129] * 32.0 + picked[rows, 129:130]
            names = jnp.where(lane[:16] == kind * RANKS + s, name, names)
    out_ref[pl.ds(24, 16, stride=25), :] = names


def place_kernel(nodes_ref, got_ref, out_ref):
    names = got_ref[pl.ds(24, 16, stride=25), :]
    names = [names] + [pltpu.roll(names, 128 - s, 1) for s in range(1, 8)]
    names = jnp.concatenate(names, 0).T
    for kind, cells, start, stop in ((0, 768, 0, 96), (1, 384, 96, 144)):
        cell = iota((cells, 128), 0)
        masks, counts = [], []
        for s, width in ((0, 128), (8, 64)):
            at = kind * RANKS + s
            name = names[at : at + 1, :width].astype(jnp.int32)
            column = ((name & 31) + 12) & 31
            line = ((name >> 5) - 1) & (31 if kind == 0 else 15)
            key = jnp.where(
                (name > 0) & (column < LIVE_BLOCKS), line * LIVE_BLOCKS + column, -1
            )
            masks.append(as_mask(cell[:, :width] == key))
        for s in range(RANKS):
            rows = got_ref[pl.ds(kind * RANKS + s, 16, stride=25), :]
            counts.append(rows.astype(jnp.bfloat16))
        grid = dot(jnp.concatenate(masks, 1), jnp.concatenate(counts, 0))
        size = stop - start
        for d in range(8):
            out_ref[d * 144 + start : d * 144 + stop, :] = grid[d * size : (d + 1) * size]


def evaluate(square, wave, strength, weight):
    inverse = lax.rsqrt(square)
    turns = wave * (square * inverse)
    turns = turns - ((turns + ROUNDER) - ROUNDER)
    arg = turns * turns
    cosine = COS_TURN[-1] * arg + COS_TURN[-2]
    for value in COS_TURN[-3::-1]:
        cosine = cosine * arg + value
    sine = SIN_TURN[-1] * arg + SIN_TURN[-2]
    for value in SIN_TURN[-3::-1]:
        sine = sine * arg + value
    amplitude = weight * (1.0 + strength * inverse)
    return amplitude * cosine, amplitude * (turns * sine)


def fill_kernel(
    nodes_ref,
    got_ref,
    first_ref,
    turn_ref,
    second_ref,
    out_ref,
    near_ref,
    fill_ref,
    turned_ref,
):
    z, group = lax.axis_index("z"), lax.axis_index("y")
    seat = lax.axis_index("x") * 2 + lax.axis_index("core")
    cluster = (z >> 1) * 4 + group
    base = ((z & 1) * 32 + cluster) * 32 + seat * 4 - HALF
    base_split = (64 + cluster) * 32 + (z & 1) * 16 + seat * 2 - HALF
    column = (
        iota((LIVE_BLOCKS, 128), 0) * 128 + iota((LIVE_BLOCKS, 128), 1) - HALF
    ).astype(jnp.float32)
    traits = [[nodes_ref[p : p + 1, e : e + 1] for e in range(4)] for p in range(PLANES)]
    counts = []
    for b in range(ROWS):
        parts = [got_ref[m * 144 + b * 24 : m * 144 + b * 24 + 24, :] for m in range(8)]
        while len(parts) > 1:
            parts = [parts[m] + parts[m + 1] for m in range(0, len(parts), 2)]
        counts.append(parts[0])
    lane = iota((16, 128), 1)
    inner = lane < 64
    for m in range(4):
        pair = counts[m][11:13]
        merged = jnp.where(inner[0:1], pair[1:2], pair[0:1])
        for p in range(PLANES):
            near_ref[p * 4 + m : p * 4 + m + 1, :] = merged
    for p in range(PLANES):
        for e in range(4):
            at = 16 + e * 16 + p * 4
            near_ref[at : at + 4, :] = jnp.broadcast_to(traits[p][e], (4, 128))
    near_counts = near_ref[0:16, :]
    near_row = (base + (iota((16, 128), 0) & 3)).astype(jnp.float32) + near_ref[48:64, :]
    near_col = jnp.where(inner, lane, lane - 128).astype(jnp.float32) + near_ref[64:80, :]
    near_wave = near_ref[16:32, :] * (0.5 / math.pi)
    near_strength = near_ref[32:48, :]
    node_row = [nodes_ref[0:1, 16 + q : 17 + q] for q in range(NODES)]
    node_col = [nodes_ref[0:1, 32 + q : 33 + q] for q in range(NODES)]
    node_weight = [nodes_ref[0:1, 48 + q : 49 + q] for q in range(NODES)]
    weights = [
        [jnp.where(counts[b] > float(q), node_weight[q], 0.0) for q in range(FAR)]
        for b in range(ROWS)
    ]
    extra_real = jnp.zeros((16, 128), jnp.float32)
    extra_imag = jnp.zeros((16, 128), jnp.float32)
    for q in range(FAR, NODES):
        row_pos = near_row + node_row[q]
        col_pos = near_col + node_col[q]
        square = row_pos * row_pos + col_pos * col_pos + HEIGHT_SQ
        weight = jnp.where(near_counts > float(q), node_weight[q], 0.0)
        real, imag = evaluate(square, near_wave, near_strength, weight)
        extra_real = extra_real + real
        extra_imag = extra_imag + imag
    inner_pair = (iota((2, 128), 0) == 1) == inner[0:2]
    turn_real = turn_ref[0:32, :]
    turn_imag = turn_ref[32:64, :]
    for p in range(PLANES):
        wave, strength = traits[p][0] * (0.5 / math.pi), traits[p][1]
        shift_row, shift_col = traits[p][2], traits[p][3]
        col_base = column + shift_col
        col_sq = []
        for q in range(FAR):
            col_pos = col_base + node_col[q]
            col_sq.append(col_pos * col_pos)
        for b in range(ROWS):
            row_offset = (base + b if b < 4 else base_split + (b - 4)).astype(jnp.float32)
            total_real = jnp.zeros((LIVE_BLOCKS, 128), jnp.float32)
            total_imag = jnp.zeros((LIVE_BLOCKS, 128), jnp.float32)
            for q in range(FAR):
                row_pos = (row_offset + shift_row) + node_row[q]
                square = col_sq[q] + (row_pos * row_pos + HEIGHT_SQ)
                real, imag = evaluate(square, wave, strength, weights[b][q])
                total_real = total_real + real
                total_imag = total_imag + imag
            lanes = slice((p * ROWS + b) * 128, (p * ROWS + b) * 128 + 128)
            fill_ref[0:24, lanes] = total_real
            fill_ref[24:48, lanes] = -total_imag
            if b < 4:
                m = p * 4 + b
                fill_ref[11:13, lanes] = fill_ref[11:13, lanes] + jnp.where(
                    inner_pair, extra_real[m : m + 1], 0.0
                )
                fill_ref[35:37, lanes] = fill_ref[35:37, lanes] - jnp.where(
                    inner_pair, extra_imag[m : m + 1], 0.0
                )
        lanes = slice(p * ROWS * 128, (p + 1) * ROWS * 128)
        high, low = split(fill_ref[:, lanes])
        stage = dot(first_ref[...], jnp.concatenate([high, low, high], 0))
        for b in range(ROWS):
            real = stage[0:32, b * 128 : (b + 1) * 128]
            imag = stage[32:64, b * 128 : (b + 1) * 128]
            next_real = real * turn_real - imag * turn_imag
            next_imag = real * turn_imag + imag * turn_real
            for j in range(4):
                rows = slice(j * 8, j * 8 + 8)
                at = (((b // 2) * 4 + j) * 2 + b % 2) * 32 + p * 8
                turned_ref[at : at + 8, 0:128] = next_real[rows]
                turned_ref[at : at + 8, 128:256] = next_imag[rows]
    contract = (((1,), (1,)), ((), ()))
    left = iota((128, 128), 1) < 64
    for i in range(3):
        high, low = split(turned_ref[i * 256 : (i + 1) * 256, :])
        both = lax.dot_general(second_ref[...], high, contract, preferred_element_type=jnp.float32)
        rest = lax.dot_general(
            second_ref[0:256, :], low, contract, preferred_element_type=jnp.float32
        )
        product = (both[0:256] + both[256:512]) + rest
        for m in range(2):
            real = product[0:128, m * 128 : (m + 1) * 128]
            imag = product[128:256, m * 128 : (m + 1) * 128]
            even = jnp.where(left, real, pltpu.roll(imag, 64, 1))
            odd = jnp.where(left, pltpu.roll(real, 64, 1), imag)
            out_ref[pl.ds(m * 6 + i, 128, stride=12), :] = even
            out_ref[pl.ds(m * 6 + 3 + i, 128, stride=12), :] = odd


def fft_list(values):
    size = len(values)
    if size == 1:
        return values
    even = fft_list(values[0::2])
    odd = fft_list(values[1::2])
    top, bottom = [], []
    for k in range(size // 2):
        real, imag = odd[k]
        if k == 0:
            pass
        elif 4 * k == size:
            real, imag = imag, -real
        elif 8 * k == size:
            half = math.sqrt(0.5)
            real, imag = (real + imag) * half, (imag - real) * half
        elif 8 * k == 3 * size:
            half = math.sqrt(0.5)
            real, imag = (imag - real) * half, -(real + imag) * half
        else:
            cos = math.cos(2.0 * math.pi * k / size)
            sin = math.sin(2.0 * math.pi * k / size)
            real, imag = real * cos + imag * sin, imag * cos - real * sin
        top.append((even[k][0] + real, even[k][1] + imag))
        bottom.append((even[k][0] - real, even[k][1] - imag))
    return top + bottom


def column_kernel(
    got_ref,
    high_ref,
    low_ref,
    turn_ref,
    real_hbm,
    imag_hbm,
    gathered_ref,
    real_ref,
    imag_ref,
    sem,
):
    blank = jnp.zeros((32, 128), jnp.float32)
    for pair in range(16):
        parts = []
        for j in range(4):
            at = ((pair >> 1) * 4 + j) * 3 + (pair & 1)
            parts.append(got_ref[pl.ds(at, 16, stride=96), :])
        for j in range(4):
            at = ((pair >> 3) * 32 + (pair & 7) * 4 + j) * 3 + 2
            parts.append(got_ref[pl.ds(at, 8, stride=192), :])
        flipped = jnp.concatenate(parts + [blank], 0).T
        for m in range(2):
            for ri in range(2):
                for p in range(PLANES):
                    at = (p * 32 + pair * 2 + m) * 8
                    gathered_ref[at : at + 8, ri * 128 : (ri + 1) * 128] = flipped[
                        ((ri * 2 + m) * 4 + p) * 8 : ((ri * 2 + m) * 4 + p) * 8 + 8
                    ]
    high, low = split(gathered_ref[...])
    stage = dot(high, high_ref[...]) + dot(low, high_ref[...]) + dot(high, low_ref[...])
    copies = []
    for p in range(PLANES):
        values = []
        for r in range(32):
            at = (p * 32 + r) * 8
            real = stage[at : at + 8, 0:128]
            imag = stage[at : at + 8, 128:256]
            if r:
                turn_real = turn_ref[r : r + 1, :]
                turn_imag = turn_ref[32 + r : 33 + r, :]
                real, imag = (
                    real * turn_real - imag * turn_imag,
                    real * turn_imag + imag * turn_real,
                )
            values.append((real, imag))
        for u, (real, imag) in enumerate(fft_list(values)):
            real_ref[p, :, u * 128 : (u + 1) * 128] = real
            imag_ref[p, :, u * 128 : (u + 1) * 128] = imag
        for m, (source, target) in enumerate(((real_ref, real_hbm), (imag_ref, imag_hbm))):
            copy = pltpu.make_async_copy(source.at[p], target.at[p], sem.at[p * 2 + m])
            copy.start()
            copies.append(copy)
    for copy in copies:
        copy.wait()


VMEM = pl.BlockSpec(memory_space=pltpu.VMEM)
SMEM = pl.BlockSpec(memory_space=pltpu.SMEM)
HBM = pl.BlockSpec(memory_space=pltpu.HBM)
PARAMS = pltpu.CompilerParams(vmem_limit_bytes=40 * 1024 * 1024)


def exchange(values, axes):
    return lax.all_to_all(values, axes, split_axis=0, concat_axis=0, tiled=True)


def shards(
    piece_ids, point_counts, wavenumber, strength, displacement, node_position, node_weights
):
    first, turn_one, second, third, turn_two = tables()
    sent, mark = pl.pallas_call(
        sort_kernel,
        out_shape=(
            jax.ShapeDtypeStruct((400, 128), jnp.float32),
            jax.ShapeDtypeStruct((8, 128), jnp.float32),
        ),
        in_specs=[HBM, HBM],
        out_specs=(VMEM, VMEM),
        scratch_shapes=[
            pltpu.VMEM((8, 128), jnp.int32),
            pltpu.VMEM((1024, 128), jnp.int32),
            pltpu.SemaphoreType.DMA((2,)),
        ],
        compiler_params=pltpu.CompilerParams(vmem_limit_bytes=62 * 1024 * 1024),
    )(piece_ids.reshape(8, 128), point_counts)
    got = exchange(sent.reshape(400, 1, 128), "z").reshape(400, 128)
    nodes = jnp.concatenate(
        [
            wavenumber,
            strength,
            displacement[0],
            displacement[1],
            jnp.zeros((12,), jnp.float32),
            node_position[0],
            jnp.zeros((1,), jnp.float32),
            node_position[1],
            jnp.zeros((1,), jnp.float32),
            node_weights,
            jnp.zeros((65,), jnp.float32),
        ]
    ).reshape(1, 128) + mark[0:1]
    nodes = lax.all_gather(nodes, "y", axis=0, tiled=True)
    grid = pl.pallas_call(
        place_kernel,
        out_shape=jax.ShapeDtypeStruct((1152, 128), jnp.float32),
        in_specs=[VMEM, VMEM],
        out_specs=VMEM,
        compiler_params=PARAMS,
    )(nodes, got)
    grid = exchange(grid.reshape(1152, 1, 128), ("x", "core")).reshape(1152, 128)
    sent = pl.pallas_call(
        fill_kernel,
        out_shape=jax.ShapeDtypeStruct((1536, 128), jnp.float32),
        in_specs=[VMEM] * 5,
        out_specs=VMEM,
        scratch_shapes=[
            pltpu.VMEM((80, 128), jnp.float32),
            pltpu.VMEM((48, PLANES * ROWS * 128), jnp.float32),
            pltpu.VMEM((768, 256), jnp.float32),
        ],
        compiler_params=PARAMS,
    )(nodes, grid, first, turn_one, second)
    got = exchange(
        sent.reshape(1536, 1, 128), ("z", "x", "core", "y")
    ).reshape(1536, 128)
    shape = jax.ShapeDtypeStruct((PLANES, 8, LENGTH), jnp.float32)
    return pl.pallas_call(
        column_kernel,
        out_shape=(shape, shape),
        in_specs=[VMEM] * 4,
        out_specs=(HBM, HBM),
        scratch_shapes=[
            pltpu.VMEM((1024, 256), jnp.float32),
            pltpu.VMEM((PLANES, 8, LENGTH), jnp.float32),
            pltpu.VMEM((PLANES, 8, LENGTH), jnp.float32),
            pltpu.SemaphoreType.DMA((2 * PLANES,)),
        ],
        compiler_params=PARAMS,
    )(got, third[0], third[1], turn_two)


def solution(mesh):
    every = ("z", "x", "core", "y")
    fine = Mesh(mesh.devices.reshape(16, 4, 2, 4), every)
    wide = every[:3]
    placed = (P(wide), P(wide, None), P("y"), P("y"), P(None, "y"), P(), P())
    return jax.shard_map(
        shards,
        mesh=fine,
        in_specs=placed,
        out_specs=(P(None, every, None), P(None, every, None)),
        check_vma=False,
    )
```

```python
import functools
import math

import jax
import jax.numpy as jnp
import numpy as np
from jax import lax
from jax.experimental import pallas as pl
from jax.experimental.pallas import tpu as pltpu
from jax.sharding import Mesh, PartitionSpec as P

LENGTH = 4096
NODES = 15
FAR = 3
HEIGHT_SQ = 0.0625
RANKS = 12
LIVE_BLOCKS = 24
HALF = 1536
ROWS = 6
PLANES = 4

ROUNDER = 12582912.0


def fit_even(function, degree):
    top = math.pi**2
    grid = (np.cos(np.pi * (np.arange(400) + 0.5) / 400) + 1.0) * 0.5 * top
    series = np.polynomial.chebyshev.Chebyshev.fit(grid, function(np.sqrt(grid)), degree, [0, top])
    return [float(x) for x in series.convert(kind=np.polynomial.Polynomial).coef]


COS_COEF = fit_even(np.cos, 6)
SIN_COEF = fit_even(lambda x: np.sin(x) / x, 5)
COS_TURN = [c * (2.0 * math.pi) ** (2 * k) for k, c in enumerate(COS_COEF)]
SIN_TURN = [c * (2.0 * math.pi) ** (2 * k + 1) for k, c in enumerate(SIN_COEF)]


def split_np(values):
    high = values.astype(np.float32).astype(jnp.bfloat16)
    low = (values - high.astype(np.float64)).astype(jnp.bfloat16)
    return high, low


def tables():
    v1 = np.arange(32)
    cb = np.arange(LIVE_BLOCKS)
    angle = 2.0 * np.pi * (((cb[None, :] - 12) * v1[:, None]) % 32) / 32
    cos, sin = np.cos(angle), np.sin(angle)
    first = np.concatenate(
        [np.concatenate([cos, sin], 1), np.concatenate([-sin, cos], 1)], 0
    )
    high, low = split_np(first)
    first = np.concatenate([high, high, low], 1)
    t = np.arange(128)
    angle = 2.0 * np.pi * (v1[:, None] * t[None, :]) / LENGTH
    turn_one = np.concatenate([np.cos(angle), -np.sin(angle)], 0).astype(np.float32)
    angle = 2.0 * np.pi * ((t[:, None] * t[None, :]) % 128) / 128
    cos, sin = np.cos(angle), np.sin(angle)
    second = np.concatenate([np.concatenate([cos, sin], 1), np.concatenate([-sin, cos], 1)], 0)
    second = np.concatenate(split_np(second / 64.0), 0)
    j, z = np.arange(4)[:, None], np.arange(16)[None, :]
    whole = ((z & 1) * 32 + (z >> 1) * 4 + j).reshape(64)
    c = np.concatenate([whole, (64 + z[:, :8] * 4 + j).reshape(32)])
    angle = 2.0 * np.pi * (((c[:, None] - 48) * t[None, :]) % 128) / 128
    third = np.zeros((2, 128, 2, 128))
    third[0, :96, 0] = np.cos(angle)
    third[0, :96, 1] = -np.sin(angle)
    third[1, :96, 0] = np.sin(angle)
    third[1, :96, 1] = np.cos(angle)
    third = split_np(third.reshape(256, 256) / 64.0)
    angle = 2.0 * np.pi * (v1[:, None] * t[None, :]) / LENGTH
    turn_two = np.concatenate([np.cos(angle), -np.sin(angle)], 0).astype(np.float32)
    return first, turn_one, second, third, turn_two


def iota(shape, axis):
    return lax.broadcasted_iota(jnp.int32, shape, axis)


def dot(left, right):
    return jnp.dot(left, right, preferred_element_type=jnp.float32)


def as_mask(chosen):
    return jnp.where(chosen, 1.0, 0.0).astype(jnp.bfloat16)


def split(values):
    high = values.astype(jnp.bfloat16)
    low = (values - high.astype(jnp.float32)).astype(jnp.bfloat16)
    return high, low


def sort_kernel(ids_hbm, counts_hbm, out_ref, mark_ref, ids_ref, counts_ref, sem):
    ids_copy = pltpu.make_async_copy(ids_hbm, ids_ref, sem.at[0])
    ids_copy.start()
    counts_copy = pltpu.make_async_copy(counts_hbm, counts_ref, sem.at[1])
    counts_copy.start()
    mark_ref[...] = jnp.zeros((8, 128), jnp.float32)
    group = lax.axis_index("y")
    seat = iota((32, 128), 0)
    lane = iota((128, 128), 1)
    prefix = jnp.concatenate(
        [as_mask(iota((128, 128), 0) < lane), jnp.ones((128, 128), jnp.bfloat16)], 1
    )
    ids_copy.wait()
    ids = ids_ref[...]
    local = ids & 1023
    block = ((ids >> 10) + 48) & 127
    role = block >> 5
    low_bit = jnp.where(role == 2, local >> 9, role)
    target = ((block >> 2) & 7) * 2 + low_bit + jnp.where(role == 2, 16, 0)
    target = jnp.where(((block & 3) == group) & (role < 3), target, -1)
    here = [seat == target[k : k + 1, :] for k in range(8)]
    sums = dot(jnp.concatenate([as_mask(mask) for mask in here], 0), prefix)
    high = ((local >> 5) + 1).astype(jnp.float32)
    low = (local & 31).astype(jnp.float32)
    pad = jnp.zeros((112, 128), jnp.float32)
    named = jnp.concatenate([high, low, pad], 0).T
    running = jnp.zeros((32, 128), jnp.float32)
    chosen = []
    for k in range(8):
        rows = slice(k * 32, (k + 1) * 32)
        rank = running + sums[rows, :128]
        running = running + sums[rows, 128:]
        chosen.append(
            jnp.concatenate([as_mask(here[k] & (rank == float(s))) for s in range(RANKS)], 0)
        )
    counts_copy.wait()
    picked = jnp.zeros((RANKS * 32, 256), jnp.float32)
    for k in range(0, 8, 2):
        rows = []
        for m in (k, k + 1):
            counts = counts_ref[m * 128 : (m + 1) * 128, :].astype(jnp.float32)
            name = jnp.where(
                lane == 0, named[:, m : m + 1], jnp.where(lane == 1, named[:, 8 + m : 9 + m], 0.0)
            )
            rows.append(jnp.concatenate([counts, name], 1).astype(jnp.bfloat16))
        picked = picked + dot(
            jnp.concatenate([chosen[k], chosen[k + 1]], 1), jnp.concatenate(rows, 0)
        )
    names = jnp.zeros((16, 128), jnp.float32)
    for kind in range(2):
        for s in range(RANKS):
            rows = slice(s * 32 + kind * 16, s * 32 + kind * 16 + 16)
            out_ref[pl.ds(kind * RANKS + s, 16, stride=25), :] = picked[rows, :128]
            name = picked[rows, 128:129] * 32.0 + picked[rows, 129:130]
            names = jnp.where(lane[:16] == kind * RANKS + s, name, names)
    out_ref[pl.ds(24, 16, stride=25), :] = names


def traits_kernel(
    wave_ref, strength_ref, shift_ref, position_ref, weight_ref, mark_ref, out_ref
):
    lane = iota((1, 128), 1)
    row = mark_ref[0:1, :]
    for m, value in enumerate((wave_ref[0], strength_ref[0], shift_ref[0, 0], shift_ref[1, 0])):
        row = jnp.where(lane == m, value, row)
    for q in range(NODES):
        row = jnp.where(lane == 16 + q, position_ref[0, q], row)
        row = jnp.where(lane == 32 + q, position_ref[1, q], row)
        row = jnp.where(lane == 48 + q, weight_ref[q], row)
    out_ref[...] = row


def place_kernel(nodes_ref, got_ref, out_ref):
    names = got_ref[pl.ds(24, 16, stride=25), :]
    names = [names] + [pltpu.roll(names, 128 - s, 1) for s in range(1, 8)]
    names = jnp.concatenate(names, 0).T
    for kind, cells, start, stop in ((0, 768, 0, 96), (1, 384, 96, 144)):
        cell = iota((cells, 128), 0)
        masks, counts = [], []
        for s, width in ((0, 128), (8, 64)):
            at = kind * RANKS + s
            name = names[at : at + 1, :width].astype(jnp.int32)
            column = ((name & 31) + 12) & 31
            line = ((name >> 5) - 1) & (31 if kind == 0 else 15)
            key = jnp.where(
                (name > 0) & (column < LIVE_BLOCKS), line * LIVE_BLOCKS + column, -1
            )
            masks.append(as_mask(cell[:, :width] == key))
        for s in range(RANKS):
            rows = got_ref[pl.ds(kind * RANKS + s, 16, stride=25), :]
            counts.append(rows.astype(jnp.bfloat16))
        grid = dot(jnp.concatenate(masks, 1), jnp.concatenate(counts, 0))
        size = stop - start
        for d in range(8):
            out_ref[d * 144 + start : d * 144 + stop, :] = grid[d * size : (d + 1) * size]


def evaluate(square, wave, strength, weight):
    inverse = lax.rsqrt(square)
    turns = wave * (square * inverse)
    turns = turns - ((turns + ROUNDER) - ROUNDER)
    arg = turns * turns
    cosine = COS_TURN[-1] * arg + COS_TURN[-2]
    for value in COS_TURN[-3::-1]:
        cosine = cosine * arg + value
    sine = SIN_TURN[-1] * arg + SIN_TURN[-2]
    for value in SIN_TURN[-3::-1]:
        sine = sine * arg + value
    amplitude = weight * (1.0 + strength * inverse)
    return amplitude * cosine, amplitude * (turns * sine)


def fill_kernel(
    nodes_ref,
    got_ref,
    first_ref,
    turn_ref,
    second_ref,
    out_ref,
    near_ref,
    fill_ref,
    turned_ref,
):
    z, group = lax.axis_index("z"), lax.axis_index("y")
    seat = lax.axis_index("x") * 2 + lax.axis_index("core")
    cluster = (z >> 1) * 4 + group
    base = ((z & 1) * 32 + cluster) * 32 + seat * 4 - HALF
    base_split = (64 + cluster) * 32 + (z & 1) * 16 + seat * 2 - HALF
    column = (
        iota((LIVE_BLOCKS, 128), 0) * 128 + iota((LIVE_BLOCKS, 128), 1) - HALF
    ).astype(jnp.float32)
    traits = [[nodes_ref[p : p + 1, e : e + 1] for e in range(4)] for p in range(PLANES)]
    counts = []
    for b in range(ROWS):
        parts = [got_ref[m * 144 + b * 24 : m * 144 + b * 24 + 24, :] for m in range(8)]
        while len(parts) > 1:
            parts = [parts[m] + parts[m + 1] for m in range(0, len(parts), 2)]
        counts.append(parts[0])
    lane = iota((16, 128), 1)
    inner = lane < 64
    for m in range(4):
        pair = counts[m][11:13]
        merged = jnp.where(inner[0:1], pair[1:2], pair[0:1])
        for p in range(PLANES):
            near_ref[p * 4 + m : p * 4 + m + 1, :] = merged
    for p in range(PLANES):
        for e in range(4):
            at = 16 + e * 16 + p * 4
            near_ref[at : at + 4, :] = jnp.broadcast_to(traits[p][e], (4, 128))
    near_counts = near_ref[0:16, :]
    near_row = (base + (iota((16, 128), 0) & 3)).astype(jnp.float32) + near_ref[48:64, :]
    near_col = jnp.where(inner, lane, lane - 128).astype(jnp.float32) + near_ref[64:80, :]
    near_wave = near_ref[16:32, :] * (0.5 / math.pi)
    near_strength = near_ref[32:48, :]
    node_row = [nodes_ref[0:1, 16 + q : 17 + q] for q in range(NODES)]
    node_col = [nodes_ref[0:1, 32 + q : 33 + q] for q in range(NODES)]
    node_weight = [nodes_ref[0:1, 48 + q : 49 + q] for q in range(NODES)]
    weights = [
        [jnp.where(counts[b] > float(q), node_weight[q], 0.0) for q in range(FAR)]
        for b in range(ROWS)
    ]
    extra_real = jnp.zeros((16, 128), jnp.float32)
    extra_imag = jnp.zeros((16, 128), jnp.float32)
    for q in range(FAR, NODES):
        row_pos = near_row + node_row[q]
        col_pos = near_col + node_col[q]
        square = row_pos * row_pos + col_pos * col_pos + HEIGHT_SQ
        weight = jnp.where(near_counts > float(q), node_weight[q], 0.0)
        real, imag = evaluate(square, near_wave, near_strength, weight)
        extra_real = extra_real + real
        extra_imag = extra_imag + imag
    inner_pair = (iota((2, 128), 0) == 1) == inner[0:2]
    turn_real = turn_ref[0:32, :]
    turn_imag = turn_ref[32:64, :]
    for p in range(PLANES):
        wave, strength = traits[p][0] * (0.5 / math.pi), traits[p][1]
        shift_row, shift_col = traits[p][2], traits[p][3]
        col_base = column + shift_col
        col_sq = []
        for q in range(FAR):
            col_pos = col_base + node_col[q]
            col_sq.append(col_pos * col_pos)
        for b in range(ROWS):
            row_offset = (base + b if b < 4 else base_split + (b - 4)).astype(jnp.float32)
            total_real = jnp.zeros((LIVE_BLOCKS, 128), jnp.float32)
            total_imag = jnp.zeros((LIVE_BLOCKS, 128), jnp.float32)
            for q in range(FAR):
                row_pos = (row_offset + shift_row) + node_row[q]
                square = col_sq[q] + (row_pos * row_pos + HEIGHT_SQ)
                real, imag = evaluate(square, wave, strength, weights[b][q])
                total_real = total_real + real
                total_imag = total_imag + imag
            lanes = slice((p * ROWS + b) * 128, (p * ROWS + b) * 128 + 128)
            fill_ref[0:24, lanes] = total_real
            fill_ref[24:48, lanes] = -total_imag
            if b < 4:
                m = p * 4 + b
                fill_ref[11:13, lanes] = fill_ref[11:13, lanes] + jnp.where(
                    inner_pair, extra_real[m : m + 1], 0.0
                )
                fill_ref[35:37, lanes] = fill_ref[35:37, lanes] - jnp.where(
                    inner_pair, extra_imag[m : m + 1], 0.0
                )
        lanes = slice(p * ROWS * 128, (p + 1) * ROWS * 128)
        high, low = split(fill_ref[:, lanes])
        stage = dot(first_ref[...], jnp.concatenate([high, low, high], 0))
        for b in range(ROWS):
            real = stage[0:32, b * 128 : (b + 1) * 128]
            imag = stage[32:64, b * 128 : (b + 1) * 128]
            next_real = real * turn_real - imag * turn_imag
            next_imag = real * turn_imag + imag * turn_real
            for j in range(4):
                rows = slice(j * 8, j * 8 + 8)
                at = (((b // 2) * 4 + j) * 2 + b % 2) * 32 + p * 8
                turned_ref[at : at + 8, 0:128] = next_real[rows]
                turned_ref[at : at + 8, 128:256] = next_imag[rows]
    contract = (((1,), (1,)), ((), ()))
    left = iota((128, 128), 1) < 64
    for i in range(3):
        high, low = split(turned_ref[i * 256 : (i + 1) * 256, :])
        both = lax.dot_general(second_ref[...], high, contract, preferred_element_type=jnp.float32)
        rest = lax.dot_general(
            second_ref[0:256, :], low, contract, preferred_element_type=jnp.float32
        )
        product = (both[0:256] + both[256:512]) + rest
        for m in range(2):
            real = product[0:128, m * 128 : (m + 1) * 128]
            imag = product[128:256, m * 128 : (m + 1) * 128]
            even = jnp.where(left, real, pltpu.roll(imag, 64, 1))
            odd = jnp.where(left, pltpu.roll(real, 64, 1), imag)
            out_ref[pl.ds(m * 6 + i, 128, stride=12), :] = even
            out_ref[pl.ds(m * 6 + 3 + i, 128, stride=12), :] = odd


def fft_list(values):
    size = len(values)
    if size == 1:
        return values
    even = fft_list(values[0::2])
    odd = fft_list(values[1::2])
    top, bottom = [], []
    for k in range(size // 2):
        real, imag = odd[k]
        if k == 0:
            pass
        elif 4 * k == size:
            real, imag = imag, -real
        elif 8 * k == size:
            half = math.sqrt(0.5)
            real, imag = (real + imag) * half, (imag - real) * half
        elif 8 * k == 3 * size:
            half = math.sqrt(0.5)
            real, imag = (imag - real) * half, -(real + imag) * half
        else:
            cos = math.cos(2.0 * math.pi * k / size)
            sin = math.sin(2.0 * math.pi * k / size)
            real, imag = real * cos + imag * sin, imag * cos - real * sin
        top.append((even[k][0] + real, even[k][1] + imag))
        bottom.append((even[k][0] - real, even[k][1] - imag))
    return top + bottom


def column_kernel(
    got_ref,
    high_ref,
    low_ref,
    turn_ref,
    real_hbm,
    imag_hbm,
    gathered_ref,
    real_ref,
    imag_ref,
    sem,
):
    blank = jnp.zeros((32, 128), jnp.float32)
    for pair in range(16):
        parts = []
        for j in range(4):
            at = ((pair >> 1) * 4 + j) * 3 + (pair & 1)
            parts.append(got_ref[pl.ds(at, 16, stride=96), :])
        for j in range(4):
            at = ((pair >> 3) * 32 + (pair & 7) * 4 + j) * 3 + 2
            parts.append(got_ref[pl.ds(at, 8, stride=192), :])
        flipped = jnp.concatenate(parts + [blank], 0).T
        for m in range(2):
            for ri in range(2):
                for p in range(PLANES):
                    at = (p * 32 + pair * 2 + m) * 8
                    gathered_ref[at : at + 8, ri * 128 : (ri + 1) * 128] = flipped[
                        ((ri * 2 + m) * 4 + p) * 8 : ((ri * 2 + m) * 4 + p) * 8 + 8
                    ]
    high, low = split(gathered_ref[...])
    stage = dot(high, high_ref[...]) + dot(low, high_ref[...]) + dot(high, low_ref[...])
    copies = []
    for p in range(PLANES):
        values = []
        for r in range(32):
            at = (p * 32 + r) * 8
            real = stage[at : at + 8, 0:128]
            imag = stage[at : at + 8, 128:256]
            if r:
                turn_real = turn_ref[r : r + 1, :]
                turn_imag = turn_ref[32 + r : 33 + r, :]
                real, imag = (
                    real * turn_real - imag * turn_imag,
                    real * turn_imag + imag * turn_real,
                )
            values.append((real, imag))
        for u, (real, imag) in enumerate(fft_list(values)):
            real_ref[p, :, u * 128 : (u + 1) * 128] = real
            imag_ref[p, :, u * 128 : (u + 1) * 128] = imag
        for m, (source, target) in enumerate(((real_ref, real_hbm), (imag_ref, imag_hbm))):
            copy = pltpu.make_async_copy(source.at[p], target.at[p], sem.at[p * 2 + m])
            copy.start()
            copies.append(copy)
    for copy in copies:
        copy.wait()


VMEM = pl.BlockSpec(memory_space=pltpu.VMEM)
SMEM = pl.BlockSpec(memory_space=pltpu.SMEM)
HBM = pl.BlockSpec(memory_space=pltpu.HBM)
PARAMS = pltpu.CompilerParams(vmem_limit_bytes=40 * 1024 * 1024)


def exchange(values, axes):
    return lax.all_to_all(values, axes, split_axis=0, concat_axis=0, tiled=True)


def shards(
    piece_ids, point_counts, wavenumber, strength, displacement, node_position, node_weights
):
    first, turn_one, second, third, turn_two = tables()
    sent, mark = pl.pallas_call(
        sort_kernel,
        out_shape=(
            jax.ShapeDtypeStruct((400, 128), jnp.float32),
            jax.ShapeDtypeStruct((8, 128), jnp.float32),
        ),
        in_specs=[HBM, HBM],
        out_specs=(VMEM, VMEM),
        scratch_shapes=[
            pltpu.VMEM((8, 128), jnp.int32),
            pltpu.VMEM((1024, 128), jnp.int32),
            pltpu.SemaphoreType.DMA((2,)),
        ],
        compiler_params=pltpu.CompilerParams(vmem_limit_bytes=62 * 1024 * 1024),
    )(piece_ids.reshape(8, 128), point_counts)
    got = exchange(sent.reshape(400, 1, 128), "z").reshape(400, 128)
    nodes = pl.pallas_call(
        traits_kernel,
        out_shape=jax.ShapeDtypeStruct((1, 128), jnp.float32),
        in_specs=[SMEM] * 5 + [VMEM],
        out_specs=VMEM,
        compiler_params=PARAMS,
    )(wavenumber, strength, displacement, node_position, node_weights, mark)
    nodes = lax.all_gather(nodes, "y", axis=0, tiled=True)
    grid = pl.pallas_call(
        place_kernel,
        out_shape=jax.ShapeDtypeStruct((1152, 128), jnp.float32),
        in_specs=[VMEM, VMEM],
        out_specs=VMEM,
        compiler_params=PARAMS,
    )(nodes, got)
    grid = exchange(grid.reshape(1152, 1, 128), ("x", "core")).reshape(1152, 128)
    sent = pl.pallas_call(
        fill_kernel,
        out_shape=jax.ShapeDtypeStruct((1536, 128), jnp.float32),
        in_specs=[VMEM] * 5,
        out_specs=VMEM,
        scratch_shapes=[
            pltpu.VMEM((80, 128), jnp.float32),
            pltpu.VMEM((48, PLANES * ROWS * 128), jnp.float32),
            pltpu.VMEM((768, 256), jnp.float32),
        ],
        compiler_params=PARAMS,
    )(nodes, grid, first, turn_one, second)
    got = exchange(
        sent.reshape(1536, 1, 128), ("z", "x", "core", "y")
    ).reshape(1536, 128)
    shape = jax.ShapeDtypeStruct((PLANES, 8, LENGTH), jnp.float32)
    return pl.pallas_call(
        column_kernel,
        out_shape=(shape, shape),
        in_specs=[VMEM] * 4,
        out_specs=(HBM, HBM),
        scratch_shapes=[
            pltpu.VMEM((1024, 256), jnp.float32),
            pltpu.VMEM((PLANES, 8, LENGTH), jnp.float32),
            pltpu.VMEM((PLANES, 8, LENGTH), jnp.float32),
            pltpu.SemaphoreType.DMA((2 * PLANES,)),
        ],
        compiler_params=PARAMS,
    )(got, third[0], third[1], turn_two)


def solution(mesh):
    every = ("z", "x", "core", "y")
    fine = Mesh(mesh.devices.reshape(16, 4, 2, 4), every)
    wide = every[:3]
    placed = (P(wide), P(wide, None), P("y"), P("y"), P(None, "y"), P(), P())
    return jax.shard_map(
        shards,
        mesh=fine,
        in_specs=placed,
        out_specs=(P(None, every, None), P(None, every, None)),
        check_vma=False,
    )
```

```python
import functools
import math

import jax
import jax.numpy as jnp
import numpy as np
from jax import lax
from jax.experimental import pallas as pl
from jax.experimental.pallas import tpu as pltpu
from jax.sharding import Mesh, PartitionSpec as P

LENGTH = 4096
NODES = 15
FAR = 3
HEIGHT_SQ = 0.0625
RANKS = 12
LIVE_BLOCKS = 24
HALF = 1536
ROWS = 6
PLANES = 4
FAR_ROWS = PLANES * ROWS * FAR * 48
TERM_ROWS = FAR_ROWS + (NODES - FAR) * 32

ROUNDER = 12582912.0


def fit_even(function, degree):
    top = math.pi**2
    grid = (np.cos(np.pi * (np.arange(400) + 0.5) / 400) + 1.0) * 0.5 * top
    series = np.polynomial.chebyshev.Chebyshev.fit(grid, function(np.sqrt(grid)), degree, [0, top])
    return [float(x) for x in series.convert(kind=np.polynomial.Polynomial).coef]


COS_COEF = fit_even(np.cos, 6)
SIN_COEF = fit_even(lambda x: np.sin(x) / x, 5)
COS_TURN = [c * (2.0 * math.pi) ** (2 * k) for k, c in enumerate(COS_COEF)]
SIN_TURN = [c * (2.0 * math.pi) ** (2 * k + 1) for k, c in enumerate(SIN_COEF)]


def split_np(values):
    high = values.astype(np.float32).astype(jnp.bfloat16)
    low = (values - high.astype(np.float64)).astype(jnp.bfloat16)
    return high, low


def tables():
    v1 = np.arange(32)
    cb = np.arange(LIVE_BLOCKS)
    angle = 2.0 * np.pi * (((cb[None, :] - 12) * v1[:, None]) % 32) / 32
    cos, sin = np.cos(angle), np.sin(angle)
    first = np.concatenate(
        [np.concatenate([cos, sin], 1), np.concatenate([-sin, cos], 1)], 0
    )
    high, low = split_np(first)
    first = np.concatenate([high, high, low], 1)
    t = np.arange(128)
    angle = 2.0 * np.pi * (v1[:, None] * t[None, :]) / LENGTH
    turn_one = np.concatenate([np.cos(angle), -np.sin(angle)], 0).astype(np.float32)
    angle = 2.0 * np.pi * ((t[:, None] * t[None, :]) % 128) / 128
    cos, sin = np.cos(angle), np.sin(angle)
    second = np.concatenate([np.concatenate([cos, sin], 1), np.concatenate([-sin, cos], 1)], 0)
    second = np.concatenate(split_np(second / 64.0), 0)
    j, z = np.arange(4)[:, None], np.arange(16)[None, :]
    whole = ((z & 1) * 32 + (z >> 1) * 4 + j).reshape(64)
    c = np.concatenate([whole, (64 + z[:, :8] * 4 + j).reshape(32)])
    angle = 2.0 * np.pi * (((c[:, None] - 48) * t[None, :]) % 128) / 128
    third = np.zeros((2, 128, 2, 128))
    third[0, :96, 0] = np.cos(angle)
    third[0, :96, 1] = -np.sin(angle)
    third[1, :96, 0] = np.sin(angle)
    third[1, :96, 1] = np.cos(angle)
    third = split_np(third.reshape(256, 256) / 64.0)
    angle = 2.0 * np.pi * (v1[:, None] * t[None, :]) / LENGTH
    turn_two = np.concatenate([np.cos(angle), -np.sin(angle)], 0).astype(np.float32)
    return first, turn_one, second, third, turn_two


def iota(shape, axis):
    return lax.broadcasted_iota(jnp.int32, shape, axis)


def dot(left, right):
    return jnp.dot(left, right, preferred_element_type=jnp.float32)


def as_mask(chosen):
    return jnp.where(chosen, 1.0, 0.0).astype(jnp.bfloat16)


def split(values):
    high = values.astype(jnp.bfloat16)
    low = (values - high.astype(jnp.float32)).astype(jnp.bfloat16)
    return high, low


def sort_kernel(
    ids_hbm,
    counts_hbm,
    wave_hbm,
    strength_hbm,
    shift_hbm,
    position_hbm,
    weight_hbm,
    out_ref,
    nodes_ref,
    ids_ref,
    counts_ref,
    wave_ref,
    strength_ref,
    shift_ref,
    position_ref,
    weight_ref,
    sem,
):
    ids_copy = pltpu.make_async_copy(ids_hbm, ids_ref, sem.at[0])
    ids_copy.start()
    counts_copy = pltpu.make_async_copy(counts_hbm, counts_ref, sem.at[1])
    counts_copy.start()
    small = [
        pltpu.make_async_copy(source, target, sem.at[2 + m])
        for m, (source, target) in enumerate(
            (
                (wave_hbm, wave_ref),
                (strength_hbm, strength_ref),
                (shift_hbm, shift_ref),
                (position_hbm, position_ref),
                (weight_hbm, weight_ref),
            )
        )
    ]
    for one in small:
        one.start()
    group = lax.axis_index("y")
    seat = iota((32, 128), 0)
    lane = iota((128, 128), 1)
    prefix = jnp.concatenate(
        [as_mask(iota((128, 128), 0) < lane), jnp.ones((128, 128), jnp.bfloat16)], 1
    )
    ids_copy.wait()
    ids = ids_ref[...]
    local = ids & 1023
    block = ((ids >> 10) + 48) & 127
    role = block >> 5
    low_bit = jnp.where(role == 2, local >> 9, role)
    target = ((block >> 2) & 7) * 2 + low_bit + jnp.where(role == 2, 16, 0)
    target = jnp.where(((block & 3) == group) & (role < 3), target, -1)
    here = [seat == target[k : k + 1, :] for k in range(8)]
    sums = dot(jnp.concatenate([as_mask(mask) for mask in here], 0), prefix)
    high = ((local >> 5) + 1).astype(jnp.float32)
    low = (local & 31).astype(jnp.float32)
    pad = jnp.zeros((112, 128), jnp.float32)
    named = jnp.concatenate([high, low, pad], 0).T
    running = jnp.zeros((32, 128), jnp.float32)
    chosen = []
    for k in range(8):
        rows = slice(k * 32, (k + 1) * 32)
        rank = running + sums[rows, :128]
        running = running + sums[rows, 128:]
        chosen.append(
            jnp.concatenate([as_mask(here[k] & (rank == float(s))) for s in range(RANKS)], 0)
        )
    for one in small:
        one.wait()
    row = jnp.zeros((1, 128), jnp.float32)
    for m, value in enumerate((wave_ref[0], strength_ref[0], shift_ref[0], shift_ref[1])):
        row = jnp.where(lane[0:1] == m, value, row)
    for q in range(NODES):
        row = jnp.where(lane[0:1] == 16 + q, position_ref[0, q], row)
        row = jnp.where(lane[0:1] == 32 + q, position_ref[1, q], row)
        row = jnp.where(lane[0:1] == 48 + q, weight_ref[q], row)
    nodes_ref[...] = row
    counts_copy.wait()
    picked = jnp.zeros((RANKS * 32, 256), jnp.float32)
    for k in range(0, 8, 2):
        rows = []
        for m in (k, k + 1):
            counts = counts_ref[m * 128 : (m + 1) * 128, :].astype(jnp.float32)
            name = jnp.where(
                lane == 0, named[:, m : m + 1], jnp.where(lane == 1, named[:, 8 + m : 9 + m], 0.0)
            )
            rows.append(jnp.concatenate([counts, name], 1).astype(jnp.bfloat16))
        picked = picked + dot(
            jnp.concatenate([chosen[k], chosen[k + 1]], 1), jnp.concatenate(rows, 0)
        )
    names = jnp.zeros((16, 128), jnp.float32)
    for kind in range(2):
        for s in range(RANKS):
            rows = slice(s * 32 + kind * 16, s * 32 + kind * 16 + 16)
            out_ref[pl.ds(kind * RANKS + s, 16, stride=25), :] = picked[rows, :128]
            name = picked[rows, 128:129] * 32.0 + picked[rows, 129:130]
            names = jnp.where(lane[:16] == kind * RANKS + s, name, names)
    out_ref[pl.ds(24, 16, stride=25), :] = names


def place_kernel(terms_ref, got_ref, out_ref):
    names = got_ref[pl.ds(24, 16, stride=25), :]
    names = [names] + [pltpu.roll(names, 128 - s, 1) for s in range(1, 8)]
    names = jnp.concatenate(names, 0).T
    for kind, cells, start, stop in ((0, 768, 0, 96), (1, 384, 96, 144)):
        cell = iota((cells, 128), 0)
        masks, counts = [], []
        for s, width in ((0, 128), (8, 64)):
            at = kind * RANKS + s
            name = names[at : at + 1, :width].astype(jnp.int32)
            column = ((name & 31) + 12) & 31
            line = ((name >> 5) - 1) & (31 if kind == 0 else 15)
            key = jnp.where(
                (name > 0) & (column < LIVE_BLOCKS), line * LIVE_BLOCKS + column, -1
            )
            masks.append(as_mask(cell[:, :width] == key))
        for s in range(RANKS):
            rows = got_ref[pl.ds(kind * RANKS + s, 16, stride=25), :]
            counts.append(rows.astype(jnp.bfloat16))
        grid = dot(jnp.concatenate(masks, 1), jnp.concatenate(counts, 0))
        size = stop - start
        for d in range(8):
            out_ref[d * 144 + start : d * 144 + stop, :] = grid[d * size : (d + 1) * size]


def evaluate(square, wave, strength, weight):
    inverse = lax.rsqrt(square)
    turns = wave * (square * inverse)
    turns = turns - ((turns + ROUNDER) - ROUNDER)
    arg = turns * turns
    cosine = COS_TURN[-1] * arg + COS_TURN[-2]
    for value in COS_TURN[-3::-1]:
        cosine = cosine * arg + value
    sine = SIN_TURN[-1] * arg + SIN_TURN[-2]
    for value in SIN_TURN[-3::-1]:
        sine = sine * arg + value
    amplitude = weight + (weight * strength) * inverse
    return amplitude * cosine, amplitude * (turns * sine)


def terms_kernel(nodes_ref, out_ref, near_ref):
    z, group = lax.axis_index("z"), lax.axis_index("y")
    seat = lax.axis_index("x") * 2 + lax.axis_index("core")
    cluster = (z >> 1) * 4 + group
    base = ((z & 1) * 32 + cluster) * 32 + seat * 4 - HALF
    base_split = (64 + cluster) * 32 + (z & 1) * 16 + seat * 2 - HALF
    column = (
        iota((LIVE_BLOCKS, 128), 0) * 128 + iota((LIVE_BLOCKS, 128), 1) - HALF
    ).astype(jnp.float32)
    traits = [[nodes_ref[p : p + 1, e : e + 1] for e in range(4)] for p in range(PLANES)]
    node_row = [nodes_ref[0:1, 16 + q : 17 + q] for q in range(NODES)]
    node_col = [nodes_ref[0:1, 32 + q : 33 + q] for q in range(NODES)]
    node_weight = [nodes_ref[0:1, 48 + q : 49 + q] for q in range(NODES)]
    for p in range(PLANES):
        for e in range(4):
            at = e * 16 + p * 4
            near_ref[at : at + 4, :] = jnp.broadcast_to(traits[p][e], (4, 128))
    lane = iota((16, 128), 1)
    near_wave = near_ref[0:16, :] * (0.5 / math.pi)
    near_strength = near_ref[16:32, :]
    near_row = (base + (iota((16, 128), 0) & 3)).astype(jnp.float32) + near_ref[32:48, :]
    near_col = jnp.where(lane < 64, lane, lane - 128).astype(jnp.float32) + near_ref[48:64, :]
    for q in range(FAR, NODES):
        row_pos = near_row + node_row[q]
        col_pos = near_col + node_col[q]
        square = row_pos * row_pos + col_pos * col_pos + HEIGHT_SQ
        real, imag = evaluate(square, near_wave, near_strength, node_weight[q])
        at = FAR_ROWS + (q - FAR) * 32
        out_ref[at : at + 16, :] = real
        out_ref[at + 16 : at + 32, :] = imag
    for p in range(PLANES):
        wave, strength = traits[p][0] * (0.5 / math.pi), traits[p][1]
        shift_row, shift_col = traits[p][2], traits[p][3]
        col_base = column + shift_col
        for q in range(FAR):
            col_pos = col_base + node_col[q]
            col_sq = col_pos * col_pos
            for b in range(ROWS):
                offset = (base + b if b < 4 else base_split + (b - 4)).astype(jnp.float32)
                row_pos = (offset + shift_row) + node_row[q]
                square = col_sq + (row_pos * row_pos + HEIGHT_SQ)
                real, imag = evaluate(square, wave, strength, node_weight[q])
                at = ((p * ROWS + b) * FAR + q) * 48
                out_ref[at : at + 24, :] = real
                out_ref[at + 24 : at + 48, :] = imag


def fill_kernel(
    terms_ref,
    got_ref,
    first_ref,
    turn_ref,
    second_ref,
    out_ref,
    near_ref,
    fill_ref,
    turned_ref,
):
    counts = []
    for b in range(ROWS):
        parts = [got_ref[m * 144 + b * 24 : m * 144 + b * 24 + 24, :] for m in range(8)]
        while len(parts) > 1:
            parts = [parts[m] + parts[m + 1] for m in range(0, len(parts), 2)]
        counts.append(parts[0])
    inner = iota((2, 128), 1) < 64
    for m in range(4):
        pair = counts[m][11:13]
        merged = jnp.where(inner[0:1], pair[1:2], pair[0:1])
        for p in range(PLANES):
            near_ref[p * 4 + m : p * 4 + m + 1, :] = merged
    near_counts = near_ref[...]
    extra_real = jnp.zeros((16, 128), jnp.float32)
    extra_imag = jnp.zeros((16, 128), jnp.float32)
    for q in range(FAR, NODES):
        used = near_counts > float(q)
        at = FAR_ROWS + (q - FAR) * 32
        extra_real = extra_real + jnp.where(used, terms_ref[at : at + 16, :], 0.0)
        extra_imag = extra_imag + jnp.where(used, terms_ref[at + 16 : at + 32, :], 0.0)
    inner_pair = (iota((2, 128), 0) == 1) == inner
    used = [[counts[b] > float(q) for q in range(FAR)] for b in range(ROWS)]
    turn_real = turn_ref[0:32, :]
    turn_imag = turn_ref[32:64, :]
    for p in range(PLANES):
        for b in range(ROWS):
            total_real = jnp.zeros((LIVE_BLOCKS, 128), jnp.float32)
            total_imag = jnp.zeros((LIVE_BLOCKS, 128), jnp.float32)
            for q in range(FAR):
                at = ((p * ROWS + b) * FAR + q) * 48
                total_real = total_real + jnp.where(used[b][q], terms_ref[at : at + 24, :], 0.0)
                total_imag = total_imag + jnp.where(
                    used[b][q], terms_ref[at + 24 : at + 48, :], 0.0
                )
            lanes = slice((p * ROWS + b) * 128, (p * ROWS + b) * 128 + 128)
            fill_ref[0:24, lanes] = total_real
            fill_ref[24:48, lanes] = -total_imag
            if b < 4:
                m = p * 4 + b
                fill_ref[11:13, lanes] = fill_ref[11:13, lanes] + jnp.where(
                    inner_pair, extra_real[m : m + 1], 0.0
                )
                fill_ref[35:37, lanes] = fill_ref[35:37, lanes] - jnp.where(
                    inner_pair, extra_imag[m : m + 1], 0.0
                )
        lanes = slice(p * ROWS * 128, (p + 1) * ROWS * 128)
        high, low = split(fill_ref[:, lanes])
        stage = dot(first_ref[...], jnp.concatenate([high, low, high], 0))
        for b in range(ROWS):
            real = stage[0:32, b * 128 : (b + 1) * 128]
            imag = stage[32:64, b * 128 : (b + 1) * 128]
            next_real = real * turn_real - imag * turn_imag
            next_imag = real * turn_imag + imag * turn_real
            for j in range(4):
                rows = slice(j * 8, j * 8 + 8)
                at = (((b // 2) * 4 + j) * 2 + b % 2) * 32 + p * 8
                turned_ref[at : at + 8, 0:128] = next_real[rows]
                turned_ref[at : at + 8, 128:256] = next_imag[rows]
    contract = (((1,), (1,)), ((), ()))
    left = iota((128, 128), 1) < 64
    for i in range(3):
        high, low = split(turned_ref[i * 256 : (i + 1) * 256, :])
        both = lax.dot_general(second_ref[...], high, contract, preferred_element_type=jnp.float32)
        rest = lax.dot_general(
            second_ref[0:256, :], low, contract, preferred_element_type=jnp.float32
        )
        product = (both[0:256] + both[256:512]) + rest
        for m in range(2):
            real = product[0:128, m * 128 : (m + 1) * 128]
            imag = product[128:256, m * 128 : (m + 1) * 128]
            even = jnp.where(left, real, pltpu.roll(imag, 64, 1))
            odd = jnp.where(left, pltpu.roll(real, 64, 1), imag)
            out_ref[pl.ds(m * 6 + i, 128, stride=12), :] = even
            out_ref[pl.ds(m * 6 + 3 + i, 128, stride=12), :] = odd


def fft_list(values):
    size = len(values)
    if size == 1:
        return values
    even = fft_list(values[0::2])
    odd = fft_list(values[1::2])
    top, bottom = [], []
    for k in range(size // 2):
        real, imag = odd[k]
        if k == 0:
            pass
        elif 4 * k == size:
            real, imag = imag, -real
        elif 8 * k == size:
            half = math.sqrt(0.5)
            real, imag = (real + imag) * half, (imag - real) * half
        elif 8 * k == 3 * size:
            half = math.sqrt(0.5)
            real, imag = (imag - real) * half, -(real + imag) * half
        else:
            cos = math.cos(2.0 * math.pi * k / size)
            sin = math.sin(2.0 * math.pi * k / size)
            real, imag = real * cos + imag * sin, imag * cos - real * sin
        top.append((even[k][0] + real, even[k][1] + imag))
        bottom.append((even[k][0] - real, even[k][1] - imag))
    return top + bottom


def column_kernel(
    got_ref,
    high_ref,
    low_ref,
    turn_ref,
    real_hbm,
    imag_hbm,
    gathered_ref,
    real_ref,
    imag_ref,
    sem,
):
    blank = jnp.zeros((32, 128), jnp.float32)
    for pair in range(16):
        parts = []
        for j in range(4):
            at = ((pair >> 1) * 4 + j) * 3 + (pair & 1)
            parts.append(got_ref[pl.ds(at, 16, stride=96), :])
        for j in range(4):
            at = ((pair >> 3) * 32 + (pair & 7) * 4 + j) * 3 + 2
            parts.append(got_ref[pl.ds(at, 8, stride=192), :])
        flipped = jnp.concatenate(parts + [blank], 0).T
        for m in range(2):
            for ri in range(2):
                for p in range(PLANES):
                    at = (p * 32 + pair * 2 + m) * 8
                    gathered_ref[at : at + 8, ri * 128 : (ri + 1) * 128] = flipped[
                        ((ri * 2 + m) * 4 + p) * 8 : ((ri * 2 + m) * 4 + p) * 8 + 8
                    ]
    high, low = split(gathered_ref[...])
    stage = dot(high, high_ref[...]) + dot(low, high_ref[...]) + dot(high, low_ref[...])
    copies = []
    for p in range(PLANES):
        values = []
        for r in range(32):
            at = (p * 32 + r) * 8
            real = stage[at : at + 8, 0:128]
            imag = stage[at : at + 8, 128:256]
            if r:
                turn_real = turn_ref[r : r + 1, :]
                turn_imag = turn_ref[32 + r : 33 + r, :]
                real, imag = (
                    real * turn_real - imag * turn_imag,
                    real * turn_imag + imag * turn_real,
                )
            values.append((real, imag))
        for u, (real, imag) in enumerate(fft_list(values)):
            real_ref[p, :, u * 128 : (u + 1) * 128] = real
            imag_ref[p, :, u * 128 : (u + 1) * 128] = imag
        for m, (source, target) in enumerate(((real_ref, real_hbm), (imag_ref, imag_hbm))):
            copy = pltpu.make_async_copy(source.at[p], target.at[p], sem.at[p * 2 + m])
            copy.start()
            copies.append(copy)
    for copy in copies:
        copy.wait()


VMEM = pl.BlockSpec(memory_space=pltpu.VMEM)
SMEM = pl.BlockSpec(memory_space=pltpu.SMEM)
HBM = pl.BlockSpec(memory_space=pltpu.HBM)
PARAMS = pltpu.CompilerParams(vmem_limit_bytes=40 * 1024 * 1024)


def exchange(values, axes):
    return lax.all_to_all(values, axes, split_axis=0, concat_axis=0, tiled=True)


def shards(
    piece_ids, point_counts, wavenumber, strength, displacement, node_position, node_weights
):
    first, turn_one, second, third, turn_two = tables()
    sent, nodes = pl.pallas_call(
        sort_kernel,
        out_shape=(
            jax.ShapeDtypeStruct((400, 128), jnp.float32),
            jax.ShapeDtypeStruct((1, 128), jnp.float32),
        ),
        in_specs=[HBM] * 7,
        out_specs=(VMEM, VMEM),
        scratch_shapes=[
            pltpu.VMEM((8, 128), jnp.int32),
            pltpu.VMEM((1024, 128), jnp.int32),
            pltpu.SMEM((1,), jnp.float32),
            pltpu.SMEM((1,), jnp.float32),
            pltpu.SMEM((2,), jnp.float32),
            pltpu.SMEM((2, NODES), jnp.float32),
            pltpu.SMEM((NODES,), jnp.float32),
            pltpu.SemaphoreType.DMA((7,)),
        ],
        compiler_params=pltpu.CompilerParams(vmem_limit_bytes=62 * 1024 * 1024),
    )(
        piece_ids.reshape(8, 128),
        point_counts,
        wavenumber,
        strength,
        displacement.reshape(2),
        node_position,
        node_weights,
    )
    got = exchange(sent.reshape(400, 1, 128), "z").reshape(400, 128)
    nodes = lax.all_gather(nodes, "y", axis=0, tiled=True)
    terms = pl.pallas_call(
        terms_kernel,
        out_shape=jax.ShapeDtypeStruct((TERM_ROWS, 128), jnp.float32),
        in_specs=[VMEM],
        out_specs=VMEM,
        scratch_shapes=[pltpu.VMEM((64, 128), jnp.float32)],
        compiler_params=PARAMS,
    )(nodes)
    grid = pl.pallas_call(
        place_kernel,
        out_shape=jax.ShapeDtypeStruct((1152, 128), jnp.float32),
        in_specs=[pl.BlockSpec(memory_space=pl.ANY), VMEM],
        out_specs=VMEM,
        compiler_params=PARAMS,
    )(terms, got)
    grid = exchange(grid.reshape(1152, 1, 128), ("x", "core")).reshape(1152, 128)
    sent = pl.pallas_call(
        fill_kernel,
        out_shape=jax.ShapeDtypeStruct((1536, 128), jnp.float32),
        in_specs=[VMEM] * 5,
        out_specs=VMEM,
        scratch_shapes=[
            pltpu.VMEM((16, 128), jnp.float32),
            pltpu.VMEM((48, PLANES * ROWS * 128), jnp.float32),
            pltpu.VMEM((768, 256), jnp.float32),
        ],
        compiler_params=PARAMS,
    )(terms, grid, first, turn_one, second)
    got = exchange(
        sent.reshape(1536, 1, 128), ("z", "x", "core", "y")
    ).reshape(1536, 128)
    shape = jax.ShapeDtypeStruct((PLANES, 8, LENGTH), jnp.float32)
    return pl.pallas_call(
        column_kernel,
        out_shape=(shape, shape),
        in_specs=[VMEM] * 4,
        out_specs=(HBM, HBM),
        scratch_shapes=[
            pltpu.VMEM((1024, 256), jnp.float32),
            pltpu.VMEM((PLANES, 8, LENGTH), jnp.float32),
            pltpu.VMEM((PLANES, 8, LENGTH), jnp.float32),
            pltpu.SemaphoreType.DMA((2 * PLANES,)),
        ],
        compiler_params=PARAMS,
    )(got, third[0], third[1], turn_two)


def solution(mesh):
    every = ("z", "x", "core", "y")
    fine = Mesh(mesh.devices.reshape(16, 4, 2, 4), every)
    wide = every[:3]
    placed = (P(wide), P(wide, None), P("y"), P("y"), P(None, "y"), P(), P())
    return jax.shard_map(
        shards,
        mesh=fine,
        in_specs=placed,
        out_specs=(P(None, every, None), P(None, every, None)),
        check_vma=False,
    )
```

```python
import functools
import math

import jax
import jax.numpy as jnp
import numpy as np
from jax import lax
from jax.experimental import pallas as pl
from jax.experimental.pallas import tpu as pltpu
from jax.sharding import Mesh, PartitionSpec as P

LENGTH = 4096
NODES = 15
FAR = 3
HEIGHT_SQ = 0.0625
RANKS = 12
LIVE_BLOCKS = 24
HALF = 1536
ROWS = 6
PLANES = 4
FAR_ROWS = PLANES * ROWS * FAR * 48
TERM_ROWS = FAR_ROWS + (NODES - FAR) * 32

ROUNDER = 12582912.0


def fit_even(function, degree):
    top = math.pi**2
    grid = (np.cos(np.pi * (np.arange(400) + 0.5) / 400) + 1.0) * 0.5 * top
    series = np.polynomial.chebyshev.Chebyshev.fit(grid, function(np.sqrt(grid)), degree, [0, top])
    return [float(x) for x in series.convert(kind=np.polynomial.Polynomial).coef]


COS_COEF = fit_even(np.cos, 6)
SIN_COEF = fit_even(lambda x: np.sin(x) / x, 5)
COS_TURN = [c * (2.0 * math.pi) ** (2 * k) for k, c in enumerate(COS_COEF)]
SIN_TURN = [c * (2.0 * math.pi) ** (2 * k + 1) for k, c in enumerate(SIN_COEF)]


def split_np(values):
    high = values.astype(np.float32).astype(jnp.bfloat16)
    low = (values - high.astype(np.float64)).astype(jnp.bfloat16)
    return high, low


def tables():
    v1 = np.arange(32)
    cb = np.arange(LIVE_BLOCKS)
    angle = 2.0 * np.pi * (((cb[None, :] - 12) * v1[:, None]) % 32) / 32
    cos, sin = np.cos(angle), np.sin(angle)
    first = np.concatenate(
        [np.concatenate([cos, sin], 1), np.concatenate([-sin, cos], 1)], 0
    )
    high, low = split_np(first)
    first = np.concatenate([high, high, low], 1)
    t = np.arange(128)
    angle = 2.0 * np.pi * (v1[:, None] * t[None, :]) / LENGTH
    turn_one = np.concatenate([np.cos(angle), -np.sin(angle)], 0).astype(np.float32)
    core, z, x = np.arange(2)[:, None, None], np.arange(16)[:, None], np.arange(4)
    wide = (z * 8 + x * 2 + core).reshape(128)
    angle = 2.0 * np.pi * ((wide[:, None] * t[None, :]) % 128) / 128
    cos, sin = np.cos(angle), np.sin(angle)
    second = np.concatenate([np.concatenate([cos, sin], 1), np.concatenate([-sin, cos], 1)], 0)
    second = np.concatenate(split_np(second / 64.0), 0)
    j, z = np.arange(4)[:, None], np.arange(16)[None, :]
    whole = ((z & 1) * 32 + (z >> 1) * 4 + j).reshape(64)
    c = np.concatenate([whole, (64 + z[:, :8] * 4 + j).reshape(32)])
    angle = 2.0 * np.pi * (((c[:, None] - 48) * t[None, :]) % 128) / 128
    third = np.zeros((2, 128, 2, 128))
    third[0, :96, 0] = np.cos(angle)
    third[0, :96, 1] = -np.sin(angle)
    third[1, :96, 0] = np.sin(angle)
    third[1, :96, 1] = np.cos(angle)
    third = split_np(third.reshape(256, 256) / 64.0)
    angle = 2.0 * np.pi * (v1[:, None] * t[None, :]) / LENGTH
    turn_two = np.concatenate([np.cos(angle), -np.sin(angle)], 0).astype(np.float32)
    return first, turn_one, second, third, turn_two


def iota(shape, axis):
    return lax.broadcasted_iota(jnp.int32, shape, axis)


def dot(left, right):
    return jnp.dot(left, right, preferred_element_type=jnp.float32)


def as_mask(chosen):
    return jnp.where(chosen, 1.0, 0.0).astype(jnp.bfloat16)


def split(values):
    high = values.astype(jnp.bfloat16)
    low = (values - high.astype(jnp.float32)).astype(jnp.bfloat16)
    return high, low


def sort_kernel(
    ids_hbm,
    counts_hbm,
    wave_hbm,
    strength_hbm,
    shift_hbm,
    position_hbm,
    weight_hbm,
    out_ref,
    nodes_ref,
    ids_ref,
    counts_ref,
    wave_ref,
    strength_ref,
    shift_ref,
    position_ref,
    weight_ref,
    sem,
):
    ids_copy = pltpu.make_async_copy(ids_hbm, ids_ref, sem.at[0])
    ids_copy.start()
    counts_copy = pltpu.make_async_copy(counts_hbm, counts_ref, sem.at[1])
    counts_copy.start()
    small = [
        pltpu.make_async_copy(source, target, sem.at[2 + m])
        for m, (source, target) in enumerate(
            (
                (wave_hbm, wave_ref),
                (strength_hbm, strength_ref),
                (shift_hbm, shift_ref),
                (position_hbm, position_ref),
                (weight_hbm, weight_ref),
            )
        )
    ]
    for one in small:
        one.start()
    group = lax.axis_index("y")
    seat = iota((32, 128), 0)
    lane = iota((128, 128), 1)
    prefix = jnp.concatenate(
        [as_mask(iota((128, 128), 0) < lane), jnp.ones((128, 128), jnp.bfloat16)], 1
    )
    ids_copy.wait()
    ids = ids_ref[...]
    local = ids & 1023
    block = ((ids >> 10) + 48) & 127
    role = block >> 5
    low_bit = jnp.where(role == 2, local >> 9, role)
    target = ((block >> 2) & 7) * 2 + low_bit + jnp.where(role == 2, 16, 0)
    target = jnp.where(((block & 3) == group) & (role < 3), target, -1)
    here = [seat == target[k : k + 1, :] for k in range(8)]
    sums = dot(jnp.concatenate([as_mask(mask) for mask in here], 0), prefix)
    high = ((local >> 5) + 1).astype(jnp.float32)
    low = (local & 31).astype(jnp.float32)
    pad = jnp.zeros((112, 128), jnp.float32)
    named = jnp.concatenate([high, low, pad], 0).T
    running = jnp.zeros((32, 128), jnp.float32)
    chosen = []
    for k in range(8):
        rows = slice(k * 32, (k + 1) * 32)
        rank = running + sums[rows, :128]
        running = running + sums[rows, 128:]
        chosen.append(
            jnp.concatenate([as_mask(here[k] & (rank == float(s))) for s in range(RANKS)], 0)
        )
    for one in small:
        one.wait()
    row = jnp.zeros((1, 128), jnp.float32)
    for m, value in enumerate((wave_ref[0], strength_ref[0], shift_ref[0], shift_ref[1])):
        row = jnp.where(lane[0:1] == m, value, row)
    for q in range(NODES):
        row = jnp.where(lane[0:1] == 16 + q, position_ref[0, q], row)
        row = jnp.where(lane[0:1] == 32 + q, position_ref[1, q], row)
        row = jnp.where(lane[0:1] == 48 + q, weight_ref[q], row)
    nodes_ref[...] = row
    counts_copy.wait()
    picked = jnp.zeros((RANKS * 32, 256), jnp.float32)
    for k in range(0, 8, 2):
        rows = []
        for m in (k, k + 1):
            counts = counts_ref[m * 128 : (m + 1) * 128, :].astype(jnp.float32)
            name = jnp.where(
                lane == 0, named[:, m : m + 1], jnp.where(lane == 1, named[:, 8 + m : 9 + m], 0.0)
            )
            rows.append(jnp.concatenate([counts, name], 1).astype(jnp.bfloat16))
        picked = picked + dot(
            jnp.concatenate([chosen[k], chosen[k + 1]], 1), jnp.concatenate(rows, 0)
        )
    names = jnp.zeros((16, 128), jnp.float32)
    for kind in range(2):
        for s in range(RANKS):
            rows = slice(s * 32 + kind * 16, s * 32 + kind * 16 + 16)
            out_ref[pl.ds(kind * RANKS + s, 16, stride=25), :] = picked[rows, :128]
            name = picked[rows, 128:129] * 32.0 + picked[rows, 129:130]
            names = jnp.where(lane[:16] == kind * RANKS + s, name, names)
    out_ref[pl.ds(24, 16, stride=25), :] = names


def place_kernel(terms_ref, got_ref, out_ref):
    names = got_ref[pl.ds(24, 16, stride=25), :]
    names = [names] + [pltpu.roll(names, 128 - s, 1) for s in range(1, 8)]
    names = jnp.concatenate(names, 0).T
    for kind, cells, start, stop in ((0, 768, 0, 96), (1, 384, 96, 144)):
        cell = iota((cells, 128), 0)
        masks, counts = [], []
        for s, width in ((0, 128), (8, 64)):
            at = kind * RANKS + s
            name = names[at : at + 1, :width].astype(jnp.int32)
            column = ((name & 31) + 12) & 31
            line = ((name >> 5) - 1) & (31 if kind == 0 else 15)
            key = jnp.where(
                (name > 0) & (column < LIVE_BLOCKS), line * LIVE_BLOCKS + column, -1
            )
            masks.append(as_mask(cell[:, :width] == key))
        for s in range(RANKS):
            rows = got_ref[pl.ds(kind * RANKS + s, 16, stride=25), :]
            counts.append(rows.astype(jnp.bfloat16))
        grid = dot(jnp.concatenate(masks, 1), jnp.concatenate(counts, 0))
        size = stop - start
        for d in range(8):
            out_ref[d * 144 + start : d * 144 + stop, :] = grid[d * size : (d + 1) * size]


def evaluate(square, wave, strength, weight):
    inverse = lax.rsqrt(square)
    turns = wave * (square * inverse)
    turns = turns - ((turns + ROUNDER) - ROUNDER)
    arg = turns * turns
    cosine = COS_TURN[-1] * arg + COS_TURN[-2]
    for value in COS_TURN[-3::-1]:
        cosine = cosine * arg + value
    sine = SIN_TURN[-1] * arg + SIN_TURN[-2]
    for value in SIN_TURN[-3::-1]:
        sine = sine * arg + value
    amplitude = weight + (weight * strength) * inverse
    return amplitude * cosine, amplitude * (turns * sine)


def terms_kernel(nodes_ref, out_ref, near_ref):
    z, group = lax.axis_index("z"), lax.axis_index("y")
    seat = lax.axis_index("x") * 2 + lax.axis_index("core")
    cluster = (z >> 1) * 4 + group
    base = ((z & 1) * 32 + cluster) * 32 + seat * 4 - HALF
    base_split = (64 + cluster) * 32 + (z & 1) * 16 + seat * 2 - HALF
    column = (
        iota((LIVE_BLOCKS, 128), 0) * 128 + iota((LIVE_BLOCKS, 128), 1) - HALF
    ).astype(jnp.float32)
    traits = [[nodes_ref[p : p + 1, e : e + 1] for e in range(4)] for p in range(PLANES)]
    node_row = [nodes_ref[0:1, 16 + q : 17 + q] for q in range(NODES)]
    node_col = [nodes_ref[0:1, 32 + q : 33 + q] for q in range(NODES)]
    node_weight = [nodes_ref[0:1, 48 + q : 49 + q] for q in range(NODES)]
    for p in range(PLANES):
        for e in range(4):
            at = e * 16 + p * 4
            near_ref[at : at + 4, :] = jnp.broadcast_to(traits[p][e], (4, 128))
    lane = iota((16, 128), 1)
    near_wave = near_ref[0:16, :] * (0.5 / math.pi)
    near_strength = near_ref[16:32, :]
    near_row = (base + (iota((16, 128), 0) & 3)).astype(jnp.float32) + near_ref[32:48, :]
    near_col = jnp.where(lane < 64, lane, lane - 128).astype(jnp.float32) + near_ref[48:64, :]
    for q in range(FAR, NODES):
        row_pos = near_row + node_row[q]
        col_pos = near_col + node_col[q]
        square = row_pos * row_pos + col_pos * col_pos + HEIGHT_SQ
        real, imag = evaluate(square, near_wave, near_strength, node_weight[q])
        at = FAR_ROWS + (q - FAR) * 32
        out_ref[at : at + 16, :] = real
        out_ref[at + 16 : at + 32, :] = imag
    for p in range(PLANES):
        wave, strength = traits[p][0] * (0.5 / math.pi), traits[p][1]
        shift_row, shift_col = traits[p][2], traits[p][3]
        col_base = column + shift_col
        for q in range(FAR):
            col_pos = col_base + node_col[q]
            col_sq = col_pos * col_pos
            for b in range(ROWS):
                offset = (base + b if b < 4 else base_split + (b - 4)).astype(jnp.float32)
                row_pos = (offset + shift_row) + node_row[q]
                square = col_sq + (row_pos * row_pos + HEIGHT_SQ)
                real, imag = evaluate(square, wave, strength, node_weight[q])
                at = ((p * ROWS + b) * FAR + q) * 48
                out_ref[at : at + 24, :] = real
                out_ref[at + 24 : at + 48, :] = imag


def fill_kernel(
    terms_ref,
    got_ref,
    first_ref,
    turn_ref,
    second_ref,
    out_ref,
    near_ref,
    fill_ref,
    turned_ref,
):
    counts = []
    for b in range(ROWS):
        parts = [got_ref[m * 144 + b * 24 : m * 144 + b * 24 + 24, :] for m in range(8)]
        while len(parts) > 1:
            parts = [parts[m] + parts[m + 1] for m in range(0, len(parts), 2)]
        counts.append(parts[0])
    inner = iota((2, 128), 1) < 64
    for m in range(4):
        pair = counts[m][11:13]
        merged = jnp.where(inner[0:1], pair[1:2], pair[0:1])
        for p in range(PLANES):
            near_ref[p * 4 + m : p * 4 + m + 1, :] = merged
    near_counts = near_ref[...]
    extra_real = jnp.zeros((16, 128), jnp.float32)
    extra_imag = jnp.zeros((16, 128), jnp.float32)
    for q in range(FAR, NODES):
        used = near_counts > float(q)
        at = FAR_ROWS + (q - FAR) * 32
        extra_real = extra_real + jnp.where(used, terms_ref[at : at + 16, :], 0.0)
        extra_imag = extra_imag + jnp.where(used, terms_ref[at + 16 : at + 32, :], 0.0)
    inner_pair = (iota((2, 128), 0) == 1) == inner
    used = [[counts[b] > float(q) for q in range(FAR)] for b in range(ROWS)]
    turn_real = turn_ref[0:32, :]
    turn_imag = turn_ref[32:64, :]
    for p in range(PLANES):
        for b in range(ROWS):
            total_real = jnp.zeros((LIVE_BLOCKS, 128), jnp.float32)
            total_imag = jnp.zeros((LIVE_BLOCKS, 128), jnp.float32)
            for q in range(FAR):
                at = ((p * ROWS + b) * FAR + q) * 48
                total_real = total_real + jnp.where(used[b][q], terms_ref[at : at + 24, :], 0.0)
                total_imag = total_imag + jnp.where(
                    used[b][q], terms_ref[at + 24 : at + 48, :], 0.0
                )
            lanes = slice((p * ROWS + b) * 128, (p * ROWS + b) * 128 + 128)
            fill_ref[0:24, lanes] = total_real
            fill_ref[24:48, lanes] = -total_imag
            if b < 4:
                m = p * 4 + b
                fill_ref[11:13, lanes] = fill_ref[11:13, lanes] + jnp.where(
                    inner_pair, extra_real[m : m + 1], 0.0
                )
                fill_ref[35:37, lanes] = fill_ref[35:37, lanes] - jnp.where(
                    inner_pair, extra_imag[m : m + 1], 0.0
                )
        lanes = slice(p * ROWS * 128, (p + 1) * ROWS * 128)
        high, low = split(fill_ref[:, lanes])
        stage = dot(first_ref[...], jnp.concatenate([high, low, high], 0))
        for b in range(ROWS):
            real = stage[0:32, b * 128 : (b + 1) * 128]
            imag = stage[32:64, b * 128 : (b + 1) * 128]
            next_real = real * turn_real - imag * turn_imag
            next_imag = real * turn_imag + imag * turn_real
            for j in range(4):
                rows = slice(j * 8, j * 8 + 8)
                at = (((b // 2) * 4 + j) * 2 + b % 2) * 32 + p * 8
                turned_ref[at : at + 8, 0:128] = next_real[rows]
                turned_ref[at : at + 8, 128:256] = next_imag[rows]
    contract = (((1,), (1,)), ((), ()))
    left = iota((128, 128), 1) < 64
    for i in range(3):
        high, low = split(turned_ref[i * 256 : (i + 1) * 256, :])
        both = lax.dot_general(second_ref[...], high, contract, preferred_element_type=jnp.float32)
        rest = lax.dot_general(
            second_ref[0:256, :], low, contract, preferred_element_type=jnp.float32
        )
        product = (both[0:256] + both[256:512]) + rest
        for m in range(2):
            real = product[0:128, m * 128 : (m + 1) * 128]
            imag = product[128:256, m * 128 : (m + 1) * 128]
            even = jnp.where(left, real, pltpu.roll(imag, 64, 1))
            odd = jnp.where(left, pltpu.roll(real, 64, 1), imag)
            out_ref[pl.ds(m * 6 + i, 128, stride=12), :] = even
            out_ref[pl.ds(m * 6 + 3 + i, 128, stride=12), :] = odd


def fft_list(values):
    size = len(values)
    if size == 1:
        return values
    even = fft_list(values[0::2])
    odd = fft_list(values[1::2])
    top, bottom = [], []
    for k in range(size // 2):
        real, imag = odd[k]
        if k == 0:
            pass
        elif 4 * k == size:
            real, imag = imag, -real
        elif 8 * k == size:
            half = math.sqrt(0.5)
            real, imag = (real + imag) * half, (imag - real) * half
        elif 8 * k == 3 * size:
            half = math.sqrt(0.5)
            real, imag = (imag - real) * half, -(real + imag) * half
        else:
            cos = math.cos(2.0 * math.pi * k / size)
            sin = math.sin(2.0 * math.pi * k / size)
            real, imag = real * cos + imag * sin, imag * cos - real * sin
        top.append((even[k][0] + real, even[k][1] + imag))
        bottom.append((even[k][0] - real, even[k][1] - imag))
    return top + bottom


def column_kernel(
    got_ref,
    high_ref,
    low_ref,
    turn_ref,
    real_hbm,
    imag_hbm,
    gathered_ref,
    real_ref,
    imag_ref,
    sem,
):
    blank = jnp.zeros((32, 128), jnp.float32)
    for pair in range(16):
        parts = []
        for j in range(4):
            at = ((pair >> 1 & 1) * 256 + (pair >> 2) * 4 + j) * 3 + (pair & 1)
            parts.append(got_ref[pl.ds(at, 16, stride=48), :])
        for j in range(4):
            at = ((pair & 1) * 256 + (pair >> 3) * 16 + (pair >> 1 & 3) * 4 + j) * 3 + 2
            parts.append(got_ref[pl.ds(at, 8, stride=96), :])
        flipped = jnp.concatenate(parts + [blank], 0).T
        for m in range(2):
            for ri in range(2):
                for p in range(PLANES):
                    at = (p * 32 + pair * 2 + m) * 8
                    gathered_ref[at : at + 8, ri * 128 : (ri + 1) * 128] = flipped[
                        ((ri * 2 + m) * 4 + p) * 8 : ((ri * 2 + m) * 4 + p) * 8 + 8
                    ]
    high, low = split(gathered_ref[...])
    stage = dot(high, high_ref[...]) + dot(low, high_ref[...]) + dot(high, low_ref[...])
    copies = []
    for p in range(PLANES):
        values = []
        for r in range(32):
            at = (p * 32 + r) * 8
            real = stage[at : at + 8, 0:128]
            imag = stage[at : at + 8, 128:256]
            if r:
                turn_real = turn_ref[r : r + 1, :]
                turn_imag = turn_ref[32 + r : 33 + r, :]
                real, imag = (
                    real * turn_real - imag * turn_imag,
                    real * turn_imag + imag * turn_real,
                )
            values.append((real, imag))
        for u, (real, imag) in enumerate(fft_list(values)):
            real_ref[p, :, u * 128 : (u + 1) * 128] = real
            imag_ref[p, :, u * 128 : (u + 1) * 128] = imag
        for m, (source, target) in enumerate(((real_ref, real_hbm), (imag_ref, imag_hbm))):
            copy = pltpu.make_async_copy(source.at[p], target.at[p], sem.at[p * 2 + m])
            copy.start()
            copies.append(copy)
    for copy in copies:
        copy.wait()


VMEM = pl.BlockSpec(memory_space=pltpu.VMEM)
SMEM = pl.BlockSpec(memory_space=pltpu.SMEM)
HBM = pl.BlockSpec(memory_space=pltpu.HBM)
PARAMS = pltpu.CompilerParams(vmem_limit_bytes=40 * 1024 * 1024)


def exchange(values, axes):
    return lax.all_to_all(values, axes, split_axis=0, concat_axis=0, tiled=True)


def shards(
    piece_ids, point_counts, wavenumber, strength, displacement, node_position, node_weights
):
    first, turn_one, second, third, turn_two = tables()
    sent, nodes = pl.pallas_call(
        sort_kernel,
        out_shape=(
            jax.ShapeDtypeStruct((400, 128), jnp.float32),
            jax.ShapeDtypeStruct((1, 128), jnp.float32),
        ),
        in_specs=[HBM] * 7,
        out_specs=(VMEM, VMEM),
        scratch_shapes=[
            pltpu.VMEM((8, 128), jnp.int32),
            pltpu.VMEM((1024, 128), jnp.int32),
            pltpu.SMEM((1,), jnp.float32),
            pltpu.SMEM((1,), jnp.float32),
            pltpu.SMEM((2,), jnp.float32),
            pltpu.SMEM((2, NODES), jnp.float32),
            pltpu.SMEM((NODES,), jnp.float32),
            pltpu.SemaphoreType.DMA((7,)),
        ],
        compiler_params=pltpu.CompilerParams(vmem_limit_bytes=62 * 1024 * 1024),
    )(
        piece_ids.reshape(8, 128),
        point_counts,
        wavenumber,
        strength,
        displacement.reshape(2),
        node_position,
        node_weights,
    )
    got = exchange(sent.reshape(400, 1, 128), "z").reshape(400, 128)
    nodes = lax.all_gather(nodes, "y", axis=0, tiled=True)
    terms = pl.pallas_call(
        terms_kernel,
        out_shape=jax.ShapeDtypeStruct((TERM_ROWS, 128), jnp.float32),
        in_specs=[VMEM],
        out_specs=VMEM,
        scratch_shapes=[pltpu.VMEM((64, 128), jnp.float32)],
        compiler_params=PARAMS,
    )(nodes)
    grid = pl.pallas_call(
        place_kernel,
        out_shape=jax.ShapeDtypeStruct((1152, 128), jnp.float32),
        in_specs=[pl.BlockSpec(memory_space=pl.ANY), VMEM],
        out_specs=VMEM,
        compiler_params=PARAMS,
    )(terms, got)
    grid = exchange(grid.reshape(1152, 1, 128), ("x", "core")).reshape(1152, 128)
    sent = pl.pallas_call(
        fill_kernel,
        out_shape=jax.ShapeDtypeStruct((1536, 128), jnp.float32),
        in_specs=[VMEM] * 5,
        out_specs=VMEM,
        scratch_shapes=[
            pltpu.VMEM((16, 128), jnp.float32),
            pltpu.VMEM((48, PLANES * ROWS * 128), jnp.float32),
            pltpu.VMEM((768, 256), jnp.float32),
        ],
        compiler_params=PARAMS,
    )(terms, grid, first, turn_one, second)
    got = exchange(
        sent.reshape(1536, 1, 128), ("core", "z", "x", "y")
    ).reshape(1536, 128)
    shape = jax.ShapeDtypeStruct((PLANES, 8, LENGTH), jnp.float32)
    return pl.pallas_call(
        column_kernel,
        out_shape=(shape, shape),
        in_specs=[VMEM] * 4,
        out_specs=(HBM, HBM),
        scratch_shapes=[
            pltpu.VMEM((1024, 256), jnp.float32),
            pltpu.VMEM((PLANES, 8, LENGTH), jnp.float32),
            pltpu.VMEM((PLANES, 8, LENGTH), jnp.float32),
            pltpu.SemaphoreType.DMA((2 * PLANES,)),
        ],
        compiler_params=PARAMS,
    )(got, third[0], third[1], turn_two)


def solution(mesh):
    every = ("z", "x", "core", "y")
    fine = Mesh(mesh.devices.reshape(16, 4, 2, 4), every)
    wide = every[:3]
    placed = (P(wide), P(wide, None), P("y"), P("y"), P(None, "y"), P(), P())
    return jax.shard_map(
        shards,
        mesh=fine,
        in_specs=placed,
        out_specs=(P(None, every, None), P(None, every, None)),
        check_vma=False,
    )
```

```python
import functools
import math

import jax
import jax.numpy as jnp
import numpy as np
from jax import lax
from jax.experimental import pallas as pl
from jax.experimental.pallas import tpu as pltpu
from jax.sharding import Mesh, PartitionSpec as P

LENGTH = 4096
NODES = 15
FAR = 3
HEIGHT_SQ = 0.0625
RANKS = 12
LIVE_BLOCKS = 24
HALF = 1536
ROWS = 6
PLANES = 4
Z_ORDER = list(range(0, 16, 2)) + list(range(1, 16, 2))
FAR_ROWS = PLANES * ROWS * FAR * 48
TERM_ROWS = FAR_ROWS + (NODES - FAR) * 32

ROUNDER = 12582912.0


def fit_even(function, degree):
    top = math.pi**2
    grid = (np.cos(np.pi * (np.arange(400) + 0.5) / 400) + 1.0) * 0.5 * top
    series = np.polynomial.chebyshev.Chebyshev.fit(grid, function(np.sqrt(grid)), degree, [0, top])
    return [float(x) for x in series.convert(kind=np.polynomial.Polynomial).coef]


COS_COEF = fit_even(np.cos, 6)
SIN_COEF = fit_even(lambda x: np.sin(x) / x, 5)
COS_TURN = [c * (2.0 * math.pi) ** (2 * k) for k, c in enumerate(COS_COEF)]
SIN_TURN = [c * (2.0 * math.pi) ** (2 * k + 1) for k, c in enumerate(SIN_COEF)]


def split_np(values):
    high = values.astype(np.float32).astype(jnp.bfloat16)
    low = (values - high.astype(np.float64)).astype(jnp.bfloat16)
    return high, low


def tables():
    v1 = np.arange(32)
    cb = np.arange(LIVE_BLOCKS)
    angle = 2.0 * np.pi * (((cb[None, :] - 12) * v1[:, None]) % 32) / 32
    cos, sin = np.cos(angle), np.sin(angle)
    first = np.concatenate(
        [np.concatenate([cos, sin], 1), np.concatenate([-sin, cos], 1)], 0
    )
    high, low = split_np(first)
    first = np.concatenate([high, high, low], 1)
    t = np.arange(128)
    angle = 2.0 * np.pi * (v1[:, None] * t[None, :]) / LENGTH
    turn_one = np.concatenate([np.cos(angle), -np.sin(angle)], 0).astype(np.float32)
    core, x = np.arange(2)[:, None, None], np.arange(4)
    z = np.array(Z_ORDER)[:, None]
    wide = (z * 8 + x * 2 + core).reshape(128)
    angle = 2.0 * np.pi * ((wide[:, None] * t[None, :]) % 128) / 128
    cos, sin = np.cos(angle), np.sin(angle)
    second = np.concatenate([np.concatenate([cos, sin], 1), np.concatenate([-sin, cos], 1)], 0)
    second = np.concatenate(split_np(second / 64.0), 0)
    j, z = np.arange(4)[:, None], np.array(Z_ORDER)[None, :]
    whole = ((z & 1) * 32 + (z >> 1) * 4 + j).reshape(64)
    c = np.concatenate([whole, (64 + np.arange(8)[None, :] * 4 + j).reshape(32)])
    angle = 2.0 * np.pi * (((c[:, None] - 48) * t[None, :]) % 128) / 128
    third = np.zeros((2, 128, 2, 128))
    third[0, :96, 0] = np.cos(angle)
    third[0, :96, 1] = -np.sin(angle)
    third[1, :96, 0] = np.sin(angle)
    third[1, :96, 1] = np.cos(angle)
    third = split_np(third.reshape(256, 256) / 64.0)
    angle = 2.0 * np.pi * (v1[:, None] * t[None, :]) / LENGTH
    turn_two = np.concatenate([np.cos(angle), -np.sin(angle)], 0).astype(np.float32)
    return first, turn_one, second, third, turn_two


def iota(shape, axis):
    return lax.broadcasted_iota(jnp.int32, shape, axis)


def dot(left, right):
    return jnp.dot(left, right, preferred_element_type=jnp.float32)


def as_mask(chosen):
    return jnp.where(chosen, 1.0, 0.0).astype(jnp.bfloat16)


def split(values):
    high = values.astype(jnp.bfloat16)
    low = (values - high.astype(jnp.float32)).astype(jnp.bfloat16)
    return high, low


def sort_kernel(
    ids_hbm,
    counts_hbm,
    wave_hbm,
    strength_hbm,
    shift_hbm,
    position_hbm,
    weight_hbm,
    out_ref,
    nodes_ref,
    ids_ref,
    counts_ref,
    wave_ref,
    strength_ref,
    shift_ref,
    position_ref,
    weight_ref,
    sem,
):
    ids_copy = pltpu.make_async_copy(ids_hbm, ids_ref, sem.at[0])
    ids_copy.start()
    counts_copy = pltpu.make_async_copy(counts_hbm, counts_ref, sem.at[1])
    counts_copy.start()
    small = [
        pltpu.make_async_copy(source, target, sem.at[2 + m])
        for m, (source, target) in enumerate(
            (
                (wave_hbm, wave_ref),
                (strength_hbm, strength_ref),
                (shift_hbm, shift_ref),
                (position_hbm, position_ref),
                (weight_hbm, weight_ref),
            )
        )
    ]
    for one in small:
        one.start()
    group = lax.axis_index("y")
    seat = iota((32, 128), 0)
    lane = iota((128, 128), 1)
    prefix = jnp.concatenate(
        [as_mask(iota((128, 128), 0) < lane), jnp.ones((128, 128), jnp.bfloat16)], 1
    )
    ids_copy.wait()
    ids = ids_ref[...]
    local = ids & 1023
    block = ((ids >> 10) + 48) & 127
    role = block >> 5
    low_bit = jnp.where(role == 2, local >> 9, role)
    target = ((block >> 2) & 7) * 2 + low_bit + jnp.where(role == 2, 16, 0)
    target = jnp.where(((block & 3) == group) & (role < 3), target, -1)
    here = [seat == target[k : k + 1, :] for k in range(8)]
    sums = dot(jnp.concatenate([as_mask(mask) for mask in here], 0), prefix)
    high = ((local >> 5) + 1).astype(jnp.float32)
    low = (local & 31).astype(jnp.float32)
    pad = jnp.zeros((112, 128), jnp.float32)
    named = jnp.concatenate([high, low, pad], 0).T
    running = jnp.zeros((32, 128), jnp.float32)
    chosen = []
    for k in range(8):
        rows = slice(k * 32, (k + 1) * 32)
        rank = running + sums[rows, :128]
        running = running + sums[rows, 128:]
        chosen.append(
            jnp.concatenate([as_mask(here[k] & (rank == float(s))) for s in range(RANKS)], 0)
        )
    for one in small:
        one.wait()
    row = jnp.zeros((1, 128), jnp.float32)
    for m, value in enumerate((wave_ref[0], strength_ref[0], shift_ref[0], shift_ref[1])):
        row = jnp.where(lane[0:1] == m, value, row)
    for q in range(NODES):
        row = jnp.where(lane[0:1] == 16 + q, position_ref[0, q], row)
        row = jnp.where(lane[0:1] == 32 + q, position_ref[1, q], row)
        row = jnp.where(lane[0:1] == 48 + q, weight_ref[q], row)
    nodes_ref[...] = row
    counts_copy.wait()
    picked = jnp.zeros((RANKS * 32, 256), jnp.float32)
    for k in range(0, 8, 2):
        rows = []
        for m in (k, k + 1):
            counts = counts_ref[m * 128 : (m + 1) * 128, :].astype(jnp.float32)
            name = jnp.where(
                lane == 0, named[:, m : m + 1], jnp.where(lane == 1, named[:, 8 + m : 9 + m], 0.0)
            )
            rows.append(jnp.concatenate([counts, name], 1).astype(jnp.bfloat16))
        picked = picked + dot(
            jnp.concatenate([chosen[k], chosen[k + 1]], 1), jnp.concatenate(rows, 0)
        )
    names = jnp.zeros((16, 128), jnp.float32)
    for kind in range(2):
        for s in range(RANKS):
            rows = slice(s * 32 + kind * 16, s * 32 + kind * 16 + 16)
            out_ref[pl.ds(kind * RANKS + s, 16, stride=25), :] = picked[rows, :128]
            name = picked[rows, 128:129] * 32.0 + picked[rows, 129:130]
            names = jnp.where(lane[:16] == kind * RANKS + s, name, names)
    out_ref[pl.ds(24, 16, stride=25), :] = names


def place_kernel(terms_ref, got_ref, out_ref):
    names = got_ref[pl.ds(24, 16, stride=25), :]
    names = [names] + [pltpu.roll(names, 128 - s, 1) for s in range(1, 8)]
    names = jnp.concatenate(names, 0).T
    for kind, cells, start, stop in ((0, 768, 0, 96), (1, 384, 96, 144)):
        cell = iota((cells, 128), 0)
        masks, counts = [], []
        for s, width in ((0, 128), (8, 64)):
            at = kind * RANKS + s
            name = names[at : at + 1, :width].astype(jnp.int32)
            column = ((name & 31) + 12) & 31
            line = ((name >> 5) - 1) & (31 if kind == 0 else 15)
            key = jnp.where(
                (name > 0) & (column < LIVE_BLOCKS), line * LIVE_BLOCKS + column, -1
            )
            masks.append(as_mask(cell[:, :width] == key))
        for s in range(RANKS):
            rows = got_ref[pl.ds(kind * RANKS + s, 16, stride=25), :]
            counts.append(rows.astype(jnp.bfloat16))
        grid = dot(jnp.concatenate(masks, 1), jnp.concatenate(counts, 0))
        size = stop - start
        for d in range(8):
            out_ref[d * 144 + start : d * 144 + stop, :] = grid[d * size : (d + 1) * size]


def evaluate(square, wave, strength, weight):
    inverse = lax.rsqrt(square)
    turns = wave * (square * inverse)
    turns = turns - ((turns + ROUNDER) - ROUNDER)
    arg = turns * turns
    cosine = COS_TURN[-1] * arg + COS_TURN[-2]
    for value in COS_TURN[-3::-1]:
        cosine = cosine * arg + value
    sine = SIN_TURN[-1] * arg + SIN_TURN[-2]
    for value in SIN_TURN[-3::-1]:
        sine = sine * arg + value
    amplitude = weight + (weight * strength) * inverse
    return amplitude * cosine, amplitude * (turns * sine)


def terms_kernel(nodes_ref, out_ref, near_ref):
    z, group = lax.axis_index("z"), lax.axis_index("y")
    seat = lax.axis_index("x") * 2 + lax.axis_index("core")
    cluster = (z >> 1) * 4 + group
    base = ((z & 1) * 32 + cluster) * 32 + seat * 4 - HALF
    base_split = (64 + cluster) * 32 + (z & 1) * 16 + seat * 2 - HALF
    column = (
        iota((LIVE_BLOCKS, 128), 0) * 128 + iota((LIVE_BLOCKS, 128), 1) - HALF
    ).astype(jnp.float32)
    traits = [[nodes_ref[p : p + 1, e : e + 1] for e in range(4)] for p in range(PLANES)]
    node_row = [nodes_ref[0:1, 16 + q : 17 + q] for q in range(NODES)]
    node_col = [nodes_ref[0:1, 32 + q : 33 + q] for q in range(NODES)]
    node_weight = [nodes_ref[0:1, 48 + q : 49 + q] for q in range(NODES)]
    for p in range(PLANES):
        for e in range(4):
            at = e * 16 + p * 4
            near_ref[at : at + 4, :] = jnp.broadcast_to(traits[p][e], (4, 128))
    lane = iota((16, 128), 1)
    near_wave = near_ref[0:16, :] * (0.5 / math.pi)
    near_strength = near_ref[16:32, :]
    near_row = (base + (iota((16, 128), 0) & 3)).astype(jnp.float32) + near_ref[32:48, :]
    near_col = jnp.where(lane < 64, lane, lane - 128).astype(jnp.float32) + near_ref[48:64, :]
    for q in range(FAR, NODES):
        row_pos = near_row + node_row[q]
        col_pos = near_col + node_col[q]
        square = row_pos * row_pos + col_pos * col_pos + HEIGHT_SQ
        real, imag = evaluate(square, near_wave, near_strength, node_weight[q])
        at = FAR_ROWS + (q - FAR) * 32
        out_ref[at : at + 16, :] = real
        out_ref[at + 16 : at + 32, :] = imag
    for p in range(PLANES):
        wave, strength = traits[p][0] * (0.5 / math.pi), traits[p][1]
        shift_row, shift_col = traits[p][2], traits[p][3]
        col_base = column + shift_col
        for q in range(FAR):
            col_pos = col_base + node_col[q]
            col_sq = col_pos * col_pos
            for b in range(ROWS):
                offset = (base + b if b < 4 else base_split + (b - 4)).astype(jnp.float32)
                row_pos = (offset + shift_row) + node_row[q]
                square = col_sq + (row_pos * row_pos + HEIGHT_SQ)
                real, imag = evaluate(square, wave, strength, node_weight[q])
                at = ((p * ROWS + b) * FAR + q) * 48
                out_ref[at : at + 24, :] = real
                out_ref[at + 24 : at + 48, :] = imag


def fill_kernel(
    terms_ref,
    got_ref,
    first_ref,
    turn_ref,
    second_ref,
    out_ref,
    near_ref,
    fill_ref,
    turned_ref,
):
    counts = []
    for b in range(ROWS):
        parts = [got_ref[m * 144 + b * 24 : m * 144 + b * 24 + 24, :] for m in range(8)]
        while len(parts) > 1:
            parts = [parts[m] + parts[m + 1] for m in range(0, len(parts), 2)]
        counts.append(parts[0])
    inner = iota((2, 128), 1) < 64
    for m in range(4):
        pair = counts[m][11:13]
        merged = jnp.where(inner[0:1], pair[1:2], pair[0:1])
        for p in range(PLANES):
            near_ref[p * 4 + m : p * 4 + m + 1, :] = merged
    near_counts = near_ref[...]
    extra_real = jnp.zeros((16, 128), jnp.float32)
    extra_imag = jnp.zeros((16, 128), jnp.float32)
    for q in range(FAR, NODES):
        used = near_counts > float(q)
        at = FAR_ROWS + (q - FAR) * 32
        extra_real = extra_real + jnp.where(used, terms_ref[at : at + 16, :], 0.0)
        extra_imag = extra_imag + jnp.where(used, terms_ref[at + 16 : at + 32, :], 0.0)
    inner_pair = (iota((2, 128), 0) == 1) == inner
    used = [[counts[b] > float(q) for q in range(FAR)] for b in range(ROWS)]
    turn_real = turn_ref[0:32, :]
    turn_imag = turn_ref[32:64, :]
    for p in range(PLANES):
        for b in range(ROWS):
            total_real = jnp.zeros((LIVE_BLOCKS, 128), jnp.float32)
            total_imag = jnp.zeros((LIVE_BLOCKS, 128), jnp.float32)
            for q in range(FAR):
                at = ((p * ROWS + b) * FAR + q) * 48
                total_real = total_real + jnp.where(used[b][q], terms_ref[at : at + 24, :], 0.0)
                total_imag = total_imag + jnp.where(
                    used[b][q], terms_ref[at + 24 : at + 48, :], 0.0
                )
            lanes = slice((p * ROWS + b) * 128, (p * ROWS + b) * 128 + 128)
            fill_ref[0:24, lanes] = total_real
            fill_ref[24:48, lanes] = -total_imag
            if b < 4:
                m = p * 4 + b
                fill_ref[11:13, lanes] = fill_ref[11:13, lanes] + jnp.where(
                    inner_pair, extra_real[m : m + 1], 0.0
                )
                fill_ref[35:37, lanes] = fill_ref[35:37, lanes] - jnp.where(
                    inner_pair, extra_imag[m : m + 1], 0.0
                )
        lanes = slice(p * ROWS * 128, (p + 1) * ROWS * 128)
        high, low = split(fill_ref[:, lanes])
        stage = dot(first_ref[...], jnp.concatenate([high, low, high], 0))
        for b in range(ROWS):
            real = stage[0:32, b * 128 : (b + 1) * 128]
            imag = stage[32:64, b * 128 : (b + 1) * 128]
            next_real = real * turn_real - imag * turn_imag
            next_imag = real * turn_imag + imag * turn_real
            for j in range(4):
                rows = slice(j * 8, j * 8 + 8)
                at = (((b // 2) * 4 + j) * 2 + b % 2) * 32 + p * 8
                turned_ref[at : at + 8, 0:128] = next_real[rows]
                turned_ref[at : at + 8, 128:256] = next_imag[rows]
    contract = (((1,), (1,)), ((), ()))
    left = iota((128, 128), 1) < 64
    for i in range(3):
        high, low = split(turned_ref[i * 256 : (i + 1) * 256, :])
        both = lax.dot_general(second_ref[...], high, contract, preferred_element_type=jnp.float32)
        rest = lax.dot_general(
            second_ref[0:256, :], low, contract, preferred_element_type=jnp.float32
        )
        product = (both[0:256] + both[256:512]) + rest
        for m in range(2):
            real = product[0:128, m * 128 : (m + 1) * 128]
            imag = product[128:256, m * 128 : (m + 1) * 128]
            even = jnp.where(left, real, pltpu.roll(imag, 64, 1))
            odd = jnp.where(left, pltpu.roll(real, 64, 1), imag)
            out_ref[pl.ds(m * 6 + i, 128, stride=12), :] = even
            out_ref[pl.ds(m * 6 + 3 + i, 128, stride=12), :] = odd


def fft_list(values):
    size = len(values)
    if size == 1:
        return values
    even = fft_list(values[0::2])
    odd = fft_list(values[1::2])
    top, bottom = [], []
    for k in range(size // 2):
        real, imag = odd[k]
        if k == 0:
            pass
        elif 4 * k == size:
            real, imag = imag, -real
        elif 8 * k == size:
            half = math.sqrt(0.5)
            real, imag = (real + imag) * half, (imag - real) * half
        elif 8 * k == 3 * size:
            half = math.sqrt(0.5)
            real, imag = (imag - real) * half, -(real + imag) * half
        else:
            cos = math.cos(2.0 * math.pi * k / size)
            sin = math.sin(2.0 * math.pi * k / size)
            real, imag = real * cos + imag * sin, imag * cos - real * sin
        top.append((even[k][0] + real, even[k][1] + imag))
        bottom.append((even[k][0] - real, even[k][1] - imag))
    return top + bottom


def column_kernel(
    got_ref,
    high_ref,
    low_ref,
    turn_ref,
    real_hbm,
    imag_hbm,
    gathered_ref,
    real_ref,
    imag_ref,
    sem,
):
    blank = jnp.zeros((32, 128), jnp.float32)
    for pair in range(16):
        parts = []
        for j in range(4):
            at = ((pair >> 1 & 1) * 256 + (pair >> 2) * 4 + j) * 3 + (pair & 1)
            parts.append(got_ref[pl.ds(at, 16, stride=48), :])
        for j in range(4):
            at = ((pair & 1) * 256 + (pair >> 3) * 128 + (pair >> 1 & 3) * 4 + j) * 3 + 2
            parts.append(got_ref[pl.ds(at, 8, stride=48), :])
        flipped = jnp.concatenate(parts + [blank], 0).T
        for m in range(2):
            for ri in range(2):
                for p in range(PLANES):
                    at = (p * 32 + pair * 2 + m) * 8
                    gathered_ref[at : at + 8, ri * 128 : (ri + 1) * 128] = flipped[
                        ((ri * 2 + m) * 4 + p) * 8 : ((ri * 2 + m) * 4 + p) * 8 + 8
                    ]
    high, low = split(gathered_ref[...])
    stage = dot(high, high_ref[...]) + dot(low, high_ref[...]) + dot(high, low_ref[...])
    copies = []
    for p in range(PLANES):
        values = []
        for r in range(32):
            at = (p * 32 + r) * 8
            real = stage[at : at + 8, 0:128]
            imag = stage[at : at + 8, 128:256]
            if r:
                turn_real = turn_ref[r : r + 1, :]
                turn_imag = turn_ref[32 + r : 33 + r, :]
                real, imag = (
                    real * turn_real - imag * turn_imag,
                    real * turn_imag + imag * turn_real,
                )
            values.append((real, imag))
        for u, (real, imag) in enumerate(fft_list(values)):
            real_ref[p, :, u * 128 : (u + 1) * 128] = real
            imag_ref[p, :, u * 128 : (u + 1) * 128] = imag
        for m, (source, target) in enumerate(((real_ref, real_hbm), (imag_ref, imag_hbm))):
            copy = pltpu.make_async_copy(source.at[p], target.at[p], sem.at[p * 2 + m])
            copy.start()
            copies.append(copy)
    for copy in copies:
        copy.wait()


VMEM = pl.BlockSpec(memory_space=pltpu.VMEM)
SMEM = pl.BlockSpec(memory_space=pltpu.SMEM)
HBM = pl.BlockSpec(memory_space=pltpu.HBM)
PARAMS = pltpu.CompilerParams(vmem_limit_bytes=40 * 1024 * 1024)


def exchange(values, axes):
    return lax.all_to_all(values, axes, split_axis=0, concat_axis=0, tiled=True)


def shards(
    piece_ids, point_counts, wavenumber, strength, displacement, node_position, node_weights
):
    first, turn_one, second, third, turn_two = tables()
    sent, nodes = pl.pallas_call(
        sort_kernel,
        out_shape=(
            jax.ShapeDtypeStruct((400, 128), jnp.float32),
            jax.ShapeDtypeStruct((1, 128), jnp.float32),
        ),
        in_specs=[HBM] * 7,
        out_specs=(VMEM, VMEM),
        scratch_shapes=[
            pltpu.VMEM((8, 128), jnp.int32),
            pltpu.VMEM((1024, 128), jnp.int32),
            pltpu.SMEM((1,), jnp.float32),
            pltpu.SMEM((1,), jnp.float32),
            pltpu.SMEM((2,), jnp.float32),
            pltpu.SMEM((2, NODES), jnp.float32),
            pltpu.SMEM((NODES,), jnp.float32),
            pltpu.SemaphoreType.DMA((7,)),
        ],
        compiler_params=pltpu.CompilerParams(vmem_limit_bytes=62 * 1024 * 1024),
    )(
        piece_ids.reshape(8, 128),
        point_counts,
        wavenumber,
        strength,
        displacement.reshape(2),
        node_position,
        node_weights,
    )
    got = exchange(sent.reshape(400, 1, 128), "z").reshape(400, 128)
    nodes = lax.all_gather(nodes, "y", axis=0, tiled=True)
    terms = pl.pallas_call(
        terms_kernel,
        out_shape=jax.ShapeDtypeStruct((TERM_ROWS, 128), jnp.float32),
        in_specs=[VMEM],
        out_specs=VMEM,
        scratch_shapes=[pltpu.VMEM((64, 128), jnp.float32)],
        compiler_params=PARAMS,
    )(nodes)
    grid = pl.pallas_call(
        place_kernel,
        out_shape=jax.ShapeDtypeStruct((1152, 128), jnp.float32),
        in_specs=[pl.BlockSpec(memory_space=pl.ANY), VMEM],
        out_specs=VMEM,
        compiler_params=PARAMS,
    )(terms, got)
    grid = exchange(grid.reshape(1152, 1, 128), ("x", "core")).reshape(1152, 128)
    sent = pl.pallas_call(
        fill_kernel,
        out_shape=jax.ShapeDtypeStruct((1536, 128), jnp.float32),
        in_specs=[VMEM] * 5,
        out_specs=VMEM,
        scratch_shapes=[
            pltpu.VMEM((16, 128), jnp.float32),
            pltpu.VMEM((48, PLANES * ROWS * 128), jnp.float32),
            pltpu.VMEM((768, 256), jnp.float32),
        ],
        compiler_params=PARAMS,
    )(terms, grid, first, turn_one, second)
    order = [
        z * 32 + x * 8 + core * 4 + y
        for core in range(2)
        for z in Z_ORDER
        for x in range(4)
        for y in range(4)
    ]
    got = lax.all_to_all(
        sent.reshape(1536, 1, 128),
        ("z", "x", "core", "y"),
        split_axis=0,
        concat_axis=0,
        axis_index_groups=[order],
        tiled=True,
    ).reshape(1536, 128)
    shape = jax.ShapeDtypeStruct((PLANES, 8, LENGTH), jnp.float32)
    return pl.pallas_call(
        column_kernel,
        out_shape=(shape, shape),
        in_specs=[VMEM] * 4,
        out_specs=(HBM, HBM),
        scratch_shapes=[
            pltpu.VMEM((1024, 256), jnp.float32),
            pltpu.VMEM((PLANES, 8, LENGTH), jnp.float32),
            pltpu.VMEM((PLANES, 8, LENGTH), jnp.float32),
            pltpu.SemaphoreType.DMA((2 * PLANES,)),
        ],
        compiler_params=PARAMS,
    )(got, third[0], third[1], turn_two)


def solution(mesh):
    every = ("z", "x", "core", "y")
    fine = Mesh(mesh.devices.reshape(16, 4, 2, 4), every)
    wide = every[:3]
    placed = (P(wide), P(wide, None), P("y"), P("y"), P(None, "y"), P(), P())
    return jax.shard_map(
        shards,
        mesh=fine,
        in_specs=placed,
        out_specs=(P(None, every, None), P(None, every, None)),
        check_vma=False,
    )
```

```python
import functools
import math

import jax
import jax.numpy as jnp
import numpy as np
from jax import lax
from jax.experimental import pallas as pl
from jax.experimental.pallas import tpu as pltpu
from jax.sharding import Mesh, PartitionSpec as P

LENGTH = 4096
NODES = 15
FAR = 3
HEIGHT_SQ = 0.0625
RANKS = 12
LIVE_BLOCKS = 24
HALF = 1536
ROWS = 6
PLANES = 4
Z_ORDER = list(range(0, 16, 2)) + list(range(1, 16, 2))
FAR_ROWS = PLANES * ROWS * FAR * 48
TERM_ROWS = FAR_ROWS + (NODES - FAR) * 32

ROUNDER = 12582912.0


def fit_even(function, degree):
    top = math.pi**2
    grid = (np.cos(np.pi * (np.arange(400) + 0.5) / 400) + 1.0) * 0.5 * top
    series = np.polynomial.chebyshev.Chebyshev.fit(grid, function(np.sqrt(grid)), degree, [0, top])
    return [float(x) for x in series.convert(kind=np.polynomial.Polynomial).coef]


COS_COEF = fit_even(np.cos, 6)
SIN_COEF = fit_even(lambda x: np.sin(x) / x, 5)
COS_TURN = [c * (2.0 * math.pi) ** (2 * k) for k, c in enumerate(COS_COEF)]
SIN_TURN = [c * (2.0 * math.pi) ** (2 * k + 1) for k, c in enumerate(SIN_COEF)]


def split_np(values):
    high = values.astype(np.float32).astype(jnp.bfloat16)
    low = (values - high.astype(np.float64)).astype(jnp.bfloat16)
    return high, low


def tables():
    v1 = np.arange(32)
    cb = np.arange(LIVE_BLOCKS)
    angle = 2.0 * np.pi * (((cb[None, :] - 12) * v1[:, None]) % 32) / 32
    cos, sin = np.cos(angle), np.sin(angle)
    first = np.concatenate(
        [np.concatenate([cos, sin], 1), np.concatenate([-sin, cos], 1)], 0
    )
    high, low = split_np(first)
    first = np.concatenate([high, high, low], 1)
    t = np.arange(128)
    angle = 2.0 * np.pi * (v1[:, None] * t[None, :]) / LENGTH
    turn_one = np.concatenate([np.cos(angle), -np.sin(angle)], 0).astype(np.float32)
    core, x = np.arange(2)[:, None, None], np.arange(4)
    z = np.array(Z_ORDER)[:, None]
    wide = (z * 8 + x * 2 + core).reshape(128)
    angle = 2.0 * np.pi * ((wide[:, None] * t[None, :]) % 128) / 128
    cos, sin = np.cos(angle), np.sin(angle)
    second = np.concatenate([np.concatenate([cos, sin], 1), np.concatenate([-sin, cos], 1)], 0)
    second = np.concatenate(split_np(second / 64.0), 0)
    j, z = np.arange(4)[:, None], np.array(Z_ORDER)[None, :]
    whole = ((z & 1) * 32 + (z >> 1) * 4 + j).reshape(64)
    c = np.concatenate([whole, (64 + np.arange(8)[None, :] * 4 + j).reshape(32)])
    angle = 2.0 * np.pi * (((c[:, None] - 48) * t[None, :]) % 128) / 128
    third = np.zeros((2, 128, 2, 128))
    third[0, :96, 0] = np.cos(angle)
    third[0, :96, 1] = -np.sin(angle)
    third[1, :96, 0] = np.sin(angle)
    third[1, :96, 1] = np.cos(angle)
    third = split_np(third.reshape(256, 256) / 64.0)
    angle = 2.0 * np.pi * (v1[:, None] * t[None, :]) / LENGTH
    turn_two = np.concatenate([np.cos(angle), -np.sin(angle)], 0).astype(np.float32)
    return first, turn_one, second, third, turn_two


def iota(shape, axis):
    return lax.broadcasted_iota(jnp.int32, shape, axis)


def dot(left, right):
    return jnp.dot(left, right, preferred_element_type=jnp.float32)


def as_mask(chosen):
    return jnp.where(chosen, 1.0, 0.0).astype(jnp.bfloat16)


def split(values):
    high = values.astype(jnp.bfloat16)
    low = (values - high.astype(jnp.float32)).astype(jnp.bfloat16)
    return high, low


def sort_kernel(
    ids_hbm,
    counts_hbm,
    wave_hbm,
    strength_hbm,
    shift_hbm,
    position_hbm,
    weight_hbm,
    out_ref,
    nodes_ref,
    ids_ref,
    counts_ref,
    wave_ref,
    strength_ref,
    shift_ref,
    position_ref,
    weight_ref,
    sem,
):
    ids_copy = pltpu.make_async_copy(ids_hbm, ids_ref, sem.at[0])
    ids_copy.start()
    counts_copy = pltpu.make_async_copy(counts_hbm, counts_ref, sem.at[1])
    counts_copy.start()
    small = [
        pltpu.make_async_copy(source, target, sem.at[2 + m])
        for m, (source, target) in enumerate(
            (
                (wave_hbm, wave_ref),
                (strength_hbm, strength_ref),
                (shift_hbm, shift_ref),
                (position_hbm, position_ref),
                (weight_hbm, weight_ref),
            )
        )
    ]
    for one in small:
        one.start()
    group = lax.axis_index("y")
    seat = iota((32, 128), 0)
    lane = iota((128, 128), 1)
    prefix = jnp.concatenate(
        [as_mask(iota((128, 128), 0) < lane), jnp.ones((128, 128), jnp.bfloat16)], 1
    )
    ids_copy.wait()
    ids = ids_ref[...]
    local = ids & 1023
    block = ((ids >> 10) + 48) & 127
    role = block >> 5
    low_bit = jnp.where(role == 2, local >> 9, role)
    target = ((block >> 2) & 7) + low_bit * 8 + jnp.where(role == 2, 16, 0)
    target = jnp.where(((block & 3) == group) & (role < 3), target, -1)
    here = [seat == target[k : k + 1, :] for k in range(8)]
    sums = dot(jnp.concatenate([as_mask(mask) for mask in here], 0), prefix)
    high = ((local >> 5) + 1).astype(jnp.float32)
    low = (local & 31).astype(jnp.float32)
    pad = jnp.zeros((112, 128), jnp.float32)
    named = jnp.concatenate([high, low, pad], 0).T
    running = jnp.zeros((32, 128), jnp.float32)
    chosen = []
    for k in range(8):
        rows = slice(k * 32, (k + 1) * 32)
        rank = running + sums[rows, :128]
        running = running + sums[rows, 128:]
        chosen.append(
            jnp.concatenate([as_mask(here[k] & (rank == float(s))) for s in range(RANKS)], 0)
        )
    for one in small:
        one.wait()
    row = jnp.zeros((1, 128), jnp.float32)
    for m, value in enumerate((wave_ref[0], strength_ref[0], shift_ref[0], shift_ref[1])):
        row = jnp.where(lane[0:1] == m, value, row)
    for q in range(NODES):
        row = jnp.where(lane[0:1] == 16 + q, position_ref[0, q], row)
        row = jnp.where(lane[0:1] == 32 + q, position_ref[1, q], row)
        row = jnp.where(lane[0:1] == 48 + q, weight_ref[q], row)
    nodes_ref[...] = row
    counts_copy.wait()
    picked = jnp.zeros((RANKS * 32, 256), jnp.float32)
    for k in range(0, 8, 2):
        rows = []
        for m in (k, k + 1):
            counts = counts_ref[m * 128 : (m + 1) * 128, :].astype(jnp.float32)
            name = jnp.where(
                lane == 0, named[:, m : m + 1], jnp.where(lane == 1, named[:, 8 + m : 9 + m], 0.0)
            )
            rows.append(jnp.concatenate([counts, name], 1).astype(jnp.bfloat16))
        picked = picked + dot(
            jnp.concatenate([chosen[k], chosen[k + 1]], 1), jnp.concatenate(rows, 0)
        )
    names = jnp.zeros((16, 128), jnp.float32)
    for kind in range(2):
        for s in range(RANKS):
            rows = slice(s * 32 + kind * 16, s * 32 + kind * 16 + 16)
            out_ref[pl.ds(kind * RANKS + s, 16, stride=25), :] = picked[rows, :128]
            name = picked[rows, 128:129] * 32.0 + picked[rows, 129:130]
            names = jnp.where(lane[:16] == kind * RANKS + s, name, names)
    out_ref[pl.ds(24, 16, stride=25), :] = names


def place_kernel(terms_ref, got_ref, out_ref):
    names = got_ref[pl.ds(24, 16, stride=25), :]
    names = [names] + [pltpu.roll(names, 128 - s, 1) for s in range(1, 8)]
    names = jnp.concatenate(names, 0).T
    for kind, cells, start, stop in ((0, 768, 0, 96), (1, 384, 96, 144)):
        cell = iota((cells, 128), 0)
        masks, counts = [], []
        for s, width in ((0, 128), (8, 64)):
            at = kind * RANKS + s
            name = names[at : at + 1, :width].astype(jnp.int32)
            column = ((name & 31) + 12) & 31
            line = ((name >> 5) - 1) & (31 if kind == 0 else 15)
            key = jnp.where(
                (name > 0) & (column < LIVE_BLOCKS), line * LIVE_BLOCKS + column, -1
            )
            masks.append(as_mask(cell[:, :width] == key))
        for s in range(RANKS):
            rows = got_ref[pl.ds(kind * RANKS + s, 16, stride=25), :]
            counts.append(rows.astype(jnp.bfloat16))
        grid = dot(jnp.concatenate(masks, 1), jnp.concatenate(counts, 0))
        size = stop - start
        for d in range(8):
            out_ref[d * 144 + start : d * 144 + stop, :] = grid[d * size : (d + 1) * size]


def evaluate(square, wave, strength, weight):
    inverse = lax.rsqrt(square)
    turns = wave * (square * inverse)
    turns = turns - ((turns + ROUNDER) - ROUNDER)
    arg = turns * turns
    cosine = COS_TURN[-1] * arg + COS_TURN[-2]
    for value in COS_TURN[-3::-1]:
        cosine = cosine * arg + value
    sine = SIN_TURN[-1] * arg + SIN_TURN[-2]
    for value in SIN_TURN[-3::-1]:
        sine = sine * arg + value
    amplitude = weight + (weight * strength) * inverse
    return amplitude * cosine, amplitude * (turns * sine)


def terms_kernel(nodes_ref, out_ref, near_ref):
    z, group = lax.axis_index("z"), lax.axis_index("y")
    seat = lax.axis_index("x") * 2 + lax.axis_index("core")
    cluster = (z >> 1) * 4 + group
    base = ((z & 1) * 32 + cluster) * 32 + seat * 4 - HALF
    base_split = (64 + cluster) * 32 + (z & 1) * 16 + seat * 2 - HALF
    column = (
        iota((LIVE_BLOCKS, 128), 0) * 128 + iota((LIVE_BLOCKS, 128), 1) - HALF
    ).astype(jnp.float32)
    traits = [[nodes_ref[p : p + 1, e : e + 1] for e in range(4)] for p in range(PLANES)]
    node_row = [nodes_ref[0:1, 16 + q : 17 + q] for q in range(NODES)]
    node_col = [nodes_ref[0:1, 32 + q : 33 + q] for q in range(NODES)]
    node_weight = [nodes_ref[0:1, 48 + q : 49 + q] for q in range(NODES)]
    for p in range(PLANES):
        for e in range(4):
            at = e * 16 + p * 4
            near_ref[at : at + 4, :] = jnp.broadcast_to(traits[p][e], (4, 128))
    lane = iota((16, 128), 1)
    near_wave = near_ref[0:16, :] * (0.5 / math.pi)
    near_strength = near_ref[16:32, :]
    near_row = (base + (iota((16, 128), 0) & 3)).astype(jnp.float32) + near_ref[32:48, :]
    near_col = jnp.where(lane < 64, lane, lane - 128).astype(jnp.float32) + near_ref[48:64, :]
    for q in range(FAR, NODES):
        row_pos = near_row + node_row[q]
        col_pos = near_col + node_col[q]
        square = row_pos * row_pos + col_pos * col_pos + HEIGHT_SQ
        real, imag = evaluate(square, near_wave, near_strength, node_weight[q])
        at = FAR_ROWS + (q - FAR) * 32
        out_ref[at : at + 16, :] = real
        out_ref[at + 16 : at + 32, :] = imag
    for p in range(PLANES):
        wave, strength = traits[p][0] * (0.5 / math.pi), traits[p][1]
        shift_row, shift_col = traits[p][2], traits[p][3]
        col_base = column + shift_col
        for q in range(FAR):
            col_pos = col_base + node_col[q]
            col_sq = col_pos * col_pos
            for b in range(ROWS):
                offset = (base + b if b < 4 else base_split + (b - 4)).astype(jnp.float32)
                row_pos = (offset + shift_row) + node_row[q]
                square = col_sq + (row_pos * row_pos + HEIGHT_SQ)
                real, imag = evaluate(square, wave, strength, node_weight[q])
                at = ((p * ROWS + b) * FAR + q) * 48
                out_ref[at : at + 24, :] = real
                out_ref[at + 24 : at + 48, :] = imag


def fill_kernel(
    terms_ref,
    got_ref,
    first_ref,
    turn_ref,
    second_ref,
    out_ref,
    near_ref,
    fill_ref,
    turned_ref,
):
    counts = []
    for b in range(ROWS):
        parts = [got_ref[m * 144 + b * 24 : m * 144 + b * 24 + 24, :] for m in range(8)]
        while len(parts) > 1:
            parts = [parts[m] + parts[m + 1] for m in range(0, len(parts), 2)]
        counts.append(parts[0])
    inner = iota((2, 128), 1) < 64
    for m in range(4):
        pair = counts[m][11:13]
        merged = jnp.where(inner[0:1], pair[1:2], pair[0:1])
        for p in range(PLANES):
            near_ref[p * 4 + m : p * 4 + m + 1, :] = merged
    near_counts = near_ref[...]
    extra_real = jnp.zeros((16, 128), jnp.float32)
    extra_imag = jnp.zeros((16, 128), jnp.float32)
    for q in range(FAR, NODES):
        used = near_counts > float(q)
        at = FAR_ROWS + (q - FAR) * 32
        extra_real = extra_real + jnp.where(used, terms_ref[at : at + 16, :], 0.0)
        extra_imag = extra_imag + jnp.where(used, terms_ref[at + 16 : at + 32, :], 0.0)
    inner_pair = (iota((2, 128), 0) == 1) == inner
    used = [[counts[b] > float(q) for q in range(FAR)] for b in range(ROWS)]
    turn_real = turn_ref[0:32, :]
    turn_imag = turn_ref[32:64, :]
    for p in range(PLANES):
        for b in range(ROWS):
            total_real = jnp.zeros((LIVE_BLOCKS, 128), jnp.float32)
            total_imag = jnp.zeros((LIVE_BLOCKS, 128), jnp.float32)
            for q in range(FAR):
                at = ((p * ROWS + b) * FAR + q) * 48
                total_real = total_real + jnp.where(used[b][q], terms_ref[at : at + 24, :], 0.0)
                total_imag = total_imag + jnp.where(
                    used[b][q], terms_ref[at + 24 : at + 48, :], 0.0
                )
            lanes = slice((p * ROWS + b) * 128, (p * ROWS + b) * 128 + 128)
            fill_ref[0:24, lanes] = total_real
            fill_ref[24:48, lanes] = -total_imag
            if b < 4:
                m = p * 4 + b
                fill_ref[11:13, lanes] = fill_ref[11:13, lanes] + jnp.where(
                    inner_pair, extra_real[m : m + 1], 0.0
                )
                fill_ref[35:37, lanes] = fill_ref[35:37, lanes] - jnp.where(
                    inner_pair, extra_imag[m : m + 1], 0.0
                )
        lanes = slice(p * ROWS * 128, (p + 1) * ROWS * 128)
        high, low = split(fill_ref[:, lanes])
        stage = dot(first_ref[...], jnp.concatenate([high, low, high], 0))
        for b in range(ROWS):
            real = stage[0:32, b * 128 : (b + 1) * 128]
            imag = stage[32:64, b * 128 : (b + 1) * 128]
            next_real = real * turn_real - imag * turn_imag
            next_imag = real * turn_imag + imag * turn_real
            for j in range(4):
                rows = slice(j * 8, j * 8 + 8)
                at = (((b // 2) * 4 + j) * 2 + b % 2) * 32 + p * 8
                turned_ref[at : at + 8, 0:128] = next_real[rows]
                turned_ref[at : at + 8, 128:256] = next_imag[rows]
    contract = (((1,), (1,)), ((), ()))
    left = iota((128, 128), 1) < 64
    for i in range(3):
        high, low = split(turned_ref[i * 256 : (i + 1) * 256, :])
        both = lax.dot_general(second_ref[...], high, contract, preferred_element_type=jnp.float32)
        rest = lax.dot_general(
            second_ref[0:256, :], low, contract, preferred_element_type=jnp.float32
        )
        product = (both[0:256] + both[256:512]) + rest
        for m in range(2):
            real = product[0:128, m * 128 : (m + 1) * 128]
            imag = product[128:256, m * 128 : (m + 1) * 128]
            even = jnp.where(left, real, pltpu.roll(imag, 64, 1))
            odd = jnp.where(left, pltpu.roll(real, 64, 1), imag)
            out_ref[pl.ds(m * 6 + i, 128, stride=12), :] = even
            out_ref[pl.ds(m * 6 + 3 + i, 128, stride=12), :] = odd


def fft_list(values):
    size = len(values)
    if size == 1:
        return values
    even = fft_list(values[0::2])
    odd = fft_list(values[1::2])
    top, bottom = [], []
    for k in range(size // 2):
        real, imag = odd[k]
        if k == 0:
            pass
        elif 4 * k == size:
            real, imag = imag, -real
        elif 8 * k == size:
            half = math.sqrt(0.5)
            real, imag = (real + imag) * half, (imag - real) * half
        elif 8 * k == 3 * size:
            half = math.sqrt(0.5)
            real, imag = (imag - real) * half, -(real + imag) * half
        else:
            cos = math.cos(2.0 * math.pi * k / size)
            sin = math.sin(2.0 * math.pi * k / size)
            real, imag = real * cos + imag * sin, imag * cos - real * sin
        top.append((even[k][0] + real, even[k][1] + imag))
        bottom.append((even[k][0] - real, even[k][1] - imag))
    return top + bottom


def column_kernel(
    got_ref,
    high_ref,
    low_ref,
    turn_ref,
    real_hbm,
    imag_hbm,
    gathered_ref,
    real_ref,
    imag_ref,
    sem,
):
    blank = jnp.zeros((32, 128), jnp.float32)
    for pair in range(16):
        parts = []
        for j in range(4):
            at = ((pair >> 1 & 1) * 256 + (pair >> 2) * 4 + j) * 3 + (pair & 1)
            parts.append(got_ref[pl.ds(at, 16, stride=48), :])
        for j in range(4):
            at = ((pair & 1) * 256 + (pair >> 3) * 128 + (pair >> 1 & 3) * 4 + j) * 3 + 2
            parts.append(got_ref[pl.ds(at, 8, stride=48), :])
        flipped = jnp.concatenate(parts + [blank], 0).T
        for m in range(2):
            for ri in range(2):
                for p in range(PLANES):
                    at = (p * 32 + pair * 2 + m) * 8
                    gathered_ref[at : at + 8, ri * 128 : (ri + 1) * 128] = flipped[
                        ((ri * 2 + m) * 4 + p) * 8 : ((ri * 2 + m) * 4 + p) * 8 + 8
                    ]
    high, low = split(gathered_ref[...])
    stage = dot(high, high_ref[...]) + dot(low, high_ref[...]) + dot(high, low_ref[...])
    copies = []
    for p in range(PLANES):
        values = []
        for r in range(32):
            at = (p * 32 + r) * 8
            real = stage[at : at + 8, 0:128]
            imag = stage[at : at + 8, 128:256]
            if r:
                turn_real = turn_ref[r : r + 1, :]
                turn_imag = turn_ref[32 + r : 33 + r, :]
                real, imag = (
                    real * turn_real - imag * turn_imag,
                    real * turn_imag + imag * turn_real,
                )
            values.append((real, imag))
        for u, (real, imag) in enumerate(fft_list(values)):
            real_ref[p, :, u * 128 : (u + 1) * 128] = real
            imag_ref[p, :, u * 128 : (u + 1) * 128] = imag
        for m, (source, target) in enumerate(((real_ref, real_hbm), (imag_ref, imag_hbm))):
            copy = pltpu.make_async_copy(source.at[p], target.at[p], sem.at[p * 2 + m])
            copy.start()
            copies.append(copy)
    for copy in copies:
        copy.wait()


VMEM = pl.BlockSpec(memory_space=pltpu.VMEM)
SMEM = pl.BlockSpec(memory_space=pltpu.SMEM)
HBM = pl.BlockSpec(memory_space=pltpu.HBM)
PARAMS = pltpu.CompilerParams(vmem_limit_bytes=40 * 1024 * 1024)


def exchange(values, axes):
    return lax.all_to_all(values, axes, split_axis=0, concat_axis=0, tiled=True)


def shards(
    piece_ids, point_counts, wavenumber, strength, displacement, node_position, node_weights
):
    first, turn_one, second, third, turn_two = tables()
    sent, nodes = pl.pallas_call(
        sort_kernel,
        out_shape=(
            jax.ShapeDtypeStruct((400, 128), jnp.float32),
            jax.ShapeDtypeStruct((1, 128), jnp.float32),
        ),
        in_specs=[HBM] * 7,
        out_specs=(VMEM, VMEM),
        scratch_shapes=[
            pltpu.VMEM((8, 128), jnp.int32),
            pltpu.VMEM((1024, 128), jnp.int32),
            pltpu.SMEM((1,), jnp.float32),
            pltpu.SMEM((1,), jnp.float32),
            pltpu.SMEM((2,), jnp.float32),
            pltpu.SMEM((2, NODES), jnp.float32),
            pltpu.SMEM((NODES,), jnp.float32),
            pltpu.SemaphoreType.DMA((7,)),
        ],
        compiler_params=pltpu.CompilerParams(vmem_limit_bytes=62 * 1024 * 1024),
    )(
        piece_ids.reshape(8, 128),
        point_counts,
        wavenumber,
        strength,
        displacement.reshape(2),
        node_position,
        node_weights,
    )
    got = lax.all_to_all(
        sent.reshape(400, 1, 128),
        "z",
        split_axis=0,
        concat_axis=0,
        axis_index_groups=[Z_ORDER],
        tiled=True,
    ).reshape(400, 128)
    nodes = lax.all_gather(nodes, "y", axis=0, tiled=True)
    terms = pl.pallas_call(
        terms_kernel,
        out_shape=jax.ShapeDtypeStruct((TERM_ROWS, 128), jnp.float32),
        in_specs=[VMEM],
        out_specs=VMEM,
        scratch_shapes=[pltpu.VMEM((64, 128), jnp.float32)],
        compiler_params=PARAMS,
    )(nodes)
    grid = pl.pallas_call(
        place_kernel,
        out_shape=jax.ShapeDtypeStruct((1152, 128), jnp.float32),
        in_specs=[pl.BlockSpec(memory_space=pl.ANY), VMEM],
        out_specs=VMEM,
        compiler_params=PARAMS,
    )(terms, got)
    grid = exchange(grid.reshape(1152, 1, 128), ("x", "core")).reshape(1152, 128)
    sent = pl.pallas_call(
        fill_kernel,
        out_shape=jax.ShapeDtypeStruct((1536, 128), jnp.float32),
        in_specs=[VMEM] * 5,
        out_specs=VMEM,
        scratch_shapes=[
            pltpu.VMEM((16, 128), jnp.float32),
            pltpu.VMEM((48, PLANES * ROWS * 128), jnp.float32),
            pltpu.VMEM((768, 256), jnp.float32),
        ],
        compiler_params=PARAMS,
    )(terms, grid, first, turn_one, second)
    order = [
        z * 32 + x * 8 + core * 4 + y
        for core in range(2)
        for z in Z_ORDER
        for x in range(4)
        for y in range(4)
    ]
    got = lax.all_to_all(
        sent.reshape(1536, 1, 128),
        ("z", "x", "core", "y"),
        split_axis=0,
        concat_axis=0,
        axis_index_groups=[order],
        tiled=True,
    ).reshape(1536, 128)
    shape = jax.ShapeDtypeStruct((PLANES, 8, LENGTH), jnp.float32)
    return pl.pallas_call(
        column_kernel,
        out_shape=(shape, shape),
        in_specs=[VMEM] * 4,
        out_specs=(HBM, HBM),
        scratch_shapes=[
            pltpu.VMEM((1024, 256), jnp.float32),
            pltpu.VMEM((PLANES, 8, LENGTH), jnp.float32),
            pltpu.VMEM((PLANES, 8, LENGTH), jnp.float32),
            pltpu.SemaphoreType.DMA((2 * PLANES,)),
        ],
        compiler_params=PARAMS,
    )(got, third[0], third[1], turn_two)


def solution(mesh):
    every = ("z", "x", "core", "y")
    fine = Mesh(mesh.devices.reshape(16, 4, 2, 4), every)
    wide = every[:3]
    placed = (P(wide), P(wide, None), P("y"), P("y"), P(None, "y"), P(), P())
    return jax.shard_map(
        shards,
        mesh=fine,
        in_specs=placed,
        out_specs=(P(None, every, None), P(None, every, None)),
        check_vma=False,
    )
```
